32 devices in a mesh: dp: 2 (over core), expert: 16 (over z, y, x).
Axes of the slice: x: 2, y: 2, z: 4, core: 2. Of those that a mesh axis runs over, the one named last changes fastest.
Arguments:
- tokens: bfloat16 [2, 2048, 1536], P(None, ('dp', 'expert')), may hold values from -6 to 6
- cotangent: bfloat16 [2, 2048, 1536], P(None, ('dp', 'expert')), may hold values from -6 to 6
- segments: int32 [2, 2048], P(None, ('dp', 'expert')), may hold values from 0 to 4, as said below
- positions: int32 [2, 2048], P(None, ('dp', 'expert')), may hold values from 0 to 2046, as said below
- routes: int32 [2, 2048, 8], P(None, ('dp', 'expert')), may hold values from 0 to 15, all different within a row; in each aligned block of 64 rows (0 to 63, 64 to 127, ..., all dimensions but the last counted through in order) at most 64 rows name the same one
- w_qkv: bfloat16 [1536, 2560], P(('dp', 'expert')), may hold values from -0.15625 to 0.15625
- w_out: bfloat16 [1536, 1536], P(('dp', 'expert')), may hold values from -1.25 to 1.25
- w_router: bfloat16 [1536, 16], P(('dp', 'expert')), may hold values from -0.078125 to 0.078125
- norm_attn: bfloat16 [1536], P(('dp', 'expert')), may hold values from 0.5 to 1.5
- norm_ffn: bfloat16 [1536], P(('dp', 'expert')), may hold values from 0.5 to 1.5
- w_gate_up: bfloat16 [16, 1536, 1024], P('expert', 'dp'), may hold values from -0.15625 to 0.15625
- w_down: bfloat16 [16, 512, 1536], P('expert', 'dp'), may hold values from -0.75 to 0.75
Outputs:
- mixed: bfloat16 [2, 2048, 1536], P(None, ('dp', 'expert'))
- grad_tokens: float32 [2, 2048, 1536], P(None, ('dp', 'expert'))
- grad_qkv: float32 [1536, 2560], P(('dp', 'expert'))
- grad_out: float32 [1536, 1536], P(('dp', 'expert'))
- grad_router: float32 [1536, 16], P(('dp', 'expert'))
- grad_norm_attn: float32 [1536], P(('dp', 'expert'))
- grad_norm_ffn: float32 [1536], P(('dp', 'expert'))
- grad_gate_up: float32 [16, 1536, 1024], P('expert', 'dp')
- grad_down: float32 [16, 512, 1536], P('expert', 'dp')
The draws below stay inside these ranges and needn't reach their ends.
Inputs may be any that keep to these rules, and one draw needn't show every extreme that they name: `segments`: within each sequence of 1024 tokens (one micro-batch, one index of dp) the numbers never fall. `positions`: within a document they rise by one from token to token. `routes`: each row names 8 different experts; among the 64 rows of one device in one micro-batch no expert is named more than 64 times.
All inputs are finite; a program needn't handle non-finite values.
Results may differ from the reference program's by a relative error of at most 0.02.
Values may be sent and summed in bfloat16 or wider, within the bound.
No kernel may reach another device: no remote copies, remote signals or barrier semaphores. Data moves between devices by JAX's collectives and lax.ppermute only.
A program may use at most 192 MiB of HBM per device.

```python
import math
import jax
import jax.numpy as jnp
import numpy as np
from jax import lax

D = 1536
HEADS = 24
KV_HEADS = 8
HEAD_DIM = 64
EXP_FF = 512
TOP = 8
MB = 2
TOK_MB = 64
EXPERTS = 16
GROUPS = 2
LENGTH = 1024
ROWS = 2048
CAP = 64
Q_WIDTH = 1536
QKV_WIDTH = 2560


def doc_layout(key):
    shape = (MB, GROUPS, 1)
    opening_end = jax.random.randint(jax.random.fold_in(key, 11), shape, 2, TOK_MB // 2 + 1)
    opening_cut = jax.random.randint(jax.random.fold_in(key, 12), shape, 1, opening_end)
    closing = LENGTH - jax.random.randint(jax.random.fold_in(key, 13), shape, 2, TOK_MB // 2 + 1)
    trailing = jax.random.randint(jax.random.fold_in(key, 14), shape, closing + 1, LENGTH)
    cuts = jnp.concatenate([opening_cut, opening_end, closing, trailing], -1)
    places = jnp.arange(LENGTH, dtype=jnp.int32)
    doc_ids = jnp.sum((places[None, None, :, None] >= cuts[:, :, None, :]).astype(jnp.int32), -1)
    starts = jnp.concatenate([jnp.zeros(shape, jnp.int32), cuts], -1)
    anchors = jax.random.randint(jax.random.fold_in(key, 15), (MB, GROUPS, 4), 0, 1024)
    anchors = anchors * (jnp.arange(4, dtype=jnp.int32) > 0).astype(jnp.int32)[None, None, :]
    anchors = jnp.concatenate([anchors, 1023 + trailing], -1)
    rotary = places[None, None, :] - jnp.take_along_axis(starts, doc_ids, -1) + jnp.take_along_axis(anchors, doc_ids, -1)
    return (doc_ids.reshape(MB, ROWS), rotary.reshape(MB, ROWS))


def draw_segments(key, part):
    layout = doc_layout(key)
    return layout[0]


def draw_positions(key, part):
    layout = doc_layout(key)
    return layout[1]


def shard_levels(own_key, dims, cuts, low, largest):
    loudness = 1.0
    for axis_at, shards_of in cuts:
        steps = jax.random.uniform(jax.random.fold_in(jax.random.fold_in(own_key, 6), axis_at), (shards_of,), jnp.float32, low / len(cuts), largest / len(cuts))
        loudness = loudness * jnp.repeat(jnp.exp(steps), dims[axis_at] // shards_of).reshape((-1,) + (1,) * (len(dims) - 1 - axis_at))
    return loudness


def shared_out(key, own, number, rows, number_of, top, bound, lean):
    sequence = jax.random.permutation(key, number_of)
    crowded, usual = portions_of(number_of, rows * top, bound, lean, True), portions_of(number_of, rows * top, bound, lean, False)
    places = jnp.arange(number_of)

    def named(lengths, rotation):
        used = int((lengths > 0).sum())
        fixed = max(1, used // 4)
        passed = fixed + (places - fixed + rotation * (used - fixed)) % max(1, number_of - fixed)
        return jnp.zeros((number_of,), jnp.int32).at[sequence[jnp.where(places < fixed, places, passed)]].set(jnp.asarray(lengths, jnp.int32))

    lengths = jnp.where(number % 4 == 0, named(crowded, number // 4), named(usual, number - number // 4 - 1))
    mixed = jax.random.permutation(jax.random.fold_in(own, 3), number_of)
    giver, sink = mixed[0:number_of // 2 * 2:2], mixed[1:number_of // 2 * 2:2]
    margin = jnp.minimum(lengths[giver] - 1, bound - lengths[sink]) // 2
    margin = jnp.where((giver == sequence[0]) | (sink == sequence[0]) | (lengths[sink] == 0), 0, jnp.maximum(margin, 0))
    passed = jax.random.randint(jax.random.fold_in(own, 4), (number_of // 2,), 0, 1 << 20) % (margin + 1)
    lengths = lengths.at[giver].add(-passed).at[sink].add(passed)
    members = jnp.searchsorted(jnp.cumsum(lengths), jnp.arange(rows * top), side="right").astype(jnp.int32)
    grid = members.reshape(top, rows).T
    grid = grid[jax.random.permutation(jax.random.fold_in(own, 1), rows)]
    rotation = jax.random.randint(jax.random.fold_in(own, 2), (rows, 1), 0, top)
    return jnp.take_along_axis(grid, (jnp.arange(top)[None, :] + rotation) % top, axis=1)


def portions_of(count, total, reach, lean, full):
    portions = [(1 << 20) // math.isqrt(standing ** lean) + 1 for standing in range(1, count + 1)]
    largest = reach if full else min(reach, max(-(-total // count), total * portions[0] // sum(portions)))
    least = 1 if total - largest >= count - 1 else 0
    given, surplus = [largest] + [least] * (count - 1), total - largest - least * (count - 1)
    while surplus > 0:
        free = [i for i in range(1, count) if given[i] < largest] or [i for i in range(1, count) if given[i] < reach]
        whole, left = sum([portions[i] for i in free]), surplus
        for i in free:
            extra = min(reach - given[i], max(1, left * portions[i] // whole), surplus)
            given[i] = given[i] + extra
            surplus = surplus - extra
    return np.array(given)


def bell_draw(stream_key, extent, scale, reach, cuts=(), kind=jnp.bfloat16):
    gain = shard_levels(stream_key, extent, cuts, -0.22, 0.18) if cuts else 1.0
    values = jax.random.normal(stream_key, extent, jnp.float32) * scale * gain
    return jnp.minimum(jnp.maximum(values, -reach), reach).astype(kind)


def setup_inputs(seed: int = 0) -> dict:
    keys = jax.random.split(jax.random.key(seed), 13)
    tokens = bell_draw(keys[0], (MB, ROWS, D), 1.0, 6.0, ((1, 32),))
    cotangent = bell_draw(keys[1], (MB, ROWS, D), 1.0, 6.0, ((1, 32),))
    segments = draw_segments(jax.random.fold_in(keys[12], 71), 0)
    positions = draw_positions(jax.random.fold_in(keys[12], 71), 0)
    routes_keys = jax.random.split(jax.random.fold_in(keys[4], 1), MB * ROWS // TOK_MB)
    routes_turns = jax.random.permutation(jax.random.fold_in(keys[4], 3), MB * ROWS // TOK_MB)
    routes = jax.vmap(lambda own, number: shared_out(jax.random.fold_in(keys[4], 2), own, number, TOK_MB, EXPERTS, TOP, CAP, 2))(routes_keys, routes_turns).reshape((MB, ROWS, TOP))
    w_qkv = bell_draw(keys[5], (D, QKV_WIDTH), D ** -0.5, 0.15625, ((0, 32),))
    w_out = bell_draw(keys[6], (D, Q_WIDTH), (max(1, D * 16 // LENGTH)) ** -0.5, 1.25, ((0, 32),))
    w_router = bell_draw(keys[7], (D, EXPERTS), (4 * D) ** -0.5, 0.078125, ((0, 32),))
    norm_attn = jnp.clip(1.0 + 0.1 * jax.random.normal(keys[8], (D,), jnp.float32), 0.5, 1.5).astype(jnp.bfloat16)
    norm_ffn = jnp.clip(1.0 + 0.1 * jax.random.normal(keys[9], (D,), jnp.float32), 0.5, 1.5).astype(jnp.bfloat16)
    w_gate_up = bell_draw(keys[10], (EXPERTS, D, 2 * EXP_FF), D ** -0.5, 0.15625, ((0, 16), (1, 2)))
    w_down = bell_draw(keys[11], (EXPERTS, EXP_FF, D), (EXP_FF // TOP) ** -0.5, 0.75, ((0, 16), (1, 2)))
    return dict(tokens=tokens, cotangent=cotangent, segments=segments, positions=positions, routes=routes, w_qkv=w_qkv, w_out=w_out, w_router=w_router, norm_attn=norm_attn, norm_ffn=norm_ffn, w_gate_up=w_gate_up, w_down=w_down)


@jax.custom_vjp
def low(v):
    return lax.optimization_barrier(v.astype(jnp.bfloat16)).astype(jnp.float32)

@jax.custom_vjp
def low_back(v):
    return v

def low_keep(v):
    return (low(v), None)

def low_pass(kept, grad):
    return (grad,)

def back_keep(v):
    return (v, None)

def back_low(kept, grad):
    return (low(grad),)
low.defvjp(low_keep, low_pass)
low_back.defvjp(back_keep, back_low)
epsilon = 1e-06
rope_base = 10000.0
masked = -1e+30
highest = lax.Precision.HIGHEST

def silu_value(inputs):
    return inputs / (1.0 + jnp.exp(-inputs))

def rotate(vectors, places, direction):
    half_dim = vectors.shape[-1] // 2
    frequency = rope_base ** (-jnp.arange(half_dim, dtype=jnp.float32) / half_dim)
    angles = places.astype(jnp.float32)[:, None] * frequency[None, :]
    cosine = jnp.cos(angles)[:, None, :]
    sine_part = direction * jnp.sin(angles)[:, None, :]
    first_half = vectors[..., :half_dim]
    second_half = vectors[..., half_dim:]
    return jnp.concatenate([first_half * cosine - second_half * sine_part, second_half * cosine + first_half * sine_part], -1)

def normed(inputs, scales):
    return inputs * lax.rsqrt(lax.optimization_barrier(jnp.mean(inputs * inputs, -1, keepdims=True)) + epsilon) * scales

def layer_block(inputs, doc_ids, places, route_rows, wqkv, wout, wrouter, gain_first, gain_second, wgateup, wdown):
    length = inputs.shape[0]
    query_width = HEADS * HEAD_DIM
    key_width = KV_HEADS * HEAD_DIM
    group_size = HEADS // KV_HEADS
    first_low = low(normed(inputs, gain_first))
    projected = jnp.dot(first_low, wqkv, precision=highest)
    query = low(rotate(low_back(projected[:, :query_width]).reshape(length, HEADS, HEAD_DIM), places, 1.0))
    keyed = low(rotate(low_back(projected[:, query_width:query_width + key_width]).reshape(length, KV_HEADS, HEAD_DIM), places, 1.0))
    valued = low(low_back(projected[:, query_width + key_width:])).reshape(length, KV_HEADS, HEAD_DIM)
    block_rows = min(512, length)
    key_places = jnp.arange(length, dtype=jnp.int32)

    def attend(row_start):
        query_part = lax.dynamic_slice_in_dim(query, row_start, block_rows, 0).reshape(block_rows, KV_HEADS, group_size, HEAD_DIM)
        query_docs = lax.dynamic_slice_in_dim(doc_ids, row_start, block_rows, 0)
        query_places = row_start + jnp.arange(block_rows, dtype=jnp.int32)
        scores = jnp.einsum('tgrd,ngd->grtn', query_part, keyed, precision=highest) * 0.125
        allowed = (query_docs[:, None] == doc_ids[None, :]) & (key_places[None, :] <= query_places[:, None])
        scores = low_back(jnp.where(allowed[None, None], scores, masked))
        raised = jnp.exp(scores - lax.optimization_barrier(jnp.max(scores, -1, keepdims=True)))
        probs = raised / lax.optimization_barrier(jnp.sum(raised, -1, keepdims=True))
        attended = jnp.einsum('grtn,ngd->tgrd', low(probs), valued, precision=highest)
        return attended.reshape(block_rows, query_width)
    starts = jnp.arange(length // block_rows, dtype=jnp.int32) * block_rows
    attended = lax.map(jax.checkpoint(attend), starts).reshape(length, query_width)
    attended_low = low(low_back(attended))
    y_one = inputs + low_back(jnp.dot(attended_low, wout.T, precision=highest))
    second_low = low(normed(y_one, gain_second))
    logits = low_back(jnp.dot(second_low, wrouter, precision=highest))
    raised = jnp.exp(logits - lax.optimization_barrier(jnp.max(logits, -1, keepdims=True)))
    router = raised / lax.optimization_barrier(jnp.sum(raised, -1, keepdims=True))
    chosen = (route_rows[:, :, None] == jnp.arange(EXPERTS, dtype=jnp.int32)[None, None, :]).astype(jnp.float32)
    picked = lax.optimization_barrier(jnp.sum(chosen * router[:, None, :], -1))
    gates = picked / lax.optimization_barrier(jnp.sum(picked, -1, keepdims=True))
    shares = lax.optimization_barrier(jnp.sum(chosen * gates[:, :, None], 1))

    def expert_step(running, expert_index):
        expert_in = low_back(second_low)
        gate_up = low_back(jnp.dot(expert_in, wgateup[expert_index], precision=highest))
        hidden = low(silu_value(gate_up[:, :EXP_FF]) * gate_up[:, EXP_FF:])
        expert_out = low(low_back(jnp.dot(hidden, wdown[expert_index], precision=highest)))
        return (running + lax.dynamic_slice_in_dim(shares, expert_index, 1, 1) * expert_out, None)
    mixture, _ = lax.scan(jax.checkpoint(expert_step), jnp.zeros_like(inputs), jnp.arange(EXPERTS, dtype=jnp.int32))
    return y_one + mixture

def reference(tokens, cotangent, segments, positions, routes, w_qkv, w_out, w_router, norm_attn, norm_ffn, w_gate_up, w_down):
    sequences = MB * GROUPS
    inputs = tokens.astype(jnp.float32).reshape(sequences, LENGTH, D)
    doc_ids = segments.reshape(sequences, LENGTH)
    places = positions.reshape(sequences, LENGTH)
    route_rows = routes.reshape(sequences, LENGTH, TOP)
    weights = tuple((w.astype(jnp.float32) for w in (w_qkv, w_out, w_router, norm_attn, norm_ffn, w_gate_up, w_down)))

    def forward(inputs, wqkv, wout, wrouter, gain_first, gain_second, wgateup, wdown):

        def step(carry, item):
            return (carry, jax.checkpoint(layer_block)(item[0], item[1], item[2], item[3], wqkv, wout, wrouter, gain_first, gain_second, wgateup, wdown))
        return lax.scan(step, jnp.zeros((), jnp.float32), (inputs, doc_ids, places, route_rows))[1]
    outputs, pullback = jax.vjp(forward, inputs, *weights)
    grads = pullback(cotangent.astype(jnp.float32).reshape(sequences, LENGTH, D))
    return (outputs.reshape(MB, ROWS, D).astype(jnp.bfloat16), grads[0].reshape(MB, ROWS, D), grads[1], grads[2], grads[3], grads[4], grads[5], grads[6], grads[7])
```

```python
import math

import jax
import jax.numpy as jnp
from jax import lax
from jax.experimental import pallas as pl
from jax.experimental.pallas import tpu as pltpu
from jax.sharding import Mesh
from jax.sharding import PartitionSpec as P

HEADS = 24
KV_HEADS = 8
HEAD_DIM = 64
EXP_FF = 512
TOP = 8

epsilon = 1e-06
rope_base = 10000.0
masked = -1e30

GROUP = HEADS // KV_HEADS
HALF = HEAD_DIM // 2
LANES = 128
SLAB = 3 * LANES
META_ROWS = 16
BLOCK = 256
SWAP = [(0, 1), (1, 0)]
bf16 = jnp.bfloat16
f32 = jnp.float32


def dot(a, b, da, db):
    return lax.dot_general(a, b, (((da,), (db,)), ((), ())), preferred_element_type=f32)


def gather_bits(x, order, every):
    have = []
    for axis in order:
        other = lax.ppermute(x, axis, SWAP)
        place = sum(every.index(h) < every.index(axis) for h in have)
        first = lax.axis_index(axis) == 0
        x = jnp.stack([jnp.where(first, x, other), jnp.where(first, other, x)], place)
        have.append(axis)
    return x


def scatter_bits(x, order, every):
    left = list(every)
    for axis in order:
        place = left.index(axis)
        mine = lax.axis_index(axis)
        keep = lax.dynamic_index_in_dim(x, mine, place, keepdims=False)
        send = lax.dynamic_index_in_dim(x, 1 - mine, place, keepdims=False)
        other = lax.ppermute(send.astype(bf16), axis, SWAP)
        left.pop(place)
        x = keep.astype(f32) + other.astype(f32)
        if left:
            x = x.astype(bf16)
    return x


def project_kernel(a_ref, b_ref, gain_ref, w_ref, cos_ref, sin_ref, low_ref, q_ref, k_ref, v_ref):
    step = pl.program_id(0)
    half = pl.num_programs(0) // 2

    def work(x_ref):
        x = x_ref[...].astype(f32)
        r = lax.rsqrt(jnp.mean(x * x, -1, keepdims=True) + epsilon)
        low = (x * r * gain_ref[...]).astype(bf16)
        low_ref[...] = low
        p = dot(low, w_ref[...], 1, 0)
        lane = lax.broadcasted_iota(jnp.int32, (x.shape[0], LANES), 1)
        u, w = p[:, :LANES], p[:, LANES : 2 * LANES]
        v = jnp.where(lane < HEAD_DIM, p[:, 2 * LANES :], 0.0)
        c, s = cos_ref[...], sin_ref[...]
        for at, turned in ((0, u * c - w * s), (LANES, w * c + u * s)):
            key = jnp.where(lane >= GROUP * HALF, turned, 0.0)
            key = pltpu.roll(key, HALF, 1) + pltpu.roll(key, 2 * HALF, 1) + pltpu.roll(key, 3 * HALF, 1)
            k_ref[:, at : at + LANES] = key.astype(bf16)
            for h in range(GROUP):
                q_ref[h, :, at : at + LANES] = jnp.where(lane // HALF == h, turned, 0.0).astype(bf16)
        zero = jnp.zeros(v.shape, bf16)
        first, second = v.astype(bf16), pltpu.roll(v, HEAD_DIM, 1).astype(bf16)
        for h in range(GROUP):
            for at in range(2):
                part = zero if h // 2 != at else (first if h % 2 == 0 else second)
                v_ref[h, :, at * LANES : (at + 1) * LANES] = part

    pl.when(step < half)(lambda: work(a_ref))
    pl.when(step >= half)(lambda: work(b_ref))


def project(part_a, part_b, gain, w_slab, cosine, sine):
    rows, width = part_a.shape
    length = 2 * rows
    steps = length // BLOCK
    half = steps // 2
    wide = 2 * LANES
    row = lambda cols: pl.BlockSpec((BLOCK, cols), lambda i: (i, 0))
    heads = pl.BlockSpec((GROUP, BLOCK, wide), lambda i: (0, i, 0))
    return pl.pallas_call(
        project_kernel,
        grid=(steps,),
        in_specs=[
            pl.BlockSpec((BLOCK, width), lambda i: (jnp.minimum(i, half - 1), 0)),
            pl.BlockSpec((BLOCK, width), lambda i: (jnp.maximum(i - half, 0), 0)),
            pl.BlockSpec((1, width), lambda i: (0, 0)),
            pl.BlockSpec((width, SLAB), lambda i: (0, 0)),
            row(LANES),
            row(LANES),
        ],
        out_specs=[row(width), heads, row(wide), heads],
        out_shape=[
            jax.ShapeDtypeStruct((length, width), bf16),
            jax.ShapeDtypeStruct((GROUP, length, wide), bf16),
            jax.ShapeDtypeStruct((length, wide), bf16),
            jax.ShapeDtypeStruct((GROUP, length, wide), bf16),
        ],
        compiler_params=pltpu.CompilerParams(vmem_limit_bytes=40 * 2**20),
        cost_estimate=pl.CostEstimate(
            flops=2 * length * width * SLAB, bytes_accessed=12 * 2**20, transcendentals=length
        ),
    )(part_a, part_b, gain, w_slab, cosine, sine)


def allowed_block(col_ref, row_ref, start, width):
    shape = (BLOCK, width)
    places = start + lax.broadcasted_iota(jnp.int32, shape, 0)
    keys = lax.broadcasted_iota(jnp.int32, shape, 1)
    same = col_ref[start : start + BLOCK, :] == row_ref[:, :width]
    return same & (keys <= places)


def attend_kernel(q_ref, k_ref, v_ref, col_ref, row_ref, o_ref, lse_ref):
    lane = lax.broadcasted_iota(jnp.int32, (BLOCK, LANES), 1)
    for start in range(0, k_ref.shape[0], BLOCK):
        width = start + BLOCK
        rows = slice(start, width)
        allowed = allowed_block(col_ref, row_ref, start, width)
        total = jnp.zeros((BLOCK, 2 * LANES), f32)
        logs = jnp.zeros((BLOCK, LANES), f32)
        for h in range(GROUP):
            s = dot(q_ref[h, rows, :], k_ref[:width, :], 1, 1) * 0.125
            s = jnp.where(allowed, s, masked)
            top = jnp.max(s, -1, keepdims=True)
            p = jnp.exp(s - top)
            below = jnp.sum(p, -1, keepdims=True)
            total = total + dot((p / below).astype(bf16), v_ref[h, :width, :], 1, 0)
            logs = jnp.where(lane == h, top + jnp.log(below), logs)
        o_ref[rows, :] = total.astype(bf16)
        lse_ref[rows, :] = logs


def attend(q, k, v, docs_col, docs_row):
    length, wide = k.shape
    return pl.pallas_call(
        attend_kernel,
        out_shape=[
            jax.ShapeDtypeStruct((length, wide), bf16),
            jax.ShapeDtypeStruct((length, LANES), f32),
        ],
        compiler_params=pltpu.CompilerParams(vmem_limit_bytes=48 * 2**20),
        cost_estimate=pl.CostEstimate(
            flops=2 * GROUP * length * length * wide,
            bytes_accessed=8 * 2**20,
            transcendentals=GROUP * length * length // 2,
        ),
    )(q, k, v, docs_col, docs_row)


def attend_back_kernel(
    q_ref, k_ref, v_ref, g_ref, lse_ref, col_ref, row_ref, cos_ref, sin_ref, out_ref, dk_ref, dv_ref
):
    length = k_ref.shape[0]
    wide = 2 * LANES
    dk_ref[...] = jnp.zeros_like(dk_ref)
    dv_ref[...] = jnp.zeros_like(dv_ref)
    lane = lax.broadcasted_iota(jnp.int32, (BLOCK, LANES), 1)
    wide_lane = lax.broadcasted_iota(jnp.int32, (BLOCK, wide), 1)
    for start in range(0, length, BLOCK):
        width = start + BLOCK
        rows = slice(start, width)
        allowed = allowed_block(col_ref, row_ref, start, width)
        dq = jnp.zeros((BLOCK, wide), f32)
        grads = g_ref[rows, :].astype(f32)
        for h in range(GROUP):
            q = q_ref[h, rows, :]
            lse = jnp.sum(jnp.where(lane == h, lse_ref[rows, :], 0.0), -1, keepdims=True)
            s = dot(q, k_ref[:width, :], 1, 1) * 0.125
            p = jnp.where(allowed, jnp.exp(jnp.where(allowed, s, masked) - lse), 0.0)
            g = jnp.where(wide_lane // HEAD_DIM == h, grads, 0.0).astype(bf16)
            dp = dot(g, v_ref[h, :width, :], 1, 1)
            delta = jnp.sum(p * dp, -1, keepdims=True)
            ds = (p * (dp - delta)).astype(bf16)
            part = dot(ds, k_ref[:width, :], 1, 0)
            dq = dq + jnp.where(wide_lane % LANES // HALF == h, part, 0.0)
            dk_ref[:width, :] += dot(ds, q, 0, 0)
            dv_ref[:width, :] += dot(p.astype(bf16), g, 0, 0)
        out_ref[rows, :LANES] = dq[:, :LANES].astype(out_ref.dtype)
        out_ref[rows, LANES:wide] = dq[:, LANES:].astype(out_ref.dtype)
    for start in range(0, length, BLOCK):
        rows = slice(start, start + BLOCK)
        halves = []
        for at in (0, LANES):
            key = dk_ref[rows, at : at + LANES]
            key = pltpu.roll(key, 3 * HALF, 1) + pltpu.roll(key, 2 * HALF, 1) + pltpu.roll(key, HALF, 1)
            both = jnp.where(lane >= GROUP * HALF, key, out_ref[rows, at : at + LANES])
            halves.append(both * 0.125)
        c, s = cos_ref[rows, :], sin_ref[rows, :]
        u, w = halves
        out_ref[rows, :LANES] = u * c + w * s
        out_ref[rows, LANES:wide] = w * c - u * s
        v = dv_ref[rows, :LANES] + dv_ref[rows, LANES:]
        v = v + pltpu.roll(v, HEAD_DIM, 1)
        out_ref[rows, wide:] = jnp.where(lane < HEAD_DIM, v, 0.0)


def attend_back_entry(*refs):
    *ins, out_ref, full_ref, dk_ref, dv_ref = refs
    attend_back_kernel(*ins, full_ref, dk_ref, dv_ref)
    out_ref[...] = full_ref[...].astype(bf16)


def attend_back(q, k, v, g, lse, docs_col, docs_row, cosine, sine):
    length, wide = k.shape
    return pl.pallas_call(
        attend_back_entry,
        out_shape=jax.ShapeDtypeStruct((length, SLAB), bf16),
        scratch_shapes=[
            pltpu.VMEM((length, SLAB), f32),
            pltpu.VMEM((length, wide), f32),
            pltpu.VMEM((length, wide), f32),
        ],
        compiler_params=pltpu.CompilerParams(vmem_limit_bytes=52 * 2**20),
        cost_estimate=pl.CostEstimate(
            flops=5 * GROUP * length * length * wide,
            bytes_accessed=8 * 2**20,
            transcendentals=GROUP * length * length // 2,
        ),
    )(q, k, v, g, lse, docs_col, docs_row, cosine, sine)


def split_columns(w_qkv):
    rows = w_qkv.shape[0]
    q_width, k_width = HEADS * HEAD_DIM, KV_HEADS * HEAD_DIM
    q = w_qkv[:, :q_width].reshape(rows, KV_HEADS, GROUP, 2, HALF)
    k = w_qkv[:, q_width : q_width + k_width].reshape(rows, KV_HEADS, 1, 2, HALF)
    both = jnp.concatenate([q, k], 2)
    return (
        both[:, :, :, 0].reshape(rows, KV_HEADS, LANES),
        both[:, :, :, 1].reshape(rows, KV_HEADS, LANES),
        w_qkv[:, q_width + k_width :].reshape(rows, KV_HEADS, HEAD_DIM),
    )


def join_columns(u, w, v):
    rows = u.shape[0]
    both = jnp.stack(
        [u.reshape(rows, KV_HEADS, GROUP + 1, HALF), w.reshape(rows, KV_HEADS, GROUP + 1, HALF)], 3
    )
    return jnp.concatenate(
        [
            both[:, :, :GROUP].reshape(rows, HEADS * HEAD_DIM),
            both[:, :, GROUP:].reshape(rows, KV_HEADS * HEAD_DIM),
            v.reshape(rows, KV_HEADS * HEAD_DIM),
        ],
        1,
    )


def halves(x):
    high = lax.reduce_precision(x, 8, 7)
    return high.astype(bf16), (x - high).astype(bf16)


def on_device(
    dp_axes,
    ex_axes,
    tokens,
    cotangent,
    segments,
    positions,
    routes,
    w_qkv,
    w_out,
    w_router,
    norm_attn,
    norm_ffn,
    w_gate_up,
    w_down,
):
    batches, local, width = tokens.shape
    experts = w_router.shape[1]
    count = 2 ** len(ex_axes)
    length = count * local
    units = batches * KV_HEADS
    parts = count // units
    shard = w_qkv.shape[0]
    rows = batches * local
    me = lax.axis_index(ex_axes)
    bit = lambda b: ex_axes[len(ex_axes) - 1 - b]
    pair_axis = bit(2)
    token_axes = tuple(a for a in ex_axes if a != pair_axis)
    far = token_axes[:-2]
    orders = (far + (bit(0), bit(1)), far + (bit(1), bit(0)))

    u_cols, w_cols, v_cols = split_columns(w_qkv)
    small = jnp.concatenate([norm_attn[:, None], norm_ffn[:, None], w_router], 1)
    small = jnp.pad(small, ((0, 0), (0, SLAB - 2 * LANES - HEAD_DIM - small.shape[1])))
    small = jnp.broadcast_to(small[:, None, :], (shard, KV_HEADS, small.shape[1]))
    slab = jnp.transpose(jnp.concatenate([u_cols, w_cols, v_cols, small], -1), (1, 0, 2))
    meta = jnp.stack([segments, positions // 64, positions % 64], 1).astype(bf16)
    meta = jnp.pad(meta, ((0, 0), (0, META_ROWS - 3), (0, SLAB - local)))
    payload = jnp.concatenate(
        [
            jnp.broadcast_to(slab[None], (batches,) + slab.shape),
            jnp.broadcast_to(meta[:, None], (batches, KV_HEADS) + meta.shape[1:]),
        ],
        2,
    ).reshape(units, shard + META_ROWS, SLAB)
    payload = jnp.concatenate([payload] * parts, 0)
    arrived = lax.all_to_all(payload, ex_axes, 0, 0, tiled=True)
    w_slab = gather_bits(arrived[:, :shard].reshape(count * shard, SLAB), dp_axes, dp_axes)
    w_slab = w_slab.reshape(width, SLAB)
    extra_at = 2 * LANES + HEAD_DIM
    gain_attn = w_slab[:, extra_at].astype(f32)
    gain_ffn = w_slab[:, extra_at + 1].astype(f32)
    router_full = w_slab[:, extra_at + 2 : extra_at + 2 + experts]
    info = arrived[:, shard : shard + 3, :local].astype(jnp.int32)
    docs = info[:, 0].reshape(length)
    places = (info[:, 1] * 64 + info[:, 2]).reshape(length)
    frequency = rope_base ** (-jnp.arange(HALF, dtype=f32) / HALF)
    angles = places.astype(f32)[:, None] * jnp.tile(frequency, GROUP + 1)[None, :]
    cosine, sine = jnp.cos(angles), jnp.sin(angles)
    docs_col, docs_row = docs[:, None], docs[None, :]

    mb_axis = bit(3)
    mine = lax.axis_index(mb_axis)
    own = lax.dynamic_index_in_dim(tokens, mine, 0, keepdims=False)
    other = lax.ppermute(
        lax.dynamic_index_in_dim(tokens, 1 - mine, 0, keepdims=False), mb_axis, SWAP
    )
    first = mine == 0
    group = jnp.stack([jnp.where(first, own, other), jnp.where(first, other, own)], 0)
    middle = tuple(a for a in ex_axes[:-2] if a != mb_axis)
    group = gather_bits(group, middle, middle)
    group = jnp.moveaxis(group, len(middle), 0)
    sides = []
    for part, last in ((group[0], (bit(0), bit(1))), (group[1], (bit(1), bit(0)))):
        pair = gather_bits(part, last, (bit(1), bit(0)))
        sides.append(jnp.moveaxis(pair, (0, 1), (len(middle), len(middle) + 1)))
    if len(middle) == 1:
        sides = [s.reshape(length // 2, width) for s in sides]
    else:
        at = ex_axes.index(mb_axis)
        whole = jnp.stack(sides, at).reshape(length, width)
        sides = [whole[: length // 2], whole[length // 2 :]]

    out_full = lax.all_gather(w_out, dp_axes + ex_axes, axis=0, tiled=True)
    grad_rows = [
        lax.all_gather(cotangent[m], token_axes, axis=0, tiled=True) for m in range(batches)
    ]
    qkv_mixed = jnp.concatenate([p.reshape(shard, -1) for p in (u_cols, w_cols, v_cols)], 1)
    qkv_full = lax.all_gather(qkv_mixed, dp_axes + ex_axes, axis=0, tiled=True)

    gu_shard, down_shard = w_gate_up[0], w_down[0]
    gu_other = lax.ppermute(gu_shard, pair_axis, SWAP)
    down_other = lax.ppermute(down_shard, pair_axis, SWAP)
    full = lambda s: gather_bits(s, dp_axes, dp_axes).reshape(-1, s.shape[1])
    gate_ups = [full(gu_shard), full(gu_other)]
    downs = [full(down_shard), full(down_other)]

    first_low, q, k, v = project(*sides, gain_attn[None, :], w_slab, cosine, sine)
    attended, lse = attend(q, k, v, docs_col, docs_row)
    back = lax.all_to_all(attended.reshape(count, local, 2 * LANES), ex_axes, 0, 0, tiled=True)
    head_width = GROUP * HEAD_DIM
    attended_low = (
        back[:units, :, :head_width]
        .reshape(batches, KV_HEADS, local, head_width)
        .transpose(0, 2, 1, 3)
        .reshape(rows, HEADS * HEAD_DIM)
    )
    x = tokens.reshape(rows, width).astype(f32)
    g = cotangent.reshape(rows, width).astype(f32)
    y_one = x + dot(attended_low, out_full, 1, 1)
    r_two = lax.rsqrt(jnp.mean(y_one * y_one, -1, keepdims=True) + epsilon)
    n_two = y_one * r_two
    second_low = (n_two * gain_ffn).astype(bf16)
    logits = dot(second_low, router_full, 1, 0)
    raised = jnp.exp(logits - jnp.max(logits, -1, keepdims=True))
    router = raised / jnp.sum(raised, -1, keepdims=True)
    numbers = jnp.arange(experts, dtype=jnp.int32)
    chosen = jnp.sum(
        (routes.reshape(rows, TOP)[:, :, None] == numbers[None, None, :]).astype(f32), 1
    )
    pick_total = jnp.sum(chosen * router, -1, keepdims=True)
    gates = chosen * router / pick_total
    tail = LANES - 2 * experts
    sent = jnp.concatenate([second_low, *halves(gates), jnp.zeros((rows, tail), bf16)], 1)
    sent = sent.reshape(batches, local, width + LANES)

    mixtures, grad_inputs, keeps = [], [], []
    for m in range(batches):
        got = gather_bits(sent[m], orders[m % 2], token_axes).reshape(-1, width + LANES)
        seen = got[:, :width]
        gate_high = got[:, width : width + experts].astype(f32)
        gate_low = got[:, width + experts : width + 2 * experts].astype(f32)
        all_gates = gate_high + gate_low
        grads = grad_rows[m]
        pairs, weighted, gate_grads = [], [], jnp.zeros(all_gates.shape, f32)
        for j, expert in enumerate((me, me ^ 4)):
            is_mine = numbers[None, :] == expert
            share = jnp.sum(jnp.where(is_mine, all_gates, 0.0), -1, keepdims=True)
            gate_up = dot(seen, gate_ups[j], 1, 0)
            gate, up = gate_up[:, :EXP_FF], gate_up[:, EXP_FF:]
            sg = 1.0 / (1.0 + jnp.exp(-gate))
            hidden = (gate * sg * up).astype(bf16).astype(f32)
            grad_plain = dot(grads, downs[j], 1, 1)
            gate_grad = jnp.sum(grad_plain * hidden, -1, keepdims=True)
            gate_grads = gate_grads + jnp.where(is_mine, gate_grad, 0.0)
            grad_hidden = share * grad_plain
            weighted.append((share * hidden).astype(bf16))
            pairs.append(
                jnp.concatenate(
                    [grad_hidden * up * sg * (1.0 + gate * (1.0 - sg)), grad_hidden * gate * sg], 1
                ).astype(bf16)
            )
        grad_in = dot(pairs[0], gate_ups[0], 1, 1) + dot(pairs[1], gate_ups[1], 1, 1)
        grad_in = jnp.concatenate(
            [grad_in.astype(bf16), *halves(gate_grads), jnp.zeros((seen.shape[0], tail), bf16)], 1
        ).reshape((2,) * len(token_axes) + (local, width + LANES))
        grad_inputs.append(scatter_bits(grad_in, orders[m % 2][::-1], token_axes))
        mixture = dot(weighted[0], downs[0], 1, 0) + dot(weighted[1], downs[1], 1, 0)
        mixtures.append(
            lax.psum_scatter(mixture.astype(bf16), token_axes, scatter_dimension=0, tiled=True)
        )
        keeps.append((seen, grads, pairs, weighted))

    grad_experts = []
    for j in range(2):
        grad_gu = sum(dot(seen, pairs[j], 0, 0) for seen, _, pairs, _ in keeps)
        grad_dn = sum(dot(weighted[j], grads, 0, 0) for _, grads, _, weighted in keeps)
        shape = (2,) * len(dp_axes)
        grad_experts.append(
            tuple(
                scatter_bits(t.reshape(shape + (-1, t.shape[1])), dp_axes, dp_axes)
                for t in (grad_gu, grad_dn)
            )
        )
    grad_gate_up, grad_down = (
        mine_part + lax.ppermute(theirs.astype(bf16), pair_axis, SWAP).astype(f32)
        for mine_part, theirs in zip(*grad_experts)
    )
    mixed = y_one + jnp.stack(mixtures).reshape(rows, width).astype(f32)

    came = jnp.stack(grad_inputs).reshape(rows, width + LANES)
    grad_gates = came[:, width : width + experts] + came[:, width + experts : width + 2 * experts]
    grad_gates = chosen * grad_gates
    grad_picked = (
        chosen * (grad_gates - jnp.sum(grad_gates * gates, -1, keepdims=True)) / pick_total
    )
    grad_logits = (
        router * (grad_picked - jnp.sum(router * grad_picked, -1, keepdims=True))
    ).astype(bf16)
    grad_router = dot(second_low, grad_logits, 0, 0)
    grad_second = came[:, :width] + dot(grad_logits, router_full, 1, 1)
    c_two = grad_second * gain_ffn
    grad_y = g + r_two * (c_two - n_two * jnp.mean(c_two * n_two, -1, keepdims=True))
    grad_gain_ffn = jnp.sum(grad_second * n_two, 0)
    grad_branch = grad_y.astype(bf16)
    grad_attended = dot(grad_branch, out_full, 1, 0).astype(bf16)
    payload = jnp.pad(
        grad_attended.reshape(batches, local, KV_HEADS, head_width).transpose(0, 2, 1, 3),
        ((0, 0), (0, 0), (0, 0), (0, 2 * LANES - head_width)),
    ).reshape(units, local, 2 * LANES)
    payload = jnp.concatenate([payload] * parts, 0)
    grad_heads = lax.all_to_all(payload, ex_axes, 0, 0, tiled=True).reshape(length, 2 * LANES)

    grad_out = dot(grad_branch, attended_low, 0, 0)
    extras = jnp.concatenate([grad_router, grad_gain_ffn[:, None]], 1)
    extras = jnp.pad(extras, ((0, 0), (0, LANES - extras.shape[1])))
    dense = jnp.concatenate([grad_out, extras], 1).astype(bf16)
    dense = scatter_bits(
        dense.reshape((2,) * len(dp_axes) + (-1, dense.shape[1])), dp_axes, dp_axes
    )
    dense = lax.psum_scatter(dense.astype(bf16), ex_axes, scatter_dimension=0, tiled=True)
    dense = dense.astype(f32)

    grad_proj = attend_back(q, k, v, grad_heads, lse, docs_col, docs_row, cosine, sine)
    back = lax.all_to_all(grad_proj.reshape(count, local, SLAB), ex_axes, 0, 0, tiled=True)
    back = back[:units].reshape(batches, KV_HEADS, local, SLAB).transpose(0, 2, 1, 3)
    back = jnp.concatenate(
        [
            back[..., :LANES].reshape(rows, -1),
            back[..., LANES : 2 * LANES].reshape(rows, -1),
            back[..., 2 * LANES : 2 * LANES + HEAD_DIM].reshape(rows, -1),
        ],
        1,
    )
    grad_first = dot(back, qkv_full, 1, 1)
    grad_slab = dot(first_low, grad_proj, 0, 0)
    grad_slab = scatter_bits(
        grad_slab.reshape((2,) * len(dp_axes) + (-1, SLAB)), dp_axes, dp_axes
    )
    grad_slab = lax.all_to_all(
        grad_slab.astype(bf16).reshape(count, shard, SLAB), ex_axes, 0, 0, tiled=True
    )
    grad_slab = jnp.sum(
        grad_slab[:units].reshape(batches, KV_HEADS, shard, SLAB).astype(f32), 0
    ).transpose(1, 0, 2)
    grad_qkv = join_columns(
        grad_slab[..., :LANES],
        grad_slab[..., LANES : 2 * LANES],
        grad_slab[..., 2 * LANES : 2 * LANES + HEAD_DIM],
    )
    grad_gain_attn = jnp.sum(grad_qkv * w_qkv.astype(f32), -1) / norm_attn.astype(f32)
    r_one = lax.rsqrt(jnp.mean(x * x, -1, keepdims=True) + epsilon)
    n_one = x * r_one
    c_one = grad_first * gain_attn
    grad_tokens = grad_y + r_one * (c_one - n_one * jnp.mean(c_one * n_one, -1, keepdims=True))

    out_width = HEADS * HEAD_DIM
    return (
        mixed.astype(bf16).reshape(tokens.shape),
        grad_tokens.reshape(tokens.shape),
        grad_qkv,
        dense[:, :out_width],
        dense[:, out_width : out_width + experts],
        grad_gain_attn,
        dense[:, out_width + experts],
        grad_gate_up[None],
        grad_down[None],
    )


def solution(mesh):
    dp_bits = int(math.log2(mesh.shape["dp"]))
    ex_bits = int(math.log2(mesh.shape["expert"]))
    dp_axes = tuple(f"d{b}" for b in reversed(range(dp_bits)))
    ex_axes = tuple(f"e{b}" for b in reversed(range(ex_bits)))
    cube = Mesh(mesh.devices.reshape((2,) * (dp_bits + ex_bits)), dp_axes + ex_axes)
    every = dp_axes + ex_axes
    by_tokens = P(None, every, None)

    def run(*arrays):
        return on_device(dp_axes, ex_axes, *arrays)

    return jax.shard_map(
        run,
        mesh=cube,
        in_specs=(
            by_tokens,
            by_tokens,
            P(None, every),
            P(None, every),
            by_tokens,
            P(every, None),
            P(every, None),
            P(every, None),
            P(every),
            P(every),
            P(ex_axes, dp_axes, None),
            P(ex_axes, dp_axes, None),
        ),
        out_specs=(
            by_tokens,
            by_tokens,
            P(every, None),
            P(every, None),
            P(every, None),
            P(every),
            P(every),
            P(ex_axes, dp_axes, None),
            P(ex_axes, dp_axes, None),
        ),
        check_vma=False,
    )
```

```python
import math

import jax
import jax.numpy as jnp
from jax import lax
from jax.experimental import pallas as pl
from jax.experimental.pallas import tpu as pltpu
from jax.sharding import Mesh
from jax.sharding import PartitionSpec as P

HEADS = 24
KV_HEADS = 8
HEAD_DIM = 64
EXP_FF = 512
TOP = 8

epsilon = 1e-06
rope_base = 10000.0
masked = -1e30

GROUP = HEADS // KV_HEADS
HALF = HEAD_DIM // 2
LANES = 128
SLAB = 3 * LANES
META_ROWS = 16
BLOCK = 256
SWAP = [(0, 1), (1, 0)]
bf16 = jnp.bfloat16
f32 = jnp.float32


def dot(a, b, da, db):
    return lax.dot_general(a, b, (((da,), (db,)), ((), ())), preferred_element_type=f32)


def gather_bits(x, order, every, waits={}):
    have = []
    for i, axis in enumerate(order):
        if i in waits:
            x = after(x, waits[i])
        other = lax.ppermute(x, axis, SWAP)
        place = sum(every.index(h) < every.index(axis) for h in have)
        first = lax.axis_index(axis) == 0
        x = jnp.stack([jnp.where(first, x, other), jnp.where(first, other, x)], place)
        have.append(axis)
    return x


def after(x, *others):
    return lax.optimization_barrier((x, *others))[0]


def scatter_bits(x, order, every, sends=None):
    left = list(every)
    for axis in order:
        place = left.index(axis)
        mine = lax.axis_index(axis)
        keep = lax.dynamic_index_in_dim(x, mine, place, keepdims=False)
        send = lax.dynamic_index_in_dim(x, 1 - mine, place, keepdims=False)
        send = send.astype(bf16)
        if sends is not None:
            sends.append(send)
        other = lax.ppermute(send, axis, SWAP)
        left.pop(place)
        x = keep.astype(f32) + other.astype(f32)
        if left:
            x = x.astype(bf16)
    return x


def project_kernel(a_ref, b_ref, gain_ref, w_ref, cos_ref, sin_ref, low_ref, q_ref, k_ref, v_ref):
    step = pl.program_id(0)
    half = pl.num_programs(0) // 2

    def work(x_ref):
        x = x_ref[...].astype(f32)
        r = lax.rsqrt(jnp.mean(x * x, -1, keepdims=True) + epsilon)
        low = (x * r * gain_ref[...]).astype(bf16)
        low_ref[...] = low
        p = dot(low, w_ref[...], 1, 0)
        lane = lax.broadcasted_iota(jnp.int32, (x.shape[0], LANES), 1)
        u, w = p[:, :LANES], p[:, LANES : 2 * LANES]
        v = jnp.where(lane < HEAD_DIM, p[:, 2 * LANES :], 0.0)
        c, s = cos_ref[...], sin_ref[...]
        for at, turned in ((0, u * c - w * s), (LANES, w * c + u * s)):
            key = jnp.where(lane >= GROUP * HALF, turned, 0.0)
            key = pltpu.roll(key, HALF, 1) + pltpu.roll(key, 2 * HALF, 1) + pltpu.roll(key, 3 * HALF, 1)
            k_ref[:, at : at + LANES] = key.astype(bf16)
            for h in range(GROUP):
                q_ref[h, :, at : at + LANES] = jnp.where(lane // HALF == h, turned, 0.0).astype(bf16)
        zero = jnp.zeros(v.shape, bf16)
        first, second = v.astype(bf16), pltpu.roll(v, HEAD_DIM, 1).astype(bf16)
        for h in range(GROUP):
            for at in range(2):
                part = zero if h // 2 != at else (first if h % 2 == 0 else second)
                v_ref[h, :, at * LANES : (at + 1) * LANES] = part

    pl.when(step < half)(lambda: work(a_ref))
    pl.when(step >= half)(lambda: work(b_ref))


def project(part_a, part_b, gain, w_slab, cosine, sine):
    rows, width = part_a.shape
    length = 2 * rows
    steps = length // BLOCK
    half = steps // 2
    wide = 2 * LANES
    row = lambda cols: pl.BlockSpec((BLOCK, cols), lambda i: (i, 0))
    heads = pl.BlockSpec((GROUP, BLOCK, wide), lambda i: (0, i, 0))
    return pl.pallas_call(
        project_kernel,
        grid=(steps,),
        in_specs=[
            pl.BlockSpec((BLOCK, width), lambda i: (jnp.minimum(i, half - 1), 0)),
            pl.BlockSpec((BLOCK, width), lambda i: (jnp.maximum(i - half, 0), 0)),
            pl.BlockSpec((1, width), lambda i: (0, 0)),
            pl.BlockSpec((width, SLAB), lambda i: (0, 0)),
            row(LANES),
            row(LANES),
        ],
        out_specs=[row(width), heads, row(wide), heads],
        out_shape=[
            jax.ShapeDtypeStruct((length, width), bf16),
            jax.ShapeDtypeStruct((GROUP, length, wide), bf16),
            jax.ShapeDtypeStruct((length, wide), bf16),
            jax.ShapeDtypeStruct((GROUP, length, wide), bf16),
        ],
        compiler_params=pltpu.CompilerParams(vmem_limit_bytes=40 * 2**20),
        cost_estimate=pl.CostEstimate(
            flops=2 * length * width * SLAB, bytes_accessed=12 * 2**20, transcendentals=length
        ),
    )(part_a, part_b, gain, w_slab, cosine, sine)


def allowed_block(col_ref, row_ref, start, width):
    shape = (BLOCK, width)
    places = start + lax.broadcasted_iota(jnp.int32, shape, 0)
    keys = lax.broadcasted_iota(jnp.int32, shape, 1)
    same = col_ref[start : start + BLOCK, :] == row_ref[:, :width]
    return same & (keys <= places)


def attend_kernel(q_ref, k_ref, v_ref, col_ref, row_ref, o_ref, lse_ref):
    lane = lax.broadcasted_iota(jnp.int32, (BLOCK, LANES), 1)
    for start in range(0, k_ref.shape[0], BLOCK):
        width = start + BLOCK
        rows = slice(start, width)
        allowed = allowed_block(col_ref, row_ref, start, width)
        total = jnp.zeros((BLOCK, 2 * LANES), f32)
        logs = jnp.zeros((BLOCK, LANES), f32)
        for h in range(GROUP):
            s = dot(q_ref[h, rows, :], k_ref[:width, :], 1, 1) * 0.125
            s = jnp.where(allowed, s, masked)
            top = jnp.max(s, -1, keepdims=True)
            p = jnp.exp(s - top)
            below = jnp.sum(p, -1, keepdims=True)
            total = total + dot((p / below).astype(bf16), v_ref[h, :width, :], 1, 0)
            logs = jnp.where(lane == h, top + jnp.log(below), logs)
        o_ref[rows, :] = total.astype(bf16)
        lse_ref[rows, :] = logs


def attend(q, k, v, docs_col, docs_row):
    length, wide = k.shape
    return pl.pallas_call(
        attend_kernel,
        out_shape=[
            jax.ShapeDtypeStruct((length, wide), bf16),
            jax.ShapeDtypeStruct((length, LANES), f32),
        ],
        compiler_params=pltpu.CompilerParams(vmem_limit_bytes=48 * 2**20),
        cost_estimate=pl.CostEstimate(
            flops=2 * GROUP * length * length * wide,
            bytes_accessed=8 * 2**20,
            transcendentals=GROUP * length * length // 2,
        ),
    )(q, k, v, docs_col, docs_row)


def attend_back_kernel(
    q_ref, k_ref, v_ref, g_ref, lse_ref, col_ref, row_ref, cos_ref, sin_ref, out_ref, dk_ref, dv_ref
):
    length = k_ref.shape[0]
    wide = 2 * LANES
    dk_ref[...] = jnp.zeros_like(dk_ref)
    dv_ref[...] = jnp.zeros_like(dv_ref)
    lane = lax.broadcasted_iota(jnp.int32, (BLOCK, LANES), 1)
    wide_lane = lax.broadcasted_iota(jnp.int32, (BLOCK, wide), 1)
    for start in range(0, length, BLOCK):
        width = start + BLOCK
        rows = slice(start, width)
        allowed = allowed_block(col_ref, row_ref, start, width)
        dq = jnp.zeros((BLOCK, wide), f32)
        grads = g_ref[rows, :].astype(f32)
        for h in range(GROUP):
            q = q_ref[h, rows, :]
            lse = jnp.sum(jnp.where(lane == h, lse_ref[rows, :], 0.0), -1, keepdims=True)
            s = dot(q, k_ref[:width, :], 1, 1) * 0.125
            p = jnp.where(allowed, jnp.exp(jnp.where(allowed, s, masked) - lse), 0.0)
            g = jnp.where(wide_lane // HEAD_DIM == h, grads, 0.0).astype(bf16)
            dp = dot(g, v_ref[h, :width, :], 1, 1)
            delta = jnp.sum(p * dp, -1, keepdims=True)
            ds = (p * (dp - delta)).astype(bf16)
            part = dot(ds, k_ref[:width, :], 1, 0)
            dq = dq + jnp.where(wide_lane % LANES // HALF == h, part, 0.0)
            dk_ref[:width, :] += dot(ds, q, 0, 0)
            dv_ref[:width, :] += dot(p.astype(bf16), g, 0, 0)
        out_ref[rows, :LANES] = dq[:, :LANES].astype(out_ref.dtype)
        out_ref[rows, LANES:wide] = dq[:, LANES:].astype(out_ref.dtype)
    for start in range(0, length, BLOCK):
        rows = slice(start, start + BLOCK)
        halves = []
        for at in (0, LANES):
            key = dk_ref[rows, at : at + LANES]
            key = pltpu.roll(key, 3 * HALF, 1) + pltpu.roll(key, 2 * HALF, 1) + pltpu.roll(key, HALF, 1)
            both = jnp.where(lane >= GROUP * HALF, key, out_ref[rows, at : at + LANES])
            halves.append(both * 0.125)
        c, s = cos_ref[rows, :], sin_ref[rows, :]
        u, w = halves
        out_ref[rows, :LANES] = u * c + w * s
        out_ref[rows, LANES:wide] = w * c - u * s
        v = dv_ref[rows, :LANES] + dv_ref[rows, LANES:]
        v = v + pltpu.roll(v, HEAD_DIM, 1)
        out_ref[rows, wide:] = jnp.where(lane < HEAD_DIM, v, 0.0)


def attend_back_entry(*refs):
    *ins, out_ref, full_ref, dk_ref, dv_ref = refs
    attend_back_kernel(*ins, full_ref, dk_ref, dv_ref)
    out_ref[...] = full_ref[...].astype(bf16)


def attend_back(q, k, v, g, lse, docs_col, docs_row, cosine, sine):
    length, wide = k.shape
    return pl.pallas_call(
        attend_back_entry,
        out_shape=jax.ShapeDtypeStruct((length, SLAB), bf16),
        scratch_shapes=[
            pltpu.VMEM((length, SLAB), f32),
            pltpu.VMEM((length, wide), f32),
            pltpu.VMEM((length, wide), f32),
        ],
        compiler_params=pltpu.CompilerParams(vmem_limit_bytes=52 * 2**20),
        cost_estimate=pl.CostEstimate(
            flops=5 * GROUP * length * length * wide,
            bytes_accessed=8 * 2**20,
            transcendentals=GROUP * length * length // 2,
        ),
    )(q, k, v, g, lse, docs_col, docs_row, cosine, sine)


def pack(gate_up, down):
    blocks = [down[:, c : c + EXP_FF] for c in range(0, down.shape[1], EXP_FF)]
    return jnp.concatenate([gate_up, jnp.concatenate(blocks, 0)], 1)


def unpack_down(packed, high):
    rows = packed.shape[0] // high
    return jnp.concatenate([packed[c * rows : (c + 1) * rows, 2 * EXP_FF :] for c in range(high)], 1)


def half_places(at_ref, half, size):
    high = at_ref[2]
    place = high if half == 0 else 1 - high
    return pl.multiple_of(place * size, LANES)


def expert_kernel(at_ref, x_ref, g_ref, pa, pb, pc, pd, sum_ref, hid_ref, pair_ref, plain_ref):
    rows = x_ref.shape[0]
    size, width = pa.shape
    part = EXP_FF // 2
    double = 2 * EXP_FF
    me, experts = at_ref[0], at_ref[1]
    extra = x_ref[:, width:].astype(f32)
    g = g_ref[:, 0].reshape(rows, width)
    lane = lax.broadcasted_iota(jnp.int32, extra.shape, 1)
    back = jnp.zeros(extra.shape, f32)
    totals = [None, None]
    for j, packed in enumerate(((pa, pb), (pc, pd))):
        expert = me if j == 0 else me ^ 4
        high = lane == expert
        low = lane == expert + experts
        share = jnp.sum(jnp.where(high | low, extra, 0.0), -1, keepdims=True)
        gate_up = None
        for half, p in enumerate(packed):
            term = dot(x_ref[:, pl.ds(half_places(at_ref, half, size), size)], p[:, :double], 1, 0)
            gate_up = term if gate_up is None else gate_up + term
            plain = None
            for c in range(width // EXP_FF):
                term = dot(
                    g[:, c * EXP_FF : (c + 1) * EXP_FF],
                    p[c * part : (c + 1) * part, double:],
                    1,
                    1,
                )
                plain = term if plain is None else plain + term
            plain_ref[:, pl.ds(half_places(at_ref, half, part), part)] = plain
        gate, up = gate_up[:, :EXP_FF], gate_up[:, EXP_FF:]
        sg = 1.0 / (1.0 + jnp.exp(-gate))
        grown = gate * sg
        hidden = (grown * up).astype(bf16).astype(f32)
        grad_plain = plain_ref[...]
        gate_grad = jnp.sum(grad_plain * hidden, -1, keepdims=True)
        gate_high = gate_grad.astype(bf16).astype(f32)
        back = jnp.where(high, gate_high, jnp.where(low, gate_grad - gate_high, back))
        grad_hidden = share * grad_plain
        at = j * EXP_FF
        hid_ref[:, at : at + EXP_FF] = (share * hidden).astype(bf16)
        at = j * double
        first = (grad_hidden * up * sg * (1.0 + gate * (1.0 - sg))).astype(bf16)
        pair_ref[:, at : at + EXP_FF] = first
        pair_ref[:, at + EXP_FF : at + double] = (grad_hidden * grown).astype(bf16)
        for half, p in enumerate(packed):
            term = dot(pair_ref[:, at : at + double], p[:, :double], 1, 1)
            totals[half] = term if totals[half] is None else totals[half] + term
    for half in range(2):
        sum_ref[:, pl.ds(half_places(at_ref, half, size), size)] = totals[half].astype(bf16)
    sum_ref[:, width:] = back.astype(bf16)


def run_experts(places, x, grads, m, packed):
    rows, wide = x.shape
    local, width = grads.shape[2:]
    size = width // 2
    block = lambda cols: pl.BlockSpec((BLOCK, cols), lambda i, _: (i, 0))
    whole = pl.BlockSpec((size, width), lambda i, _: (0, 0))
    return pl.pallas_call(
        expert_kernel,
        grid_spec=pltpu.PrefetchScalarGridSpec(
            num_scalar_prefetch=1,
            grid=(rows // BLOCK,),
            in_specs=[
                block(wide),
                pl.BlockSpec((BLOCK // local, 1, local, width), lambda i, _: (i, m, 0, 0)),
                *[whole] * 4,
            ],
            out_specs=[block(wide), block(2 * EXP_FF), block(4 * EXP_FF)],
            scratch_shapes=[pltpu.VMEM((BLOCK, EXP_FF), f32)],
        ),
        out_shape=[
            jax.ShapeDtypeStruct((rows, wide), bf16),
            jax.ShapeDtypeStruct((rows, 2 * EXP_FF), bf16),
            jax.ShapeDtypeStruct((rows, 4 * EXP_FF), bf16),
        ],
        compiler_params=pltpu.CompilerParams(vmem_limit_bytes=56 * 2**20),
        cost_estimate=pl.CostEstimate(
            flops=20 * rows * width * EXP_FF, bytes_accessed=16 * 2**20, transcendentals=rows * 2 * EXP_FF
        ),
    )(places, x, grads, *packed)


def mixture_kernel(at_ref, a_ref, b_ref, pa, pb, pc, pd, out_ref):
    size, width = pa.shape
    part = EXP_FF // 2

    def work(hid_ref):
        for c in range(width // EXP_FF):
            total = None
            for j, packed in enumerate(((pa, pb), (pc, pd))):
                for half, p in enumerate(packed):
                    at = pl.multiple_of(j * EXP_FF + half_places(at_ref, half, part), LANES)
                    term = dot(
                        hid_ref[:, pl.ds(at, part)],
                        p[c * part : (c + 1) * part, 2 * EXP_FF :],
                        1,
                        0,
                    )
                    total = term if total is None else total + term
            cols = slice(c * EXP_FF, (c + 1) * EXP_FF)
            shape = out_ref.shape[0], out_ref.shape[2], EXP_FF
            out_ref[:, 0, :, cols] = total.astype(bf16).reshape(shape)

    pl.when(pl.program_id(0) == 0)(lambda: work(a_ref))
    pl.when(pl.program_id(0) == 1)(lambda: work(b_ref))


def mix_experts(places, weighted, local, packed):
    rows = weighted[0].shape[0]
    size, width = packed[0].shape
    blocks = rows // BLOCK
    whole = pl.BlockSpec((size, width), lambda m, i, _: (0, 0))
    first = pl.BlockSpec((BLOCK, 2 * EXP_FF), lambda m, i, _: (jnp.where(m == 0, i, blocks - 1), 0))
    second = pl.BlockSpec((BLOCK, 2 * EXP_FF), lambda m, i, _: (jnp.where(m == 1, i, 0), 0))
    return pl.pallas_call(
        mixture_kernel,
        grid_spec=pltpu.PrefetchScalarGridSpec(
            num_scalar_prefetch=1,
            grid=(2, blocks),
            in_specs=[first, second, *[whole] * 4],
            out_specs=pl.BlockSpec(
                (BLOCK // local, 1, local, width), lambda m, i, _: (i, m, 0, 0)
            ),
        ),
        out_shape=jax.ShapeDtypeStruct((rows // local, 2, local, width), bf16),
        compiler_params=pltpu.CompilerParams(vmem_limit_bytes=48 * 2**20),
        cost_estimate=pl.CostEstimate(
            flops=8 * rows * width * EXP_FF, bytes_accessed=16 * 2**20, transcendentals=0
        ),
    )(places, *weighted, *packed)


def weights_kernel(
    at_ref, xa_ref, xb_ref, g_ref, ha_ref, hb_ref, pa_ref, pb_ref, send_ref, keep_ref, pass_ref
):
    size, width = keep_ref.shape
    rows = xa_ref.shape[0]
    part = EXP_FF // 2
    double = 2 * EXP_FF

    def work(half, out_ref):
        cols = pl.ds(half_places(at_ref, half, size), size)
        total = dot(xa_ref[:, cols], pa_ref[...], 0, 0) + dot(xb_ref[:, cols], pb_ref[...], 0, 0)
        out_ref[:, :double] = total.astype(out_ref.dtype)
        cols = pl.ds(half_places(at_ref, half, part), part)
        for c in range(width // EXP_FF):
            at = slice(c * EXP_FF, (c + 1) * EXP_FF)
            total = dot(ha_ref[:, cols], g_ref[:, 0, :, at].reshape(rows, EXP_FF), 0, 0)
            total = total + dot(hb_ref[:, cols], g_ref[:, 1, :, at].reshape(rows, EXP_FF), 0, 0)
            out_ref[c * part : (c + 1) * part, double:] = total.astype(out_ref.dtype)

    h, j = pl.program_id(0), pl.program_id(1)
    pl.when(h == 0)(lambda: work(1, send_ref.at[0]))
    pl.when((h == 1) & (j == 0))(lambda: work(0, keep_ref))
    pl.when((h == 1) & (j == 1))(lambda: work(0, pass_ref))


def expert_weights(places, xs, grads, weighted, pairs):
    rows, wide = xs[0].shape
    width = grads.shape[3]
    size = width // 2
    whole = pl.BlockSpec((rows, wide), lambda h, j, _: (0, 0))
    hidden = pl.BlockSpec((rows, EXP_FF), lambda h, j, _: (0, j))
    pair = pl.BlockSpec((rows, 2 * EXP_FF), lambda h, j, _: (0, j))
    return pl.pallas_call(
        weights_kernel,
        grid_spec=pltpu.PrefetchScalarGridSpec(
            num_scalar_prefetch=1,
            grid=(2, 2),
            in_specs=[
                whole,
                whole,
                pl.BlockSpec(grads.shape, lambda h, j, _: (0, 0, 0, 0)),
                hidden,
                hidden,
                pair,
                pair,
            ],
            out_specs=[
                pl.BlockSpec((1, size, width), lambda h, j, _: (jnp.where(h == 0, j, 1), 0, 0)),
                pl.BlockSpec((size, width), lambda h, j, _: (0, 0)),
                pl.BlockSpec((size, width), lambda h, j, _: (0, 0)),
            ],
        ),
        out_shape=[
            jax.ShapeDtypeStruct((2, size, width), bf16),
            jax.ShapeDtypeStruct((size, width), f32),
            jax.ShapeDtypeStruct((size, width), bf16),
        ],
        compiler_params=pltpu.CompilerParams(vmem_limit_bytes=60 * 2**20),
        cost_estimate=pl.CostEstimate(
            flops=24 * rows * width * EXP_FF, bytes_accessed=24 * 2**20, transcendentals=0
        ),
    )(places, *xs, grads, *weighted, *pairs)


def split_columns(w_qkv):
    rows = w_qkv.shape[0]
    q_width, k_width = HEADS * HEAD_DIM, KV_HEADS * HEAD_DIM
    q = w_qkv[:, :q_width].reshape(rows, KV_HEADS, GROUP, 2, HALF)
    k = w_qkv[:, q_width : q_width + k_width].reshape(rows, KV_HEADS, 1, 2, HALF)
    both = jnp.concatenate([q, k], 2)
    return (
        both[:, :, :, 0].reshape(rows, KV_HEADS, LANES),
        both[:, :, :, 1].reshape(rows, KV_HEADS, LANES),
        w_qkv[:, q_width + k_width :].reshape(rows, KV_HEADS, HEAD_DIM),
    )


def join_columns(u, w, v):
    rows = u.shape[0]
    both = jnp.stack(
        [u.reshape(rows, KV_HEADS, GROUP + 1, HALF), w.reshape(rows, KV_HEADS, GROUP + 1, HALF)], 3
    )
    return jnp.concatenate(
        [
            both[:, :, :GROUP].reshape(rows, HEADS * HEAD_DIM),
            both[:, :, GROUP:].reshape(rows, KV_HEADS * HEAD_DIM),
            v.reshape(rows, KV_HEADS * HEAD_DIM),
        ],
        1,
    )


def halves(x):
    high = lax.reduce_precision(x, 8, 7)
    return high.astype(bf16), (x - high).astype(bf16)


def gather_sequence(tokens, ex_axes, mb_axis):
    mine = lax.axis_index(mb_axis)
    own = lax.dynamic_index_in_dim(tokens, mine, 0, keepdims=False)
    other = lax.ppermute(
        lax.dynamic_index_in_dim(tokens, 1 - mine, 0, keepdims=False), mb_axis, SWAP
    )
    first = mine == 0
    group = jnp.stack([jnp.where(first, own, other), jnp.where(first, other, own)], 0)
    middle = tuple(a for a in ex_axes[:-2] if a != mb_axis)
    return gather_bits(group, middle, middle), middle, other


def on_device(
    dp_axes,
    ex_axes,
    tokens,
    cotangent,
    segments,
    positions,
    routes,
    w_qkv,
    w_out,
    w_router,
    norm_attn,
    norm_ffn,
    w_gate_up,
    w_down,
):
    batches, local, width = tokens.shape
    experts = w_router.shape[1]
    count = 2 ** len(ex_axes)
    length = count * local
    units = batches * KV_HEADS
    parts = count // units
    shard = w_qkv.shape[0]
    rows = batches * local
    me = lax.axis_index(ex_axes)
    bit = lambda b: ex_axes[len(ex_axes) - 1 - b]
    pair_axis = bit(2)
    token_axes = tuple(a for a in ex_axes if a != pair_axis)
    far = token_axes[:-2]
    orders = (far + (bit(0), bit(1)), far + (bit(1), bit(0)))

    mb_axis = bit(3)

    u_cols, w_cols, v_cols = split_columns(w_qkv)
    small = jnp.concatenate([norm_attn[:, None], norm_ffn[:, None], w_router], 1)
    small = jnp.pad(small, ((0, 0), (0, SLAB - 2 * LANES - HEAD_DIM - small.shape[1])))
    small = jnp.broadcast_to(small[:, None, :], (shard, KV_HEADS, small.shape[1]))
    slab = jnp.transpose(jnp.concatenate([u_cols, w_cols, v_cols, small], -1), (1, 0, 2))
    meta = jnp.stack([segments, positions // 64, positions % 64], 1).astype(bf16)
    meta = jnp.pad(meta, ((0, 0), (0, META_ROWS - 3), (0, SLAB - local)))
    payload = jnp.concatenate(
        [
            jnp.broadcast_to(slab[None], (batches,) + slab.shape),
            jnp.broadcast_to(meta[:, None], (batches, KV_HEADS) + meta.shape[1:]),
        ],
        2,
    ).reshape(units, shard + META_ROWS, SLAB)
    payload = jnp.concatenate([payload] * parts, 0)
    group, middle, swapped = gather_sequence(tokens, ex_axes, mb_axis)
    arrived = lax.all_to_all(after(payload, swapped), ex_axes, 0, 0, tiled=True)
    w_slab = gather_bits(arrived[:, :shard].reshape(count * shard, SLAB), dp_axes, dp_axes)
    w_slab = w_slab.reshape(width, SLAB)
    extra_at = 2 * LANES + HEAD_DIM
    gain_attn = w_slab[:, extra_at].astype(f32)
    gain_ffn = w_slab[:, extra_at + 1].astype(f32)
    router_full = w_slab[:, extra_at + 2 : extra_at + 2 + experts]
    info = arrived[:, shard : shard + 3, :local].astype(jnp.int32)
    docs = info[:, 0].reshape(length)
    places = (info[:, 1] * 64 + info[:, 2]).reshape(length)
    frequency = rope_base ** (-jnp.arange(HALF, dtype=f32) / HALF)
    angles = places.astype(f32)[:, None] * jnp.tile(frequency, GROUP + 1)[None, :]
    cosine, sine = jnp.cos(angles), jnp.sin(angles)
    docs_col, docs_row = docs[:, None], docs[None, :]

    high_axis, low_axes = dp_axes[0], dp_axes[1:]
    blocks = width // EXP_FF
    expert_own = pack(w_gate_up[0], w_down[0])
    if low_axes:
        parted = gather_bits(expert_own, low_axes, low_axes)
        parted = parted.reshape((-1,) + expert_own.shape)
        lower = parted[..., 2 * EXP_FF :].reshape(parted.shape[0], blocks, -1, EXP_FF)
        expert_own = jnp.concatenate(
            [
                parted[..., : 2 * EXP_FF].reshape(-1, 2 * EXP_FF),
                lower.transpose(1, 0, 2, 3).reshape(-1, EXP_FF),
            ],
            1,
        )
    group, expert_own = lax.optimization_barrier((group, expert_own))
    group = jnp.moveaxis(group, len(middle), 0)
    sides = []
    for part, last in ((group[0], (bit(0), bit(1))), (group[1], (bit(1), bit(0)))):
        pair = gather_bits(part, last, (bit(1), bit(0)), {1: arrived})
        sides.append(jnp.moveaxis(pair, (0, 1), (len(middle), len(middle) + 1)))
    if len(middle) == 1:
        sides = [s.reshape(length // 2, width) for s in sides]
    else:
        at = ex_axes.index(mb_axis)
        whole = jnp.stack(sides, at).reshape(length, width)
        sides = [whole[: length // 2], whole[length // 2 :]]

    out_full = lax.all_gather(w_out, dp_axes + ex_axes, axis=0, tiled=True)
    grad_rows = lax.all_gather(cotangent, token_axes, axis=0)
    qkv_mixed = jnp.concatenate([p.reshape(shard, -1) for p in (u_cols, w_cols, v_cols)], 1)
    qkv_full = lax.all_gather(qkv_mixed, dp_axes + ex_axes, axis=0, tiled=True)

    cut = expert_own.shape[0] // 2
    other_parts = [lax.ppermute(t, pair_axis, SWAP) for t in (expert_own[:cut], expert_own[cut:])]

    first_low, q, k, v = project(*sides, gain_attn[None, :], w_slab, cosine, sine)
    q = after(q, other_parts[0])
    attended, lse = attend(q, k, v, docs_col, docs_row)
    back = lax.all_to_all(attended.reshape(count, local, 2 * LANES), ex_axes, 0, 0, tiled=True)
    head_width = GROUP * HEAD_DIM
    attended_low = (
        back[:units, :, :head_width]
        .reshape(batches, KV_HEADS, local, head_width)
        .transpose(0, 2, 1, 3)
        .reshape(rows, HEADS * HEAD_DIM)
    )
    expert_other = jnp.concatenate([after(t, attended) for t in other_parts], 0)
    packed = [
        expert_own,
        lax.ppermute(expert_own, high_axis, SWAP),
        expert_other,
        lax.ppermute(expert_other, high_axis, SWAP),
    ]
    x = tokens.reshape(rows, width).astype(f32)
    g = cotangent.reshape(rows, width).astype(f32)
    y_one = x + dot(attended_low, out_full, 1, 1)
    r_two = lax.rsqrt(jnp.mean(y_one * y_one, -1, keepdims=True) + epsilon)
    n_two = y_one * r_two
    second_low = (n_two * gain_ffn).astype(bf16)
    logits = dot(second_low, router_full, 1, 0)
    raised = jnp.exp(logits - jnp.max(logits, -1, keepdims=True))
    router = raised / jnp.sum(raised, -1, keepdims=True)
    numbers = jnp.arange(experts, dtype=jnp.int32)
    chosen = jnp.sum(
        (routes.reshape(rows, TOP)[:, :, None] == numbers[None, None, :]).astype(f32), 1
    )
    pick_total = jnp.sum(chosen * router, -1, keepdims=True)
    gates = chosen * router / pick_total
    tail = LANES - 2 * experts
    sent = jnp.concatenate([second_low, *halves(gates), jnp.zeros((rows, tail), bf16)], 1)
    sent = after(sent.reshape(batches, local, width + LANES), other_parts[1])

    places_at = jnp.stack([me, jnp.int32(experts), lax.axis_index(high_axis)]).astype(jnp.int32)
    weighted, pairs, stages = [], [], []
    gathered = [
        gather_bits(sent[m], orders[m % 2], token_axes, {1: grad_rows}).reshape(-1, width + LANES)
        for m in range(batches)
    ]
    for m in range(batches):
        back_rows, hid, pair = run_experts(places_at, gathered[m], grad_rows, m, packed)
        back_rows = back_rows.reshape((2,) * len(token_axes) + (local, width + LANES))
        sends = []
        stages.append(scatter_bits(back_rows, orders[m % 2][-1:], token_axes, sends))
        weighted.append(hid)
        pairs.append(pair)
    grad_send, grad_keep, grad_pass = expert_weights(
        places_at, gathered, grad_rows, [after(t, stages[0], *sends) for t in weighted], pairs
    )
    grad_inputs = []
    for m in range(batches):
        order = orders[m % 2][::-1]
        left = tuple(a for a in token_axes if a != order[0])
        stage = stages[m] if m == 0 else after(stages[m], grad_send)
        grad_inputs.append(scatter_bits(stage, order[1:], left))
    grad_other = lax.ppermute(grad_send, high_axis, SWAP)
    if low_axes:
        count_low = 2 ** len(low_axes)
        halves_sum = jnp.stack([grad_keep, grad_pass.astype(f32)]) + grad_other.astype(f32)
        parted = halves_sum[..., : 2 * EXP_FF].reshape(2, count_low, -1, 2 * EXP_FF)
        lower = halves_sum[..., 2 * EXP_FF :].reshape(2, blocks, count_low, -1, EXP_FF)
        lower = lower.transpose(0, 2, 1, 3, 4).reshape(2, count_low, -1, EXP_FF)
        parted = jnp.concatenate([parted, lower], -1)
        parted = jnp.moveaxis(parted, 0, 1).reshape((2,) * len(low_axes) + (2, -1, width))
        halves_sum = scatter_bits(parted.astype(bf16), low_axes, low_axes)
        grad_mine, grad_theirs = [halves_sum[0]], halves_sum[1].astype(bf16)
    else:
        grad_mine = [grad_keep, grad_other[0]]
        grad_theirs = (grad_pass.astype(f32) + grad_other[1].astype(f32)).astype(bf16)
    cut = grad_theirs.shape[0] // 2
    grad_received = [
        lax.ppermute(t, pair_axis, SWAP) for t in (grad_theirs[:cut], grad_theirs[cut:])
    ]
    grad_inputs[-1] = after(grad_inputs[-1], grad_received[0])

    came = jnp.stack(grad_inputs).reshape(rows, width + LANES)
    grad_gates = came[:, width : width + experts] + came[:, width + experts : width + 2 * experts]
    grad_gates = chosen * grad_gates
    grad_picked = (
        chosen * (grad_gates - jnp.sum(grad_gates * gates, -1, keepdims=True)) / pick_total
    )
    grad_logits = (
        router * (grad_picked - jnp.sum(router * grad_picked, -1, keepdims=True))
    ).astype(bf16)
    grad_router = dot(second_low, grad_logits, 0, 0)
    grad_second = came[:, :width] + dot(grad_logits, router_full, 1, 1)
    c_two = grad_second * gain_ffn
    grad_y = g + r_two * (c_two - n_two * jnp.mean(c_two * n_two, -1, keepdims=True))
    grad_gain_ffn = jnp.sum(grad_second * n_two, 0)
    grad_branch = grad_y.astype(bf16)
    grad_attended = dot(grad_branch, out_full, 1, 0).astype(bf16)
    payload = jnp.pad(
        grad_attended.reshape(batches, local, KV_HEADS, head_width).transpose(0, 2, 1, 3),
        ((0, 0), (0, 0), (0, 0), (0, 2 * LANES - head_width)),
    ).reshape(units, local, 2 * LANES)
    payload = jnp.concatenate([payload] * parts, 0)
    grad_heads = lax.all_to_all(payload, ex_axes, 0, 0, tiled=True).reshape(length, 2 * LANES)

    mixture = mix_experts(places_at, [after(t, payload) for t in weighted], local, packed)
    mixtures = lax.psum_scatter(
        after(mixture.reshape(-1, width), qkv_full), token_axes, scatter_dimension=0, tiled=True
    )
    grad_out = dot(after(grad_branch, payload), attended_low, 0, 0)
    extras = jnp.concatenate([grad_router, grad_gain_ffn[:, None]], 1)
    extras = jnp.pad(extras, ((0, 0), (0, LANES - extras.shape[1])))
    dense = jnp.concatenate([grad_out, extras], 1).astype(bf16)
    dense = scatter_bits(
        dense.reshape((2,) * len(dp_axes) + (-1, dense.shape[1])), dp_axes, dp_axes
    )
    dense = dense.astype(bf16).reshape((2,) * len(ex_axes) + (shard, -1))
    grad_heads = after(grad_heads, dense, mixture, grad_received[1])
    dense_one = scatter_bits(dense, ex_axes[-1:], ex_axes)
    dense_two = scatter_bits(dense_one, ex_axes[-2:-1], ex_axes[:-1])
    dense = scatter_bits(dense_two, ex_axes[:-2][::-1], ex_axes[:-2])

    grad_proj = attend_back(q, k, v, grad_heads, lse, docs_col, docs_row, cosine, sine)
    back = lax.all_to_all(grad_proj.reshape(count, local, SLAB), ex_axes, 0, 0, tiled=True)
    back = back[:units].reshape(batches, KV_HEADS, local, SLAB).transpose(0, 2, 1, 3)
    back = jnp.concatenate(
        [
            back[..., :LANES].reshape(rows, -1),
            back[..., LANES : 2 * LANES].reshape(rows, -1),
            back[..., 2 * LANES : 2 * LANES + HEAD_DIM].reshape(rows, -1),
        ],
        1,
    )
    grad_first = dot(after(back, dense_two), qkv_full, 1, 1)
    grad_slab = dot(first_low, grad_proj, 0, 0)
    grad_slab = scatter_bits(
        grad_slab.reshape((2,) * len(dp_axes) + (-1, SLAB)), dp_axes, dp_axes
    )
    grad_slab = lax.all_to_all(
        after(grad_slab.astype(bf16), dense_one).reshape(count, shard, SLAB), ex_axes, 0, 0, tiled=True
    )
    grad_slab = jnp.sum(
        grad_slab[:units].reshape(batches, KV_HEADS, shard, SLAB).astype(f32), 0
    ).transpose(1, 0, 2)
    grad_qkv = join_columns(
        grad_slab[..., :LANES],
        grad_slab[..., LANES : 2 * LANES],
        grad_slab[..., 2 * LANES : 2 * LANES + HEAD_DIM],
    )
    grad_received = after(jnp.concatenate(grad_received, 0), grad_slab)
    grad_packed = sum(t.astype(f32) for t in (*grad_mine, grad_received))
    grad_gate_up = grad_packed[:, : 2 * EXP_FF]
    grad_down = unpack_down(grad_packed, blocks)
    mixed = y_one + after(mixtures, grad_slab).astype(f32)
    grad_gain_attn = jnp.sum(grad_qkv * w_qkv.astype(f32), -1) / norm_attn.astype(f32)
    r_one = lax.rsqrt(jnp.mean(x * x, -1, keepdims=True) + epsilon)
    n_one = x * r_one
    c_one = grad_first * gain_attn
    grad_tokens = grad_y + r_one * (c_one - n_one * jnp.mean(c_one * n_one, -1, keepdims=True))

    out_width = HEADS * HEAD_DIM
    return (
        mixed.astype(bf16).reshape(tokens.shape),
        grad_tokens.reshape(tokens.shape),
        grad_qkv,
        dense[:, :out_width],
        dense[:, out_width : out_width + experts],
        grad_gain_attn,
        dense[:, out_width + experts],
        grad_gate_up[None],
        grad_down[None],
    )


def solution(mesh):
    dp_bits = int(math.log2(mesh.shape["dp"]))
    ex_bits = int(math.log2(mesh.shape["expert"]))
    dp_axes = tuple(f"d{b}" for b in reversed(range(dp_bits)))
    ex_axes = tuple(f"e{b}" for b in reversed(range(ex_bits)))
    cube = Mesh(mesh.devices.reshape((2,) * (dp_bits + ex_bits)), dp_axes + ex_axes)
    every = dp_axes + ex_axes
    by_tokens = P(None, every, None)

    def run(*arrays):
        return on_device(dp_axes, ex_axes, *arrays)

    return jax.shard_map(
        run,
        mesh=cube,
        in_specs=(
            by_tokens,
            by_tokens,
            P(None, every),
            P(None, every),
            by_tokens,
            P(every, None),
            P(every, None),
            P(every, None),
            P(every),
            P(every),
            P(ex_axes, dp_axes, None),
            P(ex_axes, dp_axes, None),
        ),
        out_specs=(
            by_tokens,
            by_tokens,
            P(every, None),
            P(every, None),
            P(every, None),
            P(every),
            P(every),
            P(ex_axes, dp_axes, None),
            P(ex_axes, dp_axes, None),
        ),
        check_vma=False,
    )
```

```python
import math

import jax
import jax.numpy as jnp
from jax import lax
from jax.experimental import pallas as pl
from jax.experimental.pallas import tpu as pltpu
from jax.sharding import Mesh
from jax.sharding import PartitionSpec as P

HEADS = 24
KV_HEADS = 8
HEAD_DIM = 64
EXP_FF = 512
TOP = 8

epsilon = 1e-06
rope_base = 10000.0
masked = -1e30

GROUP = HEADS // KV_HEADS
HALF = HEAD_DIM // 2
LANES = 128
SLAB = 3 * LANES
META_ROWS = 16
BLOCK = 256
SWAP = [(0, 1), (1, 0)]
bf16 = jnp.bfloat16
f32 = jnp.float32


def dot(a, b, da, db):
    return lax.dot_general(a, b, (((da,), (db,)), ((), ())), preferred_element_type=f32)


def gather_bits(x, order, every, waits={}):
    have = []
    for i, axis in enumerate(order):
        if i in waits:
            x = after(x, waits[i])
        other = lax.ppermute(x, axis, SWAP)
        place = sum(every.index(h) < every.index(axis) for h in have)
        first = lax.axis_index(axis) == 0
        x = jnp.stack([jnp.where(first, x, other), jnp.where(first, other, x)], place)
        have.append(axis)
    return x


def after(x, *others):
    return lax.optimization_barrier((x, *others))[0]


def scatter_bits(x, order, every, sends=None):
    left = list(every)
    for axis in order:
        place = left.index(axis)
        mine = lax.axis_index(axis)
        keep = lax.dynamic_index_in_dim(x, mine, place, keepdims=False)
        send = lax.dynamic_index_in_dim(x, 1 - mine, place, keepdims=False)
        send = send.astype(bf16)
        if sends is not None:
            sends.append(send)
        other = lax.ppermute(send, axis, SWAP)
        left.pop(place)
        x = keep.astype(f32) + other.astype(f32)
        if left:
            x = x.astype(bf16)
    return x


def project_kernel(a_ref, b_ref, gain_ref, w_ref, cos_ref, sin_ref, low_ref, q_ref, k_ref, v_ref):
    step = pl.program_id(0)
    half = pl.num_programs(0) // 2

    def work(x_ref):
        x = x_ref[...].astype(f32)
        r = lax.rsqrt(jnp.mean(x * x, -1, keepdims=True) + epsilon)
        low = (x * r * gain_ref[...]).astype(bf16)
        low_ref[...] = low
        p = dot(low, w_ref[...], 1, 0)
        lane = lax.broadcasted_iota(jnp.int32, (x.shape[0], LANES), 1)
        u, w = p[:, :LANES], p[:, LANES : 2 * LANES]
        v = jnp.where(lane < HEAD_DIM, p[:, 2 * LANES :], 0.0)
        c, s = cos_ref[...], sin_ref[...]
        for at, turned in ((0, u * c - w * s), (LANES, w * c + u * s)):
            key = jnp.where(lane >= GROUP * HALF, turned, 0.0)
            key = pltpu.roll(key, HALF, 1) + pltpu.roll(key, 2 * HALF, 1) + pltpu.roll(key, 3 * HALF, 1)
            k_ref[:, at : at + LANES] = key.astype(bf16)
            for h in range(GROUP):
                q_ref[h, :, at : at + LANES] = jnp.where(lane // HALF == h, turned, 0.0).astype(bf16)
        zero = jnp.zeros(v.shape, bf16)
        first, second = v.astype(bf16), pltpu.roll(v, HEAD_DIM, 1).astype(bf16)
        for h in range(GROUP):
            for at in range(2):
                part = zero if h // 2 != at else (first if h % 2 == 0 else second)
                v_ref[h, :, at * LANES : (at + 1) * LANES] = part

    pl.when(step < half)(lambda: work(a_ref))
    pl.when(step >= half)(lambda: work(b_ref))


def project(part_a, part_b, gain, w_slab, cosine, sine):
    rows, width = part_a.shape
    length = 2 * rows
    steps = length // BLOCK
    half = steps // 2
    wide = 2 * LANES
    row = lambda cols: pl.BlockSpec((BLOCK, cols), lambda i: (i, 0))
    heads = pl.BlockSpec((GROUP, BLOCK, wide), lambda i: (0, i, 0))
    return pl.pallas_call(
        project_kernel,
        grid=(steps,),
        in_specs=[
            pl.BlockSpec((BLOCK, width), lambda i: (jnp.minimum(i, half - 1), 0)),
            pl.BlockSpec((BLOCK, width), lambda i: (jnp.maximum(i - half, 0), 0)),
            pl.BlockSpec((1, width), lambda i: (0, 0)),
            pl.BlockSpec((width, SLAB), lambda i: (0, 0)),
            row(LANES),
            row(LANES),
        ],
        out_specs=[row(width), heads, row(wide), heads],
        out_shape=[
            jax.ShapeDtypeStruct((length, width), bf16),
            jax.ShapeDtypeStruct((GROUP, length, wide), bf16),
            jax.ShapeDtypeStruct((length, wide), bf16),
            jax.ShapeDtypeStruct((GROUP, length, wide), bf16),
        ],
        compiler_params=pltpu.CompilerParams(vmem_limit_bytes=40 * 2**20),
        cost_estimate=pl.CostEstimate(
            flops=2 * length * width * SLAB, bytes_accessed=12 * 2**20, transcendentals=length
        ),
    )(part_a, part_b, gain, w_slab, cosine, sine)


def allowed_block(col_ref, row_ref, start, width):
    shape = (BLOCK, width)
    places = start + lax.broadcasted_iota(jnp.int32, shape, 0)
    keys = lax.broadcasted_iota(jnp.int32, shape, 1)
    same = col_ref[start : start + BLOCK, :] == row_ref[:, :width]
    return same & (keys <= places)


def attend_kernel(q_ref, k_ref, v_ref, col_ref, row_ref, o_ref, lse_ref):
    lane = lax.broadcasted_iota(jnp.int32, (BLOCK, LANES), 1)
    for start in range(0, k_ref.shape[0], BLOCK):
        width = start + BLOCK
        rows = slice(start, width)
        allowed = allowed_block(col_ref, row_ref, start, width)
        total = jnp.zeros((BLOCK, 2 * LANES), f32)
        logs = jnp.zeros((BLOCK, LANES), f32)
        for h in range(GROUP):
            s = dot(q_ref[h, rows, :], k_ref[:width, :], 1, 1) * 0.125
            s = jnp.where(allowed, s, masked)
            top = jnp.max(s, -1, keepdims=True)
            p = jnp.exp(s - top)
            below = jnp.sum(p, -1, keepdims=True)
            total = total + dot((p / below).astype(bf16), v_ref[h, :width, :], 1, 0)
            logs = jnp.where(lane == h, top + jnp.log(below), logs)
        o_ref[rows, :] = total.astype(bf16)
        lse_ref[rows, :] = logs


def attend(q, k, v, docs_col, docs_row):
    length, wide = k.shape
    return pl.pallas_call(
        attend_kernel,
        out_shape=[
            jax.ShapeDtypeStruct((length, wide), bf16),
            jax.ShapeDtypeStruct((length, LANES), f32),
        ],
        compiler_params=pltpu.CompilerParams(vmem_limit_bytes=48 * 2**20),
        cost_estimate=pl.CostEstimate(
            flops=2 * GROUP * length * length * wide,
            bytes_accessed=8 * 2**20,
            transcendentals=GROUP * length * length // 2,
        ),
    )(q, k, v, docs_col, docs_row)


def attend_back_kernel(
    q_ref, k_ref, v_ref, g_ref, lse_ref, col_ref, row_ref, cos_ref, sin_ref, out_ref, dk_ref, dv_ref
):
    length = k_ref.shape[0]
    wide = 2 * LANES
    dk_ref[...] = jnp.zeros_like(dk_ref)
    dv_ref[...] = jnp.zeros_like(dv_ref)
    lane = lax.broadcasted_iota(jnp.int32, (BLOCK, LANES), 1)
    wide_lane = lax.broadcasted_iota(jnp.int32, (BLOCK, wide), 1)
    for start in range(0, length, BLOCK):
        width = start + BLOCK
        rows = slice(start, width)
        allowed = allowed_block(col_ref, row_ref, start, width)
        dq = jnp.zeros((BLOCK, wide), f32)
        grads = g_ref[rows, :].astype(f32)
        for h in range(GROUP):
            q = q_ref[h, rows, :]
            lse = jnp.sum(jnp.where(lane == h, lse_ref[rows, :], 0.0), -1, keepdims=True)
            s = dot(q, k_ref[:width, :], 1, 1) * 0.125
            p = jnp.where(allowed, jnp.exp(jnp.where(allowed, s, masked) - lse), 0.0)
            g = jnp.where(wide_lane // HEAD_DIM == h, grads, 0.0).astype(bf16)
            dp = dot(g, v_ref[h, :width, :], 1, 1)
            delta = jnp.sum(p * dp, -1, keepdims=True)
            ds = (p * (dp - delta)).astype(bf16)
            part = dot(ds, k_ref[:width, :], 1, 0)
            dq = dq + jnp.where(wide_lane % LANES // HALF == h, part, 0.0)
            dk_ref[:width, :] += dot(ds, q, 0, 0)
            dv_ref[:width, :] += dot(p.astype(bf16), g, 0, 0)
        out_ref[rows, :LANES] = dq[:, :LANES].astype(out_ref.dtype)
        out_ref[rows, LANES:wide] = dq[:, LANES:].astype(out_ref.dtype)
    for start in range(0, length, BLOCK):
        rows = slice(start, start + BLOCK)
        halves = []
        for at in (0, LANES):
            key = dk_ref[rows, at : at + LANES]
            key = pltpu.roll(key, 3 * HALF, 1) + pltpu.roll(key, 2 * HALF, 1) + pltpu.roll(key, HALF, 1)
            both = jnp.where(lane >= GROUP * HALF, key, out_ref[rows, at : at + LANES])
            halves.append(both * 0.125)
        c, s = cos_ref[rows, :], sin_ref[rows, :]
        u, w = halves
        out_ref[rows, :LANES] = u * c + w * s
        out_ref[rows, LANES:wide] = w * c - u * s
        v = dv_ref[rows, :LANES] + dv_ref[rows, LANES:]
        v = v + pltpu.roll(v, HEAD_DIM, 1)
        out_ref[rows, wide:] = jnp.where(lane < HEAD_DIM, v, 0.0)


def attend_back_entry(*refs):
    *ins, out_ref, full_ref, dk_ref, dv_ref = refs
    attend_back_kernel(*ins, full_ref, dk_ref, dv_ref)
    out_ref[...] = full_ref[...].astype(bf16)


def attend_back(q, k, v, g, lse, docs_col, docs_row, cosine, sine):
    length, wide = k.shape
    return pl.pallas_call(
        attend_back_entry,
        out_shape=jax.ShapeDtypeStruct((length, SLAB), bf16),
        scratch_shapes=[
            pltpu.VMEM((length, SLAB), f32),
            pltpu.VMEM((length, wide), f32),
            pltpu.VMEM((length, wide), f32),
        ],
        compiler_params=pltpu.CompilerParams(vmem_limit_bytes=52 * 2**20),
        cost_estimate=pl.CostEstimate(
            flops=5 * GROUP * length * length * wide,
            bytes_accessed=8 * 2**20,
            transcendentals=GROUP * length * length // 2,
        ),
    )(q, k, v, g, lse, docs_col, docs_row, cosine, sine)


def pack(gate_up, down):
    blocks = [down[:, c : c + EXP_FF] for c in range(0, down.shape[1], EXP_FF)]
    return jnp.concatenate([gate_up, jnp.concatenate(blocks, 0)], 1)


def unpack_down(packed, high):
    rows = packed.shape[0] // high
    return jnp.concatenate([packed[c * rows : (c + 1) * rows, 2 * EXP_FF :] for c in range(high)], 1)


def half_places(at_ref, half, size):
    high = at_ref[2]
    place = high if half == 0 else 1 - high
    return pl.multiple_of(place * size, LANES)


def plain_kernel(at_ref, g_ref, pa, pb, pc, pd, out_ref):
    rows = g_ref.shape[0] * g_ref.shape[2]
    part = EXP_FF // 2
    width = g_ref.shape[3]
    g = g_ref[:, 0].reshape(rows, width)
    for j, packed in enumerate(((pa, pb), (pc, pd))):
        for half, p in enumerate(packed):
            plain = None
            for c in range(width // EXP_FF):
                cols = slice(c * EXP_FF, (c + 1) * EXP_FF)
                term = dot(g[:, cols], p[c * part : (c + 1) * part, :], 1, 1)
                plain = term if plain is None else plain + term
            at = pl.multiple_of(j * EXP_FF + half_places(at_ref, half, part), LANES)
            out_ref[:, 0, :, pl.ds(at, part)] = plain.reshape(g_ref.shape[0], g_ref.shape[2], part)


def plain_grads(places, grads, packed):
    holders, batches, local, width = grads.shape
    size = packed[0].shape[0]
    near = BLOCK // local
    block = lambda cols: pl.BlockSpec((near, 1, local, cols), lambda i, m, _: (i, m, 0, 0))
    return pl.pallas_call(
        plain_kernel,
        grid_spec=pltpu.PrefetchScalarGridSpec(
            num_scalar_prefetch=1,
            grid=(holders // near, batches),
            in_specs=[
                block(width),
                *[pl.BlockSpec((size, EXP_FF), lambda i, m, _: (0, 2))] * 4,
            ],
            out_specs=block(2 * EXP_FF),
        ),
        out_shape=jax.ShapeDtypeStruct((holders, batches, local, 2 * EXP_FF), f32),
        compiler_params=pltpu.CompilerParams(vmem_limit_bytes=40 * 2**20),
        cost_estimate=pl.CostEstimate(
            flops=4 * holders * batches * local * width * EXP_FF,
            bytes_accessed=14 * 2**20,
            transcendentals=0,
        ),
    )(places, grads, *packed)


def expert_kernel(at_ref, x_ref, g_ref, pa, pb, pc, pd, sum_ref, hid_ref, pair_ref):
    rows = x_ref.shape[0]
    size, width = pa.shape[0], 2 * pa.shape[0]
    double = 2 * EXP_FF
    me, experts = at_ref[0], at_ref[1]
    extra = x_ref[:, width:].astype(f32)
    both_plain = g_ref[:, 0].reshape(rows, double)
    lane = lax.broadcasted_iota(jnp.int32, extra.shape, 1)
    back = jnp.zeros(extra.shape, f32)
    totals = [None, None]
    for j, packed in enumerate(((pa, pb), (pc, pd))):
        expert = me if j == 0 else me ^ 4
        high = lane == expert
        low = lane == expert + experts
        share = jnp.sum(jnp.where(high | low, extra, 0.0), -1, keepdims=True)
        gate_up = None
        for half, p in enumerate(packed):
            term = dot(x_ref[:, pl.ds(half_places(at_ref, half, size), size)], p[...], 1, 0)
            gate_up = term if gate_up is None else gate_up + term
        gate, up = gate_up[:, :EXP_FF], gate_up[:, EXP_FF:]
        sg = 1.0 / (1.0 + jnp.exp(-gate))
        grown = gate * sg
        hidden = (grown * up).astype(bf16).astype(f32)
        grad_plain = both_plain[:, j * EXP_FF : (j + 1) * EXP_FF]
        gate_grad = jnp.sum(grad_plain * hidden, -1, keepdims=True)
        gate_high = gate_grad.astype(bf16).astype(f32)
        back = jnp.where(high, gate_high, jnp.where(low, gate_grad - gate_high, back))
        grad_hidden = share * grad_plain
        at = j * EXP_FF
        hid_ref[:, at : at + EXP_FF] = (share * hidden).astype(bf16)
        at = j * double
        first = (grad_hidden * up * sg * (1.0 + gate * (1.0 - sg))).astype(bf16)
        pair_ref[:, at : at + EXP_FF] = first
        pair_ref[:, at + EXP_FF : at + double] = (grad_hidden * grown).astype(bf16)
        for half, p in enumerate(packed):
            term = dot(pair_ref[:, at : at + double], p[...], 1, 1)
            totals[half] = term if totals[half] is None else totals[half] + term
    for half in range(2):
        sum_ref[:, pl.ds(half_places(at_ref, half, size), size)] = totals[half].astype(bf16)
    sum_ref[:, width:] = back.astype(bf16)


def run_experts(places, x, plain, m, packed):
    rows, wide = x.shape
    local = plain.shape[2]
    size, width = packed[0].shape
    block = lambda cols: pl.BlockSpec((BLOCK, cols), lambda i, _: (i, 0))
    whole = pl.BlockSpec((size, 2 * EXP_FF), lambda i, _: (0, 0))
    return pl.pallas_call(
        expert_kernel,
        grid_spec=pltpu.PrefetchScalarGridSpec(
            num_scalar_prefetch=1,
            grid=(rows // BLOCK,),
            in_specs=[
                block(wide),
                pl.BlockSpec((BLOCK // local, 1, local, 2 * EXP_FF), lambda i, _: (i, m, 0, 0)),
                *[whole] * 4,
            ],
            out_specs=[block(wide), block(2 * EXP_FF), block(4 * EXP_FF)],
        ),
        out_shape=[
            jax.ShapeDtypeStruct((rows, wide), bf16),
            jax.ShapeDtypeStruct((rows, 2 * EXP_FF), bf16),
            jax.ShapeDtypeStruct((rows, 4 * EXP_FF), bf16),
        ],
        compiler_params=pltpu.CompilerParams(vmem_limit_bytes=56 * 2**20),
        cost_estimate=pl.CostEstimate(
            flops=16 * rows * width * EXP_FF, bytes_accessed=16 * 2**20, transcendentals=rows * 2 * EXP_FF
        ),
    )(places, x, plain, *packed)


def mixture_kernel(at_ref, a_ref, b_ref, pa, pb, pc, pd, out_ref):
    size, width = pa.shape
    part = EXP_FF // 2

    def work(hid_ref):
        for c in range(width // EXP_FF):
            total = None
            for j, packed in enumerate(((pa, pb), (pc, pd))):
                for half, p in enumerate(packed):
                    at = pl.multiple_of(j * EXP_FF + half_places(at_ref, half, part), LANES)
                    term = dot(
                        hid_ref[:, pl.ds(at, part)],
                        p[c * part : (c + 1) * part, 2 * EXP_FF :],
                        1,
                        0,
                    )
                    total = term if total is None else total + term
            cols = slice(c * EXP_FF, (c + 1) * EXP_FF)
            shape = out_ref.shape[0], out_ref.shape[2], EXP_FF
            out_ref[:, 0, :, cols] = total.astype(bf16).reshape(shape)

    pl.when(pl.program_id(0) == 0)(lambda: work(a_ref))
    pl.when(pl.program_id(0) == 1)(lambda: work(b_ref))


def mix_experts(places, weighted, local, packed):
    rows = weighted[0].shape[0]
    size, width = packed[0].shape
    blocks = rows // BLOCK
    whole = pl.BlockSpec((size, width), lambda m, i, _: (0, 0))
    first = pl.BlockSpec((BLOCK, 2 * EXP_FF), lambda m, i, _: (jnp.where(m == 0, i, blocks - 1), 0))
    second = pl.BlockSpec((BLOCK, 2 * EXP_FF), lambda m, i, _: (jnp.where(m == 1, i, 0), 0))
    return pl.pallas_call(
        mixture_kernel,
        grid_spec=pltpu.PrefetchScalarGridSpec(
            num_scalar_prefetch=1,
            grid=(2, blocks),
            in_specs=[first, second, *[whole] * 4],
            out_specs=pl.BlockSpec(
                (BLOCK // local, 1, local, width), lambda m, i, _: (i, m, 0, 0)
            ),
        ),
        out_shape=jax.ShapeDtypeStruct((rows // local, 2, local, width), bf16),
        compiler_params=pltpu.CompilerParams(vmem_limit_bytes=48 * 2**20),
        cost_estimate=pl.CostEstimate(
            flops=8 * rows * width * EXP_FF, bytes_accessed=16 * 2**20, transcendentals=0
        ),
    )(places, *weighted, *packed)


def weights_kernel(
    at_ref, xa_ref, xb_ref, g_ref, ha_ref, hb_ref, pa_ref, pb_ref, send_ref, keep_ref
):
    size, width = keep_ref.shape
    rows = xa_ref.shape[0]
    part = EXP_FF // 2
    double = 2 * EXP_FF

    def work(half, out_ref):
        cols = pl.ds(half_places(at_ref, half, size), size)
        total = dot(xa_ref[:, cols], pa_ref[...], 0, 0) + dot(xb_ref[:, cols], pb_ref[...], 0, 0)
        out_ref[:, :double] = total.astype(out_ref.dtype)
        cols = pl.ds(half_places(at_ref, half, part), part)
        for c in range(width // EXP_FF):
            at = slice(c * EXP_FF, (c + 1) * EXP_FF)
            total = dot(ha_ref[:, cols], g_ref[:, 0, :, at].reshape(rows, EXP_FF), 0, 0)
            total = total + dot(hb_ref[:, cols], g_ref[:, 1, :, at].reshape(rows, EXP_FF), 0, 0)
            out_ref[c * part : (c + 1) * part, double:] = total.astype(out_ref.dtype)

    pl.when(pl.program_id(0) == 0)(lambda: work(1, send_ref))
    pl.when(pl.program_id(0) == 1)(lambda: work(0, keep_ref))


def expert_weights(j, places, xs, grads, weighted, pairs):
    rows, wide = xs[0].shape
    width = grads.shape[3]
    size = width // 2
    whole = pl.BlockSpec((rows, wide), lambda h, _: (0, 0))
    hidden = pl.BlockSpec((rows, EXP_FF), lambda h, _: (0, j))
    pair = pl.BlockSpec((rows, 2 * EXP_FF), lambda h, _: (0, j))
    half = pl.BlockSpec((size, width), lambda h, _: (0, 0))
    return pl.pallas_call(
        weights_kernel,
        grid_spec=pltpu.PrefetchScalarGridSpec(
            num_scalar_prefetch=1,
            grid=(2,),
            in_specs=[
                whole,
                whole,
                pl.BlockSpec(grads.shape, lambda h, _: (0, 0, 0, 0)),
                hidden,
                hidden,
                pair,
                pair,
            ],
            out_specs=[half, half],
        ),
        out_shape=[
            jax.ShapeDtypeStruct((size, width), bf16),
            jax.ShapeDtypeStruct((size, width), f32 if j == 0 else bf16),
        ],
        compiler_params=pltpu.CompilerParams(vmem_limit_bytes=60 * 2**20),
        cost_estimate=pl.CostEstimate(
            flops=12 * rows * width * EXP_FF, bytes_accessed=16 * 2**20, transcendentals=0
        ),
    )(places, *xs, grads, *weighted, *pairs)


def heads_to_rows(a, b):
    lane = lax.broadcasted_iota(jnp.int32, (a.shape[0], LANES), 1)
    low = lane < HEAD_DIM
    b_first, b_second = (pltpu.roll(t, HEAD_DIM, 1) for t in (b[:, :LANES], b[:, LANES:]))
    return (a[:, :LANES], jnp.where(low, a[:, LANES:], b_first), jnp.where(low, b_first, b_second))


def rows_to_heads(first, second, third):
    lane = lax.broadcasted_iota(jnp.int32, first.shape, 1)
    low = lane < HEAD_DIM
    second_turned, third_turned = (pltpu.roll(t, HEAD_DIM, 1) for t in (second, third))
    a = (first, jnp.where(low, second, 0.0))
    b = (jnp.where(low, second_turned, third_turned), jnp.where(low, third_turned, 0.0))
    return a, b


def middle_kernel(
    experts, heads_ref, x_ref, w_ref, gain_ref, router_ref, routes_ref,
    y_ref, sent_ref, low_ref, probs_ref, gates_ref, chosen_ref, pick_ref, scale_ref,
):
    batches, local, width = x_ref.shape
    for m in range(batches):
        for k in range(0, KV_HEADS, 2):
            a, b = (heads_ref[m * KV_HEADS + k + i].astype(f32) for i in range(2))
            at = k * GROUP * HEAD_DIM
            for i, part in enumerate(heads_to_rows(a, b)):
                cols = slice(at + i * LANES, at + (i + 1) * LANES)
                low_ref[m * local : (m + 1) * local, cols] = part.astype(bf16)
    rows = batches * local
    y = x_ref[...].reshape(rows, width).astype(f32) + dot(low_ref[...], w_ref[...], 1, 1)
    y_ref[...] = y
    r = lax.rsqrt(jnp.mean(y * y, -1, keepdims=True) + epsilon)
    second = (y * r * gain_ref[...]).astype(bf16)
    lane = lax.broadcasted_iota(jnp.int32, (rows, LANES), 1)
    logits = jnp.where(lane < experts, dot(second, router_ref[...], 1, 0), masked)
    raised = jnp.exp(logits - jnp.max(logits, -1, keepdims=True))
    probs = raised / jnp.sum(raised, -1, keepdims=True)
    chosen = jnp.zeros((rows, LANES), f32)
    for k in range(TOP):
        chosen = jnp.where(routes_ref[:, k : k + 1] == lane, 1.0, chosen)
    picked = jnp.sum(chosen * probs, -1, keepdims=True)
    gates = chosen * probs / picked
    high = gates.astype(bf16).astype(f32)
    extra = high + pltpu.roll(gates - high, experts, 1)
    sent_ref[:, :, :width] = second.reshape(batches, local, width)
    sent_ref[:, :, width:] = extra.astype(bf16).reshape(batches, local, LANES)
    probs_ref[...] = probs
    gates_ref[...] = gates
    chosen_ref[...] = chosen
    pick_ref[...] = picked
    scale_ref[...] = r


def middle_rows(experts, heads, tokens, out_full, gain, router, routes):
    batches, local, width = tokens.shape
    rows = batches * local
    small = jax.ShapeDtypeStruct((rows, LANES), f32)
    column = jax.ShapeDtypeStruct((rows, 1), f32)
    return pl.pallas_call(
        lambda *refs: middle_kernel(experts, *refs),
        out_shape=[
            jax.ShapeDtypeStruct((rows, width), f32),
            jax.ShapeDtypeStruct((batches, local, width + LANES), bf16),
            jax.ShapeDtypeStruct((rows, width), bf16),
            small,
            small,
            small,
            column,
            column,
        ],
        compiler_params=pltpu.CompilerParams(vmem_limit_bytes=40 * 2**20),
        cost_estimate=pl.CostEstimate(
            flops=2 * rows * width * width, bytes_accessed=8 * 2**20, transcendentals=rows * LANES
        ),
    )(heads, tokens, out_full, gain, router, routes)


def middle_back_kernel(
    experts, came_a_ref, came_b_ref, g_ref, y_ref, probs_ref, gates_ref, chosen_ref,
    pick_ref, scale_ref, gain_ref, router_ref, w_ref,
    heads_ref, grad_ref, branch_ref, logits_ref, gain_grad_ref,
):
    batches, local, width = g_ref.shape
    rows = batches * local
    came = jnp.concatenate([came_a_ref[...], came_b_ref[...]], 0)
    extra = came[:, width:]
    lane = lax.broadcasted_iota(jnp.int32, (rows, LANES), 1)
    chosen, probs, gates = chosen_ref[...], probs_ref[...], gates_ref[...]
    both = extra + pltpu.roll(extra, LANES - experts, 1)
    grad_gates = jnp.where(lane < experts, both, 0.0) * chosen
    mean = jnp.sum(grad_gates * gates, -1, keepdims=True)
    grad_picked = chosen * (grad_gates - mean) / pick_ref[...]
    grad_logits = probs * (grad_picked - jnp.sum(probs * grad_picked, -1, keepdims=True))
    grad_logits = grad_logits.astype(bf16)
    logits_ref[...] = grad_logits
    grad_second = came[:, :width] + dot(grad_logits, router_ref[...], 1, 1)
    r = scale_ref[...]
    n = y_ref[...] * r
    gain_grad_ref[...] = jnp.sum(grad_second * n, 0, keepdims=True)
    c = grad_second * gain_ref[...]
    grad_y = g_ref[...].reshape(rows, width).astype(f32)
    grad_y = grad_y + r * (c - n * jnp.mean(c * n, -1, keepdims=True))
    grad_ref[...] = grad_y
    branch = grad_y.astype(bf16)
    branch_ref[...] = branch
    grad = dot(branch, w_ref[...], 1, 0)
    for k in range(0, KV_HEADS, 2):
        at = k * GROUP * HEAD_DIM
        parts = (grad[:, at + i * LANES : at + (i + 1) * LANES] for i in range(3))
        for j, head in enumerate(rows_to_heads(*parts)):
            for i, part in enumerate(head):
                part = part.astype(bf16).reshape(batches, local, LANES)
                for m in range(batches):
                    cols = slice(i * LANES, (i + 1) * LANES)
                    heads_ref[m * KV_HEADS + k + j, :, cols] = part[m]


def middle_back(experts, came, cotangent, kept, gain, router, out_full):
    batches, local, width = cotangent.shape
    rows = batches * local
    return pl.pallas_call(
        lambda *refs: middle_back_kernel(experts, *refs),
        out_shape=[
            jax.ShapeDtypeStruct((batches * KV_HEADS, local, 2 * LANES), bf16),
            jax.ShapeDtypeStruct((rows, width), f32),
            jax.ShapeDtypeStruct((rows, width), bf16),
            jax.ShapeDtypeStruct((rows, LANES), bf16),
            jax.ShapeDtypeStruct((1, width), f32),
        ],
        compiler_params=pltpu.CompilerParams(vmem_limit_bytes=40 * 2**20),
        cost_estimate=pl.CostEstimate(
            flops=2 * rows * width * width, bytes_accessed=10 * 2**20, transcendentals=0
        ),
    )(*came, cotangent, *kept, gain, router, out_full)


def split_columns(w_qkv):
    rows = w_qkv.shape[0]
    q_width, k_width = HEADS * HEAD_DIM, KV_HEADS * HEAD_DIM
    q = w_qkv[:, :q_width].reshape(rows, KV_HEADS, GROUP, 2, HALF)
    k = w_qkv[:, q_width : q_width + k_width].reshape(rows, KV_HEADS, 1, 2, HALF)
    both = jnp.concatenate([q, k], 2)
    return (
        both[:, :, :, 0].reshape(rows, KV_HEADS, LANES),
        both[:, :, :, 1].reshape(rows, KV_HEADS, LANES),
        w_qkv[:, q_width + k_width :].reshape(rows, KV_HEADS, HEAD_DIM),
    )


def join_columns(u, w, v):
    rows = u.shape[0]
    both = jnp.stack(
        [u.reshape(rows, KV_HEADS, GROUP + 1, HALF), w.reshape(rows, KV_HEADS, GROUP + 1, HALF)], 3
    )
    return jnp.concatenate(
        [
            both[:, :, :GROUP].reshape(rows, HEADS * HEAD_DIM),
            both[:, :, GROUP:].reshape(rows, KV_HEADS * HEAD_DIM),
            v.reshape(rows, KV_HEADS * HEAD_DIM),
        ],
        1,
    )


def halves(x):
    high = lax.reduce_precision(x, 8, 7)
    return high.astype(bf16), (x - high).astype(bf16)


def gather_sequence(tokens, ex_axes, mb_axis):
    mine = lax.axis_index(mb_axis)
    own = lax.dynamic_index_in_dim(tokens, mine, 0, keepdims=False)
    other = lax.ppermute(
        lax.dynamic_index_in_dim(tokens, 1 - mine, 0, keepdims=False), mb_axis, SWAP
    )
    first = mine == 0
    group = jnp.stack([jnp.where(first, own, other), jnp.where(first, other, own)], 0)
    middle = tuple(a for a in ex_axes[:-2] if a != mb_axis)
    return gather_bits(group, middle, middle), middle, other


def on_device(
    dp_axes,
    ex_axes,
    tokens,
    cotangent,
    segments,
    positions,
    routes,
    w_qkv,
    w_out,
    w_router,
    norm_attn,
    norm_ffn,
    w_gate_up,
    w_down,
):
    batches, local, width = tokens.shape
    experts = w_router.shape[1]
    count = 2 ** len(ex_axes)
    length = count * local
    units = batches * KV_HEADS
    parts = count // units
    shard = w_qkv.shape[0]
    rows = batches * local
    me = lax.axis_index(ex_axes)
    bit = lambda b: ex_axes[len(ex_axes) - 1 - b]
    pair_axis = bit(2)
    token_axes = tuple(a for a in ex_axes if a != pair_axis)
    far = token_axes[:-2]
    orders = (far + (bit(0), bit(1)), far + (bit(1), bit(0)))

    mb_axis = bit(3)

    u_cols, w_cols, v_cols = split_columns(w_qkv)
    small = jnp.concatenate([norm_attn[:, None], norm_ffn[:, None], w_router], 1)
    small = jnp.pad(small, ((0, 0), (0, SLAB - 2 * LANES - HEAD_DIM - small.shape[1])))
    small = jnp.broadcast_to(small[:, None, :], (shard, KV_HEADS, small.shape[1]))
    slab = jnp.transpose(jnp.concatenate([u_cols, w_cols, v_cols, small], -1), (1, 0, 2))
    meta = jnp.stack([segments, positions // 64, positions % 64], 1).astype(bf16)
    meta = jnp.pad(meta, ((0, 0), (0, META_ROWS - 3), (0, SLAB - local)))
    payload = jnp.concatenate(
        [
            jnp.broadcast_to(slab[None], (batches,) + slab.shape),
            jnp.broadcast_to(meta[:, None], (batches, KV_HEADS) + meta.shape[1:]),
        ],
        2,
    ).reshape(units, shard + META_ROWS, SLAB)
    payload = jnp.concatenate([payload] * parts, 0)
    group, middle, swapped = gather_sequence(tokens, ex_axes, mb_axis)
    arrived = lax.all_to_all(after(payload, swapped), ex_axes, 0, 0, tiled=True)
    w_slab = gather_bits(arrived[:, :shard].reshape(count * shard, SLAB), dp_axes, dp_axes)
    w_slab = w_slab.reshape(width, SLAB)
    extra_at = 2 * LANES + HEAD_DIM
    gain_attn = w_slab[:, extra_at].astype(f32)
    gain_ffn = w_slab[:, extra_at + 1].astype(f32)
    router_full = w_slab[:, extra_at + 2 : extra_at + 2 + experts]
    info = arrived[:, shard : shard + 3, :local].astype(jnp.int32)
    docs = info[:, 0].reshape(length)
    places = (info[:, 1] * 64 + info[:, 2]).reshape(length)
    frequency = rope_base ** (-jnp.arange(HALF, dtype=f32) / HALF)
    angles = places.astype(f32)[:, None] * jnp.tile(frequency, GROUP + 1)[None, :]
    cosine, sine = jnp.cos(angles), jnp.sin(angles)
    docs_col, docs_row = docs[:, None], docs[None, :]

    high_axis, low_axes = dp_axes[0], dp_axes[1:]
    blocks = width // EXP_FF
    expert_own = pack(w_gate_up[0], w_down[0])
    if low_axes:
        parted = gather_bits(expert_own, low_axes, low_axes)
        parted = parted.reshape((-1,) + expert_own.shape)
        lower = parted[..., 2 * EXP_FF :].reshape(parted.shape[0], blocks, -1, EXP_FF)
        expert_own = jnp.concatenate(
            [
                parted[..., : 2 * EXP_FF].reshape(-1, 2 * EXP_FF),
                lower.transpose(1, 0, 2, 3).reshape(-1, EXP_FF),
            ],
            1,
        )
    group, expert_own = lax.optimization_barrier((group, expert_own))
    group = jnp.moveaxis(group, len(middle), 0)
    sides = []
    for part, last in ((group[0], (bit(0), bit(1))), (group[1], (bit(1), bit(0)))):
        pair = gather_bits(part, last, (bit(1), bit(0)), {1: arrived})
        sides.append(jnp.moveaxis(pair, (0, 1), (len(middle), len(middle) + 1)))
    if len(middle) == 1:
        sides = [s.reshape(length // 2, width) for s in sides]
    else:
        at = ex_axes.index(mb_axis)
        whole = jnp.stack(sides, at).reshape(length, width)
        sides = [whole[: length // 2], whole[length // 2 :]]

    out_full = lax.all_gather(w_out, dp_axes + ex_axes, axis=0, tiled=True)
    grad_rows = lax.all_gather(cotangent, token_axes, axis=0)
    qkv_mixed = jnp.concatenate([p.reshape(shard, -1) for p in (u_cols, w_cols, v_cols)], 1)
    qkv_full = lax.all_gather(qkv_mixed, dp_axes + ex_axes, axis=0, tiled=True)

    cut = expert_own.shape[0] // 2
    other_parts = [lax.ppermute(t, pair_axis, SWAP) for t in (expert_own[:cut], expert_own[cut:])]

    first_low, q, k, v = project(*sides, gain_attn[None, :], w_slab, cosine, sine)
    q = after(q, other_parts[0])
    attended, lse = attend(q, k, v, docs_col, docs_row)
    back = lax.all_to_all(attended.reshape(count, local, 2 * LANES), ex_axes, 0, 0, tiled=True)
    expert_other = jnp.concatenate([after(t, attended) for t in other_parts], 0)
    packed = [
        expert_own,
        lax.ppermute(expert_own, high_axis, SWAP),
        expert_other,
        lax.ppermute(expert_other, high_axis, SWAP),
    ]
    x = tokens.reshape(rows, width).astype(f32)
    router_full = jnp.pad(router_full, ((0, 0), (0, LANES - experts)))
    y_one, sent, attended_low, *kept = middle_rows(
        experts, back[:units], tokens, out_full, gain_ffn[None, :], router_full, routes.reshape(rows, TOP)
    )
    second_low = sent[:, :, :width].reshape(rows, width)
    sent = after(sent, other_parts[1])

    places_at = jnp.stack([me, jnp.int32(experts), lax.axis_index(high_axis)]).astype(jnp.int32)
    weighted, pairs, stages = [], [], []
    gathered = []
    ahead = sent
    for m in range(batches):
        far_part = gather_bits(after(sent[m], ahead), far, far)
        ahead = far_part
        if m == 0:
            grads = after(grad_rows, far_part)
            plain = plain_grads(places_at, grads, packed)
        last = orders[m % 2][len(far) :]
        part = gather_bits(far_part, last, (bit(1), bit(0)), {1: plain} if m else {})
        part = jnp.moveaxis(part, (0, 1), (len(far), len(far) + 1))
        gathered.append(part.reshape(-1, width + LANES))
    for m in range(batches):
        back_rows, hid, pair = run_experts(places_at, gathered[m], plain, m, packed)
        back_rows = back_rows.reshape((2,) * len(token_axes) + (local, width + LANES))
        stages.append(scatter_bits(back_rows, orders[m % 2][-1:], token_axes))
        weighted.append(hid)
        pairs.append(pair)
    grad_inputs = []
    for m in range(batches):
        order = orders[m % 2][::-1]
        left = tuple(a for a in token_axes if a != order[0])
        grad_inputs.append(scatter_bits(stages[m], order[1:], left))

    def expert_grads(j, *others):
        send, keep = expert_weights(
            j, places_at, gathered, grad_rows, [after(t, *others) for t in weighted], pairs
        )
        grad = keep.astype(f32) + lax.ppermute(send, high_axis, SWAP).astype(f32)
        if low_axes:
            count_low = 2 ** len(low_axes)
            parted = grad[:, : 2 * EXP_FF].reshape(count_low, -1, 2 * EXP_FF)
            lower = grad[:, 2 * EXP_FF :].reshape(blocks, count_low, -1, EXP_FF)
            lower = lower.transpose(1, 0, 2, 3).reshape(count_low, -1, EXP_FF)
            parted = jnp.concatenate([parted, lower], -1)
            parted = parted.reshape((2,) * len(low_axes) + parted.shape[1:])
            grad = scatter_bits(parted.astype(bf16), low_axes, low_axes)
        return grad

    grad_theirs = expert_grads(1, *stages).astype(bf16)
    cut = grad_theirs.shape[0] // 2
    grad_received = [
        lax.ppermute(t, pair_axis, SWAP) for t in (grad_theirs[:cut], grad_theirs[cut:])
    ]
    grad_inputs[-1] = after(grad_inputs[-1], grad_theirs)

    payload, grad_y, grad_branch, grad_logits, grad_gain_ffn = middle_back(
        experts, grad_inputs, cotangent, [y_one, *kept], gain_ffn[None, :], router_full, out_full
    )
    payload = jnp.concatenate([payload] * parts, 0)
    grad_heads = lax.all_to_all(payload, ex_axes, 0, 0, tiled=True).reshape(length, 2 * LANES)

    mixture = mix_experts(places_at, [after(t, payload) for t in weighted], local, packed)
    mixtures = lax.psum_scatter(
        after(mixture.reshape(-1, width), qkv_full), token_axes, scatter_dimension=0, tiled=True
    )
    grad_branch = after(grad_branch, payload)
    grad_out = dot(grad_branch, attended_low, 0, 0)
    extras = dot(after(second_low, payload), grad_logits, 0, 0)
    extras = jnp.where(jnp.arange(LANES) == experts, grad_gain_ffn.reshape(width, 1), extras)
    dense = jnp.concatenate([grad_out, extras], 1).astype(bf16)
    dense = scatter_bits(
        dense.reshape((2,) * len(dp_axes) + (-1, dense.shape[1])), dp_axes, dp_axes
    )
    dense = dense.astype(bf16).reshape((2,) * len(ex_axes) + (shard, -1))
    grad_heads = after(grad_heads, dense, mixture, grad_received[0])
    dense_one = scatter_bits(dense, ex_axes[-1:], ex_axes)
    dense_two = scatter_bits(dense_one, ex_axes[-2:-1], ex_axes[:-1])
    dense = scatter_bits(dense_two, ex_axes[:-2][::-1], ex_axes[:-2])

    grad_proj = attend_back(q, k, v, grad_heads, lse, docs_col, docs_row, cosine, sine)
    back = lax.all_to_all(grad_proj.reshape(count, local, SLAB), ex_axes, 0, 0, tiled=True)
    back = back[:units].reshape(batches, KV_HEADS, local, SLAB).transpose(0, 2, 1, 3)
    back = jnp.concatenate(
        [
            back[..., :LANES].reshape(rows, -1),
            back[..., LANES : 2 * LANES].reshape(rows, -1),
            back[..., 2 * LANES : 2 * LANES + HEAD_DIM].reshape(rows, -1),
        ],
        1,
    )
    grad_first = dot(after(back, dense_two), qkv_full, 1, 1)
    grad_slab = dot(first_low, grad_proj, 0, 0)
    grad_slab = scatter_bits(
        grad_slab.reshape((2,) * len(dp_axes) + (-1, SLAB)), dp_axes, dp_axes
    )
    grad_slab = lax.all_to_all(
        after(grad_slab.astype(bf16), dense_one, grad_received[1]).reshape(count, shard, SLAB), ex_axes, 0, 0, tiled=True
    )
    grad_slab = jnp.sum(
        grad_slab[:units].reshape(batches, KV_HEADS, shard, SLAB).astype(f32), 0
    ).transpose(1, 0, 2)
    grad_qkv = join_columns(
        grad_slab[..., :LANES],
        grad_slab[..., LANES : 2 * LANES],
        grad_slab[..., 2 * LANES : 2 * LANES + HEAD_DIM],
    )
    grad_packed = expert_grads(0, grad_proj) + jnp.concatenate(grad_received, 0).astype(f32)
    grad_gate_up = grad_packed[:, : 2 * EXP_FF]
    grad_down = unpack_down(grad_packed, blocks)
    mixed = y_one + after(mixtures, grad_slab).astype(f32)
    grad_gain_attn = jnp.sum(grad_qkv * w_qkv.astype(f32), -1) / norm_attn.astype(f32)
    r_one = lax.rsqrt(jnp.mean(x * x, -1, keepdims=True) + epsilon)
    n_one = x * r_one
    c_one = grad_first * gain_attn
    grad_tokens = grad_y + r_one * (c_one - n_one * jnp.mean(c_one * n_one, -1, keepdims=True))

    out_width = HEADS * HEAD_DIM
    return (
        mixed.astype(bf16).reshape(tokens.shape),
        grad_tokens.reshape(tokens.shape),
        grad_qkv,
        dense[:, :out_width],
        dense[:, out_width : out_width + experts],
        grad_gain_attn,
        dense[:, out_width + experts],
        grad_gate_up[None],
        grad_down[None],
    )


def solution(mesh):
    dp_bits = int(math.log2(mesh.shape["dp"]))
    ex_bits = int(math.log2(mesh.shape["expert"]))
    dp_axes = tuple(f"d{b}" for b in reversed(range(dp_bits)))
    ex_axes = tuple(f"e{b}" for b in reversed(range(ex_bits)))
    cube = Mesh(mesh.devices.reshape((2,) * (dp_bits + ex_bits)), dp_axes + ex_axes)
    every = dp_axes + ex_axes
    by_tokens = P(None, every, None)

    def run(*arrays):
        return on_device(dp_axes, ex_axes, *arrays)

    return jax.shard_map(
        run,
        mesh=cube,
        in_specs=(
            by_tokens,
            by_tokens,
            P(None, every),
            P(None, every),
            by_tokens,
            P(every, None),
            P(every, None),
            P(every, None),
            P(every),
            P(every),
            P(ex_axes, dp_axes, None),
            P(ex_axes, dp_axes, None),
        ),
        out_specs=(
            by_tokens,
            by_tokens,
            P(every, None),
            P(every, None),
            P(every, None),
            P(every),
            P(every),
            P(ex_axes, dp_axes, None),
            P(ex_axes, dp_axes, None),
        ),
        check_vma=False,
    )
```

```python
import math

import jax
import jax.numpy as jnp
from jax import lax
from jax.experimental import pallas as pl
from jax.experimental.pallas import tpu as pltpu
from jax.sharding import Mesh
from jax.sharding import PartitionSpec as P

HEADS = 24
KV_HEADS = 8
HEAD_DIM = 64
EXP_FF = 512
TOP = 8

epsilon = 1e-06
rope_base = 10000.0
masked = -1e30

GROUP = HEADS // KV_HEADS
HALF = HEAD_DIM // 2
LANES = 128
SLAB = 3 * LANES
META_ROWS = 16
BLOCK = 256
SWAP = [(0, 1), (1, 0)]
bf16 = jnp.bfloat16
f32 = jnp.float32


def dot(a, b, da, db):
    return lax.dot_general(a, b, (((da,), (db,)), ((), ())), preferred_element_type=f32)


def gather_bits(x, order, every, waits={}):
    have = []
    for i, axis in enumerate(order):
        if i in waits:
            x = after(x, waits[i])
        other = lax.ppermute(x, axis, SWAP)
        place = sum(every.index(h) < every.index(axis) for h in have)
        first = lax.axis_index(axis) == 0
        x = jnp.stack([jnp.where(first, x, other), jnp.where(first, other, x)], place)
        have.append(axis)
    return x


def after(x, *others):
    return lax.optimization_barrier((x, *others))[0]


def scatter_bits(x, order, every, sends=None):
    left = list(every)
    for axis in order:
        place = left.index(axis)
        mine = lax.axis_index(axis)
        keep = lax.dynamic_index_in_dim(x, mine, place, keepdims=False)
        send = lax.dynamic_index_in_dim(x, 1 - mine, place, keepdims=False)
        send = send.astype(bf16)
        if sends is not None:
            sends.append(send)
        other = lax.ppermute(send, axis, SWAP)
        left.pop(place)
        x = keep.astype(f32) + other.astype(f32)
        if left:
            x = x.astype(bf16)
    return x


def project_kernel(a_ref, b_ref, gain_ref, w_ref, cos_ref, sin_ref, low_ref, q_ref, k_ref, v_ref):
    step = pl.program_id(0)
    half = pl.num_programs(0) // 2

    def work(x_ref):
        x = x_ref[...].astype(f32)
        r = lax.rsqrt(jnp.mean(x * x, -1, keepdims=True) + epsilon)
        low = (x * r * gain_ref[...]).astype(bf16)
        low_ref[...] = low
        p = dot(low, w_ref[...], 1, 0)
        lane = lax.broadcasted_iota(jnp.int32, (x.shape[0], LANES), 1)
        u, w = p[:, :LANES], p[:, LANES : 2 * LANES]
        v = jnp.where(lane < HEAD_DIM, p[:, 2 * LANES :], 0.0)
        c, s = cos_ref[...], sin_ref[...]
        for at, turned in ((0, u * c - w * s), (LANES, w * c + u * s)):
            key = jnp.where(lane >= GROUP * HALF, turned, 0.0)
            key = pltpu.roll(key, HALF, 1) + pltpu.roll(key, 2 * HALF, 1) + pltpu.roll(key, 3 * HALF, 1)
            k_ref[:, at : at + LANES] = key.astype(bf16)
            for h in range(GROUP):
                q_ref[h, :, at : at + LANES] = jnp.where(lane // HALF == h, turned, 0.0).astype(bf16)
        zero = jnp.zeros(v.shape, bf16)
        first, second = v.astype(bf16), pltpu.roll(v, HEAD_DIM, 1).astype(bf16)
        for h in range(GROUP):
            for at in range(2):
                part = zero if h // 2 != at else (first if h % 2 == 0 else second)
                v_ref[h, :, at * LANES : (at + 1) * LANES] = part

    pl.when(step < half)(lambda: work(a_ref))
    pl.when(step >= half)(lambda: work(b_ref))


def project(part_a, part_b, gain, w_slab, cosine, sine):
    rows, width = part_a.shape
    length = 2 * rows
    steps = length // BLOCK
    half = steps // 2
    wide = 2 * LANES
    row = lambda cols: pl.BlockSpec((BLOCK, cols), lambda i: (i, 0))
    heads = pl.BlockSpec((GROUP, BLOCK, wide), lambda i: (0, i, 0))
    return pl.pallas_call(
        project_kernel,
        grid=(steps,),
        in_specs=[
            pl.BlockSpec((BLOCK, width), lambda i: (jnp.minimum(i, half - 1), 0)),
            pl.BlockSpec((BLOCK, width), lambda i: (jnp.maximum(i - half, 0), 0)),
            pl.BlockSpec((1, width), lambda i: (0, 0)),
            pl.BlockSpec((width, SLAB), lambda i: (0, 0)),
            row(LANES),
            row(LANES),
        ],
        out_specs=[row(width), heads, row(wide), heads],
        out_shape=[
            jax.ShapeDtypeStruct((length, width), bf16),
            jax.ShapeDtypeStruct((GROUP, length, wide), bf16),
            jax.ShapeDtypeStruct((length, wide), bf16),
            jax.ShapeDtypeStruct((GROUP, length, wide), bf16),
        ],
        compiler_params=pltpu.CompilerParams(vmem_limit_bytes=40 * 2**20),
        cost_estimate=pl.CostEstimate(
            flops=2 * length * width * SLAB, bytes_accessed=12 * 2**20, transcendentals=length
        ),
    )(part_a, part_b, gain, w_slab, cosine, sine)


def allowed_block(col_ref, row_ref, start, width):
    shape = (BLOCK, width)
    places = start + lax.broadcasted_iota(jnp.int32, shape, 0)
    keys = lax.broadcasted_iota(jnp.int32, shape, 1)
    same = col_ref[start : start + BLOCK, :] == row_ref[:, :width]
    return same & (keys <= places)


def attend_kernel(q_ref, k_ref, v_ref, col_ref, row_ref, o_ref, lse_ref):
    lane = lax.broadcasted_iota(jnp.int32, (BLOCK, LANES), 1)
    for start in range(0, k_ref.shape[0], BLOCK):
        width = start + BLOCK
        rows = slice(start, width)
        allowed = allowed_block(col_ref, row_ref, start, width)
        total = jnp.zeros((BLOCK, 2 * LANES), f32)
        logs = jnp.zeros((BLOCK, LANES), f32)
        for h in range(GROUP):
            s = dot(q_ref[h, rows, :], k_ref[:width, :], 1, 1) * 0.125
            s = jnp.where(allowed, s, masked)
            top = jnp.max(s, -1, keepdims=True)
            p = jnp.exp(s - top)
            below = jnp.sum(p, -1, keepdims=True)
            total = total + dot((p / below).astype(bf16), v_ref[h, :width, :], 1, 0)
            logs = jnp.where(lane == h, top + jnp.log(below), logs)
        o_ref[rows, :] = total.astype(bf16)
        lse_ref[rows, :] = logs


def attend(q, k, v, docs_col, docs_row):
    length, wide = k.shape
    return pl.pallas_call(
        attend_kernel,
        out_shape=[
            jax.ShapeDtypeStruct((length, wide), bf16),
            jax.ShapeDtypeStruct((length, LANES), f32),
        ],
        compiler_params=pltpu.CompilerParams(vmem_limit_bytes=48 * 2**20),
        cost_estimate=pl.CostEstimate(
            flops=2 * GROUP * length * length * wide,
            bytes_accessed=8 * 2**20,
            transcendentals=GROUP * length * length // 2,
        ),
    )(q, k, v, docs_col, docs_row)


def attend_back_kernel(
    q_ref, k_ref, v_ref, g_ref, lse_ref, col_ref, row_ref, cos_ref, sin_ref, out_ref, dk_ref, dv_ref
):
    length = k_ref.shape[0]
    wide = 2 * LANES
    dk_ref[...] = jnp.zeros_like(dk_ref)
    dv_ref[...] = jnp.zeros_like(dv_ref)
    lane = lax.broadcasted_iota(jnp.int32, (BLOCK, LANES), 1)
    wide_lane = lax.broadcasted_iota(jnp.int32, (BLOCK, wide), 1)
    for start in range(0, length, BLOCK):
        width = start + BLOCK
        rows = slice(start, width)
        allowed = allowed_block(col_ref, row_ref, start, width)
        dq = jnp.zeros((BLOCK, wide), f32)
        grads = g_ref[rows, :].astype(f32)
        for h in range(GROUP):
            q = q_ref[h, rows, :]
            lse = jnp.sum(jnp.where(lane == h, lse_ref[rows, :], 0.0), -1, keepdims=True)
            s = dot(q, k_ref[:width, :], 1, 1) * 0.125
            p = jnp.where(allowed, jnp.exp(jnp.where(allowed, s, masked) - lse), 0.0)
            g = jnp.where(wide_lane // HEAD_DIM == h, grads, 0.0).astype(bf16)
            dp = dot(g, v_ref[h, :width, :], 1, 1)
            delta = jnp.sum(p * dp, -1, keepdims=True)
            ds = (p * (dp - delta)).astype(bf16)
            part = dot(ds, k_ref[:width, :], 1, 0)
            dq = dq + jnp.where(wide_lane % LANES // HALF == h, part, 0.0)
            dk_ref[:width, :] += dot(ds, q, 0, 0)
            dv_ref[:width, :] += dot(p.astype(bf16), g, 0, 0)
        out_ref[rows, :LANES] = dq[:, :LANES].astype(out_ref.dtype)
        out_ref[rows, LANES:wide] = dq[:, LANES:].astype(out_ref.dtype)
    for start in range(0, length, BLOCK):
        rows = slice(start, start + BLOCK)
        halves = []
        for at in (0, LANES):
            key = dk_ref[rows, at : at + LANES]
            key = pltpu.roll(key, 3 * HALF, 1) + pltpu.roll(key, 2 * HALF, 1) + pltpu.roll(key, HALF, 1)
            both = jnp.where(lane >= GROUP * HALF, key, out_ref[rows, at : at + LANES])
            halves.append(both * 0.125)
        c, s = cos_ref[rows, :], sin_ref[rows, :]
        u, w = halves
        out_ref[rows, :LANES] = u * c + w * s
        out_ref[rows, LANES:wide] = w * c - u * s
        v = dv_ref[rows, :LANES] + dv_ref[rows, LANES:]
        v = v + pltpu.roll(v, HEAD_DIM, 1)
        out_ref[rows, wide:] = jnp.where(lane < HEAD_DIM, v, 0.0)


def attend_back_entry(*refs):
    *ins, out_ref, full_ref, dk_ref, dv_ref = refs
    attend_back_kernel(*ins, full_ref, dk_ref, dv_ref)
    out_ref[...] = full_ref[...].astype(bf16)


def attend_back(q, k, v, g, lse, docs_col, docs_row, cosine, sine):
    length, wide = k.shape
    return pl.pallas_call(
        attend_back_entry,
        out_shape=jax.ShapeDtypeStruct((length, SLAB), bf16),
        scratch_shapes=[
            pltpu.VMEM((length, SLAB), f32),
            pltpu.VMEM((length, wide), f32),
            pltpu.VMEM((length, wide), f32),
        ],
        compiler_params=pltpu.CompilerParams(vmem_limit_bytes=52 * 2**20),
        cost_estimate=pl.CostEstimate(
            flops=5 * GROUP * length * length * wide,
            bytes_accessed=8 * 2**20,
            transcendentals=GROUP * length * length // 2,
        ),
    )(q, k, v, g, lse, docs_col, docs_row, cosine, sine)


def pack(gate_up, down):
    blocks = [down[:, c : c + EXP_FF] for c in range(0, down.shape[1], EXP_FF)]
    return jnp.concatenate([gate_up, jnp.concatenate(blocks, 0)], 1)


def unpack_down(packed, high):
    rows = packed.shape[0] // high
    return jnp.concatenate([packed[c * rows : (c + 1) * rows, 2 * EXP_FF :] for c in range(high)], 1)


def half_places(at_ref, half, size):
    high = at_ref[2]
    place = high if half == 0 else 1 - high
    return pl.multiple_of(place * size, LANES)


def plain_kernel(at_ref, g_ref, pa, pb, pc, pd, out_ref):
    rows = g_ref.shape[0] * g_ref.shape[2]
    part = EXP_FF // 2
    width = g_ref.shape[3]
    g = g_ref[:, 0].reshape(rows, width)
    for j, packed in enumerate(((pa, pb), (pc, pd))):
        for half, p in enumerate(packed):
            plain = None
            for c in range(width // EXP_FF):
                cols = slice(c * EXP_FF, (c + 1) * EXP_FF)
                term = dot(g[:, cols], p[c * part : (c + 1) * part, :], 1, 1)
                plain = term if plain is None else plain + term
            at = pl.multiple_of(j * EXP_FF + half_places(at_ref, half, part), LANES)
            out_ref[:, 0, :, pl.ds(at, part)] = plain.reshape(g_ref.shape[0], g_ref.shape[2], part)


def plain_grads(places, grads, packed):
    holders, batches, local, width = grads.shape
    size = packed[0].shape[0]
    near = BLOCK // local
    block = lambda cols: pl.BlockSpec((near, 1, local, cols), lambda i, m, _: (i, m, 0, 0))
    return pl.pallas_call(
        plain_kernel,
        grid_spec=pltpu.PrefetchScalarGridSpec(
            num_scalar_prefetch=1,
            grid=(holders // near, batches),
            in_specs=[
                block(width),
                *[pl.BlockSpec((size, EXP_FF), lambda i, m, _: (0, 2))] * 4,
            ],
            out_specs=block(2 * EXP_FF),
        ),
        out_shape=jax.ShapeDtypeStruct((holders, batches, local, 2 * EXP_FF), f32),
        compiler_params=pltpu.CompilerParams(vmem_limit_bytes=40 * 2**20),
        cost_estimate=pl.CostEstimate(
            flops=4 * holders * batches * local * width * EXP_FF,
            bytes_accessed=14 * 2**20,
            transcendentals=0,
        ),
    )(places, grads, *packed)


def expert_kernel(at_ref, x_ref, g_ref, pa, pb, pc, pd, sum_ref, hid_ref, pair_ref):
    rows = x_ref.shape[0]
    size, width = pa.shape[0], 2 * pa.shape[0]
    double = 2 * EXP_FF
    me, experts = at_ref[0], at_ref[1]
    extra = x_ref[:, width:].astype(f32)
    both_plain = g_ref[:, 0].reshape(rows, double)
    lane = lax.broadcasted_iota(jnp.int32, extra.shape, 1)
    back = jnp.zeros(extra.shape, f32)
    totals = [None, None]
    for j, packed in enumerate(((pa, pb), (pc, pd))):
        expert = me if j == 0 else me ^ 4
        high = lane == expert
        low = lane == expert + experts
        share = jnp.sum(jnp.where(high | low, extra, 0.0), -1, keepdims=True)
        gate_up = None
        for half, p in enumerate(packed):
            term = dot(x_ref[:, pl.ds(half_places(at_ref, half, size), size)], p[...], 1, 0)
            gate_up = term if gate_up is None else gate_up + term
        gate, up = gate_up[:, :EXP_FF], gate_up[:, EXP_FF:]
        sg = 1.0 / (1.0 + jnp.exp(-gate))
        grown = gate * sg
        hidden = (grown * up).astype(bf16).astype(f32)
        grad_plain = both_plain[:, j * EXP_FF : (j + 1) * EXP_FF]
        gate_grad = jnp.sum(grad_plain * hidden, -1, keepdims=True)
        gate_high = gate_grad.astype(bf16).astype(f32)
        back = jnp.where(high, gate_high, jnp.where(low, gate_grad - gate_high, back))
        grad_hidden = share * grad_plain
        at = j * EXP_FF
        hid_ref[:, at : at + EXP_FF] = (share * hidden).astype(bf16)
        at = j * double
        first = (grad_hidden * up * sg * (1.0 + gate * (1.0 - sg))).astype(bf16)
        pair_ref[:, at : at + EXP_FF] = first
        pair_ref[:, at + EXP_FF : at + double] = (grad_hidden * grown).astype(bf16)
        for half, p in enumerate(packed):
            term = dot(pair_ref[:, at : at + double], p[...], 1, 1)
            totals[half] = term if totals[half] is None else totals[half] + term
    for half in range(2):
        sum_ref[:, pl.ds(half_places(at_ref, half, size), size)] = totals[half].astype(bf16)
    sum_ref[:, width:] = back.astype(bf16)


def run_experts(places, x, plain, m, packed):
    rows, wide = x.shape
    local = plain.shape[2]
    size, width = packed[0].shape
    block = lambda cols: pl.BlockSpec((BLOCK, cols), lambda i, _: (i, 0))
    whole = pl.BlockSpec((size, 2 * EXP_FF), lambda i, _: (0, 0))
    return pl.pallas_call(
        expert_kernel,
        grid_spec=pltpu.PrefetchScalarGridSpec(
            num_scalar_prefetch=1,
            grid=(rows // BLOCK,),
            in_specs=[
                block(wide),
                pl.BlockSpec((BLOCK // local, 1, local, 2 * EXP_FF), lambda i, _: (i, m, 0, 0)),
                *[whole] * 4,
            ],
            out_specs=[block(wide), block(2 * EXP_FF), block(4 * EXP_FF)],
        ),
        out_shape=[
            jax.ShapeDtypeStruct((rows, wide), bf16),
            jax.ShapeDtypeStruct((rows, 2 * EXP_FF), bf16),
            jax.ShapeDtypeStruct((rows, 4 * EXP_FF), bf16),
        ],
        compiler_params=pltpu.CompilerParams(vmem_limit_bytes=56 * 2**20),
        cost_estimate=pl.CostEstimate(
            flops=16 * rows * width * EXP_FF, bytes_accessed=16 * 2**20, transcendentals=rows * 2 * EXP_FF
        ),
    )(places, x, plain, *packed)


def mixture_kernel(at_ref, a_ref, b_ref, pa, pb, pc, pd, out_ref):
    size, width = pa.shape
    part = EXP_FF // 2

    def work(hid_ref):
        for c in range(width // EXP_FF):
            total = None
            for j, packed in enumerate(((pa, pb), (pc, pd))):
                for half, p in enumerate(packed):
                    at = pl.multiple_of(j * EXP_FF + half_places(at_ref, half, part), LANES)
                    term = dot(
                        hid_ref[:, pl.ds(at, part)],
                        p[c * part : (c + 1) * part, 2 * EXP_FF :],
                        1,
                        0,
                    )
                    total = term if total is None else total + term
            cols = slice(c * EXP_FF, (c + 1) * EXP_FF)
            shape = out_ref.shape[0], out_ref.shape[2], EXP_FF
            out_ref[:, 0, :, cols] = total.astype(bf16).reshape(shape)

    pl.when(pl.program_id(0) == 0)(lambda: work(a_ref))
    pl.when(pl.program_id(0) == 1)(lambda: work(b_ref))


def mix_experts(places, weighted, local, packed):
    rows = weighted[0].shape[0]
    size, width = packed[0].shape
    blocks = rows // BLOCK
    whole = pl.BlockSpec((size, width), lambda m, i, _: (0, 0))
    first = pl.BlockSpec((BLOCK, 2 * EXP_FF), lambda m, i, _: (jnp.where(m == 0, i, blocks - 1), 0))
    second = pl.BlockSpec((BLOCK, 2 * EXP_FF), lambda m, i, _: (jnp.where(m == 1, i, 0), 0))
    return pl.pallas_call(
        mixture_kernel,
        grid_spec=pltpu.PrefetchScalarGridSpec(
            num_scalar_prefetch=1,
            grid=(2, blocks),
            in_specs=[first, second, *[whole] * 4],
            out_specs=pl.BlockSpec(
                (BLOCK // local, 1, local, width), lambda m, i, _: (i, m, 0, 0)
            ),
        ),
        out_shape=jax.ShapeDtypeStruct((rows // local, 2, local, width), bf16),
        compiler_params=pltpu.CompilerParams(vmem_limit_bytes=48 * 2**20),
        cost_estimate=pl.CostEstimate(
            flops=8 * rows * width * EXP_FF, bytes_accessed=16 * 2**20, transcendentals=0
        ),
    )(places, *weighted, *packed)


def weights_kernel(at_ref, xa_ref, xb_ref, g_ref, ha_ref, hb_ref, pa_ref, pb_ref, send_ref, keep_ref):
    rows = pa_ref.shape[0]
    size, width = keep_ref.shape
    part = EXP_FF // 2
    double = 2 * EXP_FF

    def work(out_ref):
        total = dot(xa_ref[...], pa_ref[...], 1, 0) + dot(xb_ref[...], pb_ref[...], 1, 0)
        out_ref[:, :double] = total.astype(out_ref.dtype)
        for c in range(width // EXP_FF):
            at = slice(c * EXP_FF, (c + 1) * EXP_FF)
            total = dot(ha_ref[...], g_ref[:, 0, :, at].reshape(rows, EXP_FF), 1, 0)
            total = total + dot(hb_ref[...], g_ref[:, 1, :, at].reshape(rows, EXP_FF), 1, 0)
            out_ref[c * part : (c + 1) * part, double:] = total.astype(out_ref.dtype)

    pl.when(pl.program_id(0) == 0)(lambda: work(send_ref))
    pl.when(pl.program_id(0) == 1)(lambda: work(keep_ref))


def expert_weights(j, places, xs, grads, weighted, pairs):
    rows = xs[0].shape[1]
    width = grads.shape[3]
    size = width // 2
    pick = lambda h, at: jnp.where(h == 0, 1 - at[2], at[2])
    x_spec = pl.BlockSpec((size, rows), lambda h, at: (pick(h, at), 0))
    hidden = pl.BlockSpec((EXP_FF // 2, rows), lambda h, at: (2 * j + pick(h, at), 0))
    pair = pl.BlockSpec((rows, 2 * EXP_FF), lambda h, _: (0, j))
    half = pl.BlockSpec((size, width), lambda h, _: (0, 0))
    return pl.pallas_call(
        weights_kernel,
        grid_spec=pltpu.PrefetchScalarGridSpec(
            num_scalar_prefetch=1,
            grid=(2,),
            in_specs=[
                x_spec,
                x_spec,
                pl.BlockSpec(grads.shape, lambda h, _: (0, 0, 0, 0)),
                hidden,
                hidden,
                pair,
                pair,
            ],
            out_specs=[half, half],
        ),
        out_shape=[
            jax.ShapeDtypeStruct((size, width), bf16),
            jax.ShapeDtypeStruct((size, width), f32 if j == 0 else bf16),
        ],
        compiler_params=pltpu.CompilerParams(vmem_limit_bytes=60 * 2**20),
        cost_estimate=pl.CostEstimate(
            flops=12 * rows * width * EXP_FF, bytes_accessed=16 * 2**20, transcendentals=0
        ),
    )(places, *xs, grads, *weighted, *pairs)


def heads_to_rows(a, b):
    lane = lax.broadcasted_iota(jnp.int32, (a.shape[0], LANES), 1)
    low = lane < HEAD_DIM
    b_first, b_second = (pltpu.roll(t, HEAD_DIM, 1) for t in (b[:, :LANES], b[:, LANES:]))
    return (a[:, :LANES], jnp.where(low, a[:, LANES:], b_first), jnp.where(low, b_first, b_second))


def rows_to_heads(first, second, third):
    lane = lax.broadcasted_iota(jnp.int32, first.shape, 1)
    low = lane < HEAD_DIM
    second_turned, third_turned = (pltpu.roll(t, HEAD_DIM, 1) for t in (second, third))
    a = (first, jnp.where(low, second, 0.0))
    b = (jnp.where(low, second_turned, third_turned), jnp.where(low, third_turned, 0.0))
    return a, b


def middle_kernel(
    experts, heads_ref, x_ref, w_ref, gain_ref, router_ref, routes_ref,
    y_ref, sent_ref, low_ref, probs_ref, gates_ref, chosen_ref, pick_ref, scale_ref,
):
    batches, local, width = x_ref.shape
    for m in range(batches):
        for k in range(0, KV_HEADS, 2):
            a, b = (heads_ref[m * KV_HEADS + k + i].astype(f32) for i in range(2))
            at = k * GROUP * HEAD_DIM
            for i, part in enumerate(heads_to_rows(a, b)):
                cols = slice(at + i * LANES, at + (i + 1) * LANES)
                low_ref[m * local : (m + 1) * local, cols] = part.astype(bf16)
    rows = batches * local
    y = x_ref[...].reshape(rows, width).astype(f32) + dot(low_ref[...], w_ref[...], 1, 1)
    y_ref[...] = y
    r = lax.rsqrt(jnp.mean(y * y, -1, keepdims=True) + epsilon)
    second = (y * r * gain_ref[...]).astype(bf16)
    lane = lax.broadcasted_iota(jnp.int32, (rows, LANES), 1)
    logits = jnp.where(lane < experts, dot(second, router_ref[...], 1, 0), masked)
    raised = jnp.exp(logits - jnp.max(logits, -1, keepdims=True))
    probs = raised / jnp.sum(raised, -1, keepdims=True)
    chosen = jnp.zeros((rows, LANES), f32)
    for k in range(TOP):
        chosen = jnp.where(routes_ref[:, k : k + 1] == lane, 1.0, chosen)
    picked = jnp.sum(chosen * probs, -1, keepdims=True)
    gates = chosen * probs / picked
    high = gates.astype(bf16).astype(f32)
    extra = high + pltpu.roll(gates - high, experts, 1)
    sent_ref[:, :, :width] = second.reshape(batches, local, width)
    sent_ref[:, :, width:] = extra.astype(bf16).reshape(batches, local, LANES)
    probs_ref[...] = probs
    gates_ref[...] = gates
    chosen_ref[...] = chosen
    pick_ref[...] = picked
    scale_ref[...] = r


def middle_rows(experts, heads, tokens, out_full, gain, router, routes):
    batches, local, width = tokens.shape
    rows = batches * local
    small = jax.ShapeDtypeStruct((rows, LANES), f32)
    column = jax.ShapeDtypeStruct((rows, 1), f32)
    return pl.pallas_call(
        lambda *refs: middle_kernel(experts, *refs),
        out_shape=[
            jax.ShapeDtypeStruct((rows, width), f32),
            jax.ShapeDtypeStruct((batches, local, width + LANES), bf16),
            jax.ShapeDtypeStruct((rows, width), bf16),
            small,
            small,
            small,
            column,
            column,
        ],
        compiler_params=pltpu.CompilerParams(vmem_limit_bytes=40 * 2**20),
        cost_estimate=pl.CostEstimate(
            flops=2 * rows * width * width, bytes_accessed=8 * 2**20, transcendentals=rows * LANES
        ),
    )(heads, tokens, out_full, gain, router, routes)


def middle_back_kernel(
    experts, came_a_ref, came_b_ref, g_ref, y_ref, probs_ref, gates_ref, chosen_ref,
    pick_ref, scale_ref, gain_ref, router_ref, w_ref,
    heads_ref, grad_ref, branch_ref, logits_ref, gain_grad_ref,
):
    batches, local, width = g_ref.shape
    rows = batches * local
    came = jnp.concatenate([came_a_ref[...], came_b_ref[...]], 0)
    extra = came[:, width:]
    lane = lax.broadcasted_iota(jnp.int32, (rows, LANES), 1)
    chosen, probs, gates = chosen_ref[...], probs_ref[...], gates_ref[...]
    both = extra + pltpu.roll(extra, LANES - experts, 1)
    grad_gates = jnp.where(lane < experts, both, 0.0) * chosen
    mean = jnp.sum(grad_gates * gates, -1, keepdims=True)
    grad_picked = chosen * (grad_gates - mean) / pick_ref[...]
    grad_logits = probs * (grad_picked - jnp.sum(probs * grad_picked, -1, keepdims=True))
    grad_logits = grad_logits.astype(bf16)
    logits_ref[...] = grad_logits
    grad_second = came[:, :width] + dot(grad_logits, router_ref[...], 1, 1)
    r = scale_ref[...]
    n = y_ref[...] * r
    gain_grad_ref[...] = jnp.sum(grad_second * n, 0, keepdims=True)
    c = grad_second * gain_ref[...]
    grad_y = g_ref[...].reshape(rows, width).astype(f32)
    grad_y = grad_y + r * (c - n * jnp.mean(c * n, -1, keepdims=True))
    grad_ref[...] = grad_y
    branch = grad_y.astype(bf16)
    branch_ref[...] = branch
    grad = dot(branch, w_ref[...], 1, 0)
    for k in range(0, KV_HEADS, 2):
        at = k * GROUP * HEAD_DIM
        parts = (grad[:, at + i * LANES : at + (i + 1) * LANES] for i in range(3))
        for j, head in enumerate(rows_to_heads(*parts)):
            for i, part in enumerate(head):
                part = part.astype(bf16).reshape(batches, local, LANES)
                for m in range(batches):
                    cols = slice(i * LANES, (i + 1) * LANES)
                    heads_ref[m * KV_HEADS + k + j, :, cols] = part[m]


def middle_back(experts, came, cotangent, kept, gain, router, out_full):
    batches, local, width = cotangent.shape
    rows = batches * local
    return pl.pallas_call(
        lambda *refs: middle_back_kernel(experts, *refs),
        out_shape=[
            jax.ShapeDtypeStruct((batches * KV_HEADS, local, 2 * LANES), bf16),
            jax.ShapeDtypeStruct((rows, width), f32),
            jax.ShapeDtypeStruct((rows, width), bf16),
            jax.ShapeDtypeStruct((rows, LANES), bf16),
            jax.ShapeDtypeStruct((1, width), f32),
        ],
        compiler_params=pltpu.CompilerParams(vmem_limit_bytes=40 * 2**20),
        cost_estimate=pl.CostEstimate(
            flops=2 * rows * width * width, bytes_accessed=10 * 2**20, transcendentals=0
        ),
    )(*came, cotangent, *kept, gain, router, out_full)


def finish_kernel(slab_ref, w_ref, gain_ref, grad_ref, gain_grad_ref):
    rows = w_ref.shape[0]
    lane = lax.broadcasted_iota(jnp.int32, (rows, LANES), 1)
    per_tile = LANES // HALF

    def tile(pieces):
        out = None
        for i, (source, group) in enumerate(pieces):
            shift = (i - group) % per_tile * HALF
            moved = pltpu.roll(source, shift, 1) if shift else source
            out = moved if out is None else jnp.where(lane // HALF == i, moved, out)
        return out

    batches = slab_ref.shape[0] // KV_HEADS
    total = jnp.zeros((rows, 1), f32)

    def put(at, value):
        grad_ref[:, at : at + LANES] = value
        return jnp.sum(value * w_ref[:, at : at + LANES].astype(f32), -1, keepdims=True)

    for k in range(0, KV_HEADS, 2):
        sums = []
        for i in range(2):
            terms = [slab_ref[m * KV_HEADS + k + i].astype(f32) for m in range(batches)]
            sums.append(sum(terms[1:], terms[0]))
        u, w, v = zip(*((t[:, :LANES], t[:, LANES : 2 * LANES], t[:, 2 * LANES :]) for t in sums))
        halves_of = [(part, group) for i in range(2) for group in range(GROUP) for part in (u[i], w[i])]
        for i in range(0, len(halves_of), per_tile):
            at = k * GROUP * HEAD_DIM + i * HALF
            total = total + put(at, tile(halves_of[i : i + per_tile]))
        at = HEADS * HEAD_DIM + k * HEAD_DIM
        total = total + put(at, tile([(part, GROUP) for i in range(2) for part in (u[i], w[i])]))
        at = (HEADS + KV_HEADS) * HEAD_DIM + k * HEAD_DIM
        total = total + put(at, jnp.where(lane < HEAD_DIM, v[0], pltpu.roll(v[1], HEAD_DIM, 1)))
    gain_grad_ref[...] = total / gain_ref[...].astype(f32)


def finish(slab, w_qkv, gain):
    return pl.pallas_call(
        finish_kernel,
        out_shape=[
            jax.ShapeDtypeStruct(w_qkv.shape, f32),
            jax.ShapeDtypeStruct(gain.shape, f32),
        ],
        compiler_params=pltpu.CompilerParams(vmem_limit_bytes=32 * 2**20),
    )(slab, w_qkv, gain)


def split_columns(w_qkv):
    rows = w_qkv.shape[0]
    q_width, k_width = HEADS * HEAD_DIM, KV_HEADS * HEAD_DIM
    q = w_qkv[:, :q_width].reshape(rows, KV_HEADS, GROUP, 2, HALF)
    k = w_qkv[:, q_width : q_width + k_width].reshape(rows, KV_HEADS, 1, 2, HALF)
    both = jnp.concatenate([q, k], 2)
    return (
        both[:, :, :, 0].reshape(rows, KV_HEADS, LANES),
        both[:, :, :, 1].reshape(rows, KV_HEADS, LANES),
        w_qkv[:, q_width + k_width :].reshape(rows, KV_HEADS, HEAD_DIM),
    )


def halves(x):
    high = lax.reduce_precision(x, 8, 7)
    return high.astype(bf16), (x - high).astype(bf16)


def gather_sequence(tokens, ex_axes, mb_axis):
    mine = lax.axis_index(mb_axis)
    own = lax.dynamic_index_in_dim(tokens, mine, 0, keepdims=False)
    other = lax.ppermute(
        lax.dynamic_index_in_dim(tokens, 1 - mine, 0, keepdims=False), mb_axis, SWAP
    )
    first = mine == 0
    group = jnp.stack([jnp.where(first, own, other), jnp.where(first, other, own)], 0)
    middle = tuple(a for a in ex_axes[:-2] if a != mb_axis)
    return gather_bits(group, middle, middle), middle, other


def on_device(
    dp_axes,
    ex_axes,
    tokens,
    cotangent,
    segments,
    positions,
    routes,
    w_qkv,
    w_out,
    w_router,
    norm_attn,
    norm_ffn,
    w_gate_up,
    w_down,
):
    batches, local, width = tokens.shape
    experts = w_router.shape[1]
    count = 2 ** len(ex_axes)
    length = count * local
    units = batches * KV_HEADS
    parts = count // units
    shard = w_qkv.shape[0]
    rows = batches * local
    me = lax.axis_index(ex_axes)
    bit = lambda b: ex_axes[len(ex_axes) - 1 - b]
    pair_axis = bit(2)
    far = tuple(a for a in ex_axes[:-2] if a != pair_axis)
    token_axes = ex_axes[-2:] + far
    orders = (far + (bit(0), bit(1)), far + (bit(1), bit(0)))

    mb_axis = bit(3)

    u_cols, w_cols, v_cols = split_columns(w_qkv)
    small = jnp.concatenate([norm_attn[:, None], norm_ffn[:, None], w_router], 1)
    small = jnp.pad(small, ((0, 0), (0, SLAB - 2 * LANES - HEAD_DIM - small.shape[1])))
    small = jnp.broadcast_to(small[:, None, :], (shard, KV_HEADS, small.shape[1]))
    slab = jnp.transpose(jnp.concatenate([u_cols, w_cols, v_cols, small], -1), (1, 0, 2))
    meta = jnp.stack([segments, positions // 64, positions % 64], 1).astype(bf16)
    meta = jnp.pad(meta, ((0, 0), (0, META_ROWS - 3), (0, SLAB - local)))
    payload = jnp.concatenate(
        [
            jnp.broadcast_to(slab[None], (batches,) + slab.shape),
            jnp.broadcast_to(meta[:, None], (batches, KV_HEADS) + meta.shape[1:]),
        ],
        2,
    ).reshape(units, shard + META_ROWS, SLAB)
    payload = jnp.concatenate([payload] * parts, 0)
    group, middle, swapped = gather_sequence(tokens, ex_axes, mb_axis)
    arrived = lax.all_to_all(after(payload, swapped), ex_axes, 0, 0, tiled=True)
    w_slab = gather_bits(arrived[:, :shard].reshape(count * shard, SLAB), dp_axes, dp_axes)
    w_slab = w_slab.reshape(width, SLAB)
    extra_at = 2 * LANES + HEAD_DIM
    gain_attn = w_slab[:, extra_at].astype(f32)
    gain_ffn = w_slab[:, extra_at + 1].astype(f32)
    router_full = w_slab[:, extra_at + 2 : extra_at + 2 + experts]
    info = arrived[:, shard : shard + 3, :local].astype(jnp.int32)
    docs = info[:, 0].reshape(length)
    places = (info[:, 1] * 64 + info[:, 2]).reshape(length)
    frequency = rope_base ** (-jnp.arange(HALF, dtype=f32) / HALF)
    angles = places.astype(f32)[:, None] * jnp.tile(frequency, GROUP + 1)[None, :]
    cosine, sine = jnp.cos(angles), jnp.sin(angles)
    docs_col, docs_row = docs[:, None], docs[None, :]

    high_axis, low_axes = dp_axes[0], dp_axes[1:]
    blocks = width // EXP_FF
    expert_own = pack(w_gate_up[0], w_down[0])
    if low_axes:
        parted = gather_bits(expert_own, low_axes, low_axes)
        parted = parted.reshape((-1,) + expert_own.shape)
        lower = parted[..., 2 * EXP_FF :].reshape(parted.shape[0], blocks, -1, EXP_FF)
        expert_own = jnp.concatenate(
            [
                parted[..., : 2 * EXP_FF].reshape(-1, 2 * EXP_FF),
                lower.transpose(1, 0, 2, 3).reshape(-1, EXP_FF),
            ],
            1,
        )
    group, expert_own = lax.optimization_barrier((group, expert_own))
    group = jnp.moveaxis(group, len(middle), 0)
    sides = []
    for part, last in ((group[0], (bit(0), bit(1))), (group[1], (bit(1), bit(0)))):
        pair = gather_bits(part, last, (bit(1), bit(0)), {1: arrived})
        sides.append(jnp.moveaxis(pair, (0, 1), (len(middle), len(middle) + 1)))
    if len(middle) == 1:
        sides = [s.reshape(length // 2, width) for s in sides]
    else:
        at = ex_axes.index(mb_axis)
        whole = jnp.stack(sides, at).reshape(length, width)
        sides = [whole[: length // 2], whole[length // 2 :]]

    out_full = lax.all_gather(w_out, dp_axes + ex_axes, axis=0, tiled=True)
    grad_rows = gather_bits(after(cotangent, group), far, far)
    grad_rows = lax.all_gather(grad_rows, ex_axes[-2:], axis=0)
    grad_rows = grad_rows.reshape((-1,) + cotangent.shape)
    qkv_mixed = jnp.concatenate([p.reshape(shard, -1) for p in (u_cols, w_cols, v_cols)], 1)
    qkv_full = lax.all_gather(qkv_mixed, dp_axes + ex_axes, axis=0, tiled=True)

    cut = expert_own.shape[0] // 2
    other_parts = [lax.ppermute(t, pair_axis, SWAP) for t in (expert_own[:cut], expert_own[cut:])]

    first_low, q, k, v = project(*sides, gain_attn[None, :], w_slab, cosine, sine)
    q = after(q, other_parts[0])
    attended, lse = attend(q, k, v, docs_col, docs_row)
    back = lax.all_to_all(attended.reshape(count, local, 2 * LANES), ex_axes, 0, 0, tiled=True)
    expert_other = jnp.concatenate([after(t, attended) for t in other_parts], 0)
    packed = [
        expert_own,
        lax.ppermute(expert_own, high_axis, SWAP),
        expert_other,
        lax.ppermute(expert_other, high_axis, SWAP),
    ]
    x = tokens.reshape(rows, width).astype(f32)
    router_full = jnp.pad(router_full, ((0, 0), (0, LANES - experts)))
    y_one, sent, attended_low, *kept = middle_rows(
        experts, back[:units], tokens, out_full, gain_ffn[None, :], router_full, routes.reshape(rows, TOP)
    )
    second_low = sent[:, :, :width].reshape(rows, width)
    sent = after(sent, other_parts[1])

    places_at = jnp.stack([me, jnp.int32(experts), lax.axis_index(high_axis)]).astype(jnp.int32)
    weighted, pairs, stages = [], [], []
    gathered = []
    ahead = sent
    for m in range(batches):
        far_part = gather_bits(after(sent[m], ahead), far, far)
        ahead = far_part
        if m == 0:
            grads = after(grad_rows, far_part)
            plain = plain_grads(places_at, grads, packed)
        last = orders[m % 2][len(far) :]
        part = gather_bits(far_part, last, (bit(1), bit(0)), {1: plain} if m else {})
        gathered.append(part.reshape(-1, width + LANES))
    for m in range(batches):
        back_rows, hid, pair = run_experts(places_at, gathered[m], plain, m, packed)
        back_rows = back_rows.reshape((2,) * len(token_axes) + (local, width + LANES))
        stages.append(scatter_bits(back_rows, orders[m % 2][-1:], token_axes))
        weighted.append(hid)
        pairs.append(pair)
    grad_inputs = []
    for m in range(batches):
        order = orders[m % 2][::-1]
        left = tuple(a for a in token_axes if a != order[0])
        grad_inputs.append(scatter_bits(stages[m], order[1:], left))

    turned = [lax.optimization_barrier(t.T) for t in gathered]
    weighted_turned = [lax.optimization_barrier(t.T) for t in weighted]

    def expert_grads(j, *others):
        send, keep = expert_weights(
            j, places_at, turned, grad_rows, [after(t, *others) for t in weighted_turned], pairs
        )
        grad = keep.astype(f32) + lax.ppermute(send, high_axis, SWAP).astype(f32)
        if low_axes:
            count_low = 2 ** len(low_axes)
            parted = grad[:, : 2 * EXP_FF].reshape(count_low, -1, 2 * EXP_FF)
            lower = grad[:, 2 * EXP_FF :].reshape(blocks, count_low, -1, EXP_FF)
            lower = lower.transpose(1, 0, 2, 3).reshape(count_low, -1, EXP_FF)
            parted = jnp.concatenate([parted, lower], -1)
            parted = parted.reshape((2,) * len(low_axes) + parted.shape[1:])
            grad = scatter_bits(parted.astype(bf16), low_axes, low_axes)
        return grad

    grad_theirs = expert_grads(1, *stages).astype(bf16)
    cut = grad_theirs.shape[0] // 2
    grad_received = [
        lax.ppermute(t, pair_axis, SWAP) for t in (grad_theirs[:cut], grad_theirs[cut:])
    ]
    grad_inputs[-1] = after(grad_inputs[-1], grad_theirs)

    payload, grad_y, grad_branch, grad_logits, grad_gain_ffn = middle_back(
        experts, grad_inputs, cotangent, [y_one, *kept], gain_ffn[None, :], router_full, out_full
    )
    payload = jnp.concatenate([payload] * parts, 0)
    grad_heads = lax.all_to_all(payload, ex_axes, 0, 0, tiled=True).reshape(length, 2 * LANES)

    mixture = mix_experts(places_at, [after(t, payload) for t in weighted], local, packed)
    mixtures = lax.psum_scatter(
        after(mixture.reshape(-1, width), qkv_full), token_axes, scatter_dimension=0, tiled=True
    )
    grad_branch = after(grad_branch, payload)
    grad_out = dot(grad_branch, attended_low, 0, 0)
    extras = dot(after(second_low, payload), grad_logits, 0, 0)
    extras = jnp.where(jnp.arange(LANES) == experts, grad_gain_ffn.reshape(width, 1), extras)
    dense = jnp.concatenate([grad_out, extras], 1).astype(bf16)
    dense = scatter_bits(
        dense.reshape((2,) * len(dp_axes) + (-1, dense.shape[1])), dp_axes, dp_axes
    )
    dense = dense.astype(bf16).reshape((2,) * len(ex_axes) + (shard, -1))
    grad_heads = after(grad_heads, dense, mixture, grad_received[0])
    dense_one = scatter_bits(dense, ex_axes[-1:], ex_axes)
    dense_two = scatter_bits(dense_one, ex_axes[-2:-1], ex_axes[:-1])
    dense = scatter_bits(dense_two, ex_axes[:-2][::-1], ex_axes[:-2])

    grad_proj = attend_back(q, k, v, grad_heads, lse, docs_col, docs_row, cosine, sine)
    back = lax.all_to_all(grad_proj.reshape(count, local, SLAB), ex_axes, 0, 0, tiled=True)
    back = back[:units].reshape(batches, KV_HEADS, local, SLAB).transpose(0, 2, 1, 3)
    back = jnp.concatenate(
        [
            back[..., :LANES].reshape(rows, -1),
            back[..., LANES : 2 * LANES].reshape(rows, -1),
            back[..., 2 * LANES : 2 * LANES + HEAD_DIM].reshape(rows, -1),
        ],
        1,
    )
    grad_first = dot(after(back, dense_two), qkv_full, 1, 1)
    grad_slab = dot(first_low, grad_proj, 0, 0)
    grad_slab = scatter_bits(
        grad_slab.reshape((2,) * len(dp_axes) + (-1, SLAB)), dp_axes, dp_axes
    )
    grad_slab = lax.all_to_all(
        after(grad_slab.astype(bf16), dense_one, grad_received[1]).reshape(count, shard, SLAB), ex_axes, 0, 0, tiled=True
    )
    grad_qkv, grad_gain_attn = finish(grad_slab[:units], w_qkv, norm_attn[:, None])
    grad_gain_attn = grad_gain_attn[:, 0]
    grad_packed = expert_grads(0, grad_proj) + jnp.concatenate(grad_received, 0).astype(f32)
    grad_gate_up = grad_packed[:, : 2 * EXP_FF]
    grad_down = unpack_down(grad_packed, blocks)
    mixed = y_one + after(mixtures, grad_slab).astype(f32)
    r_one = lax.rsqrt(jnp.mean(x * x, -1, keepdims=True) + epsilon)
    n_one = x * r_one
    c_one = grad_first * gain_attn
    grad_tokens = grad_y + r_one * (c_one - n_one * jnp.mean(c_one * n_one, -1, keepdims=True))

    out_width = HEADS * HEAD_DIM
    return (
        mixed.astype(bf16).reshape(tokens.shape),
        grad_tokens.reshape(tokens.shape),
        grad_qkv,
        dense[:, :out_width],
        dense[:, out_width : out_width + experts],
        grad_gain_attn,
        dense[:, out_width + experts],
        grad_gate_up[None],
        grad_down[None],
    )


def solution(mesh):
    dp_bits = int(math.log2(mesh.shape["dp"]))
    ex_bits = int(math.log2(mesh.shape["expert"]))
    dp_axes = tuple(f"d{b}" for b in reversed(range(dp_bits)))
    ex_axes = tuple(f"e{b}" for b in reversed(range(ex_bits)))
    cube = Mesh(mesh.devices.reshape((2,) * (dp_bits + ex_bits)), dp_axes + ex_axes)
    every = dp_axes + ex_axes
    by_tokens = P(None, every, None)

    def run(*arrays):
        return on_device(dp_axes, ex_axes, *arrays)

    return jax.shard_map(
        run,
        mesh=cube,
        in_specs=(
            by_tokens,
            by_tokens,
            P(None, every),
            P(None, every),
            by_tokens,
            P(every, None),
            P(every, None),
            P(every, None),
            P(every),
            P(every),
            P(ex_axes, dp_axes, None),
            P(ex_axes, dp_axes, None),
        ),
        out_specs=(
            by_tokens,
            by_tokens,
            P(every, None),
            P(every, None),
            P(every, None),
            P(every),
            P(every),
            P(ex_axes, dp_axes, None),
            P(ex_axes, dp_axes, None),
        ),
        check_vma=False,
    )
```

```python
import math

import jax
import jax.numpy as jnp
from jax import lax
from jax.experimental import pallas as pl
from jax.experimental.pallas import tpu as pltpu
from jax.sharding import Mesh
from jax.sharding import PartitionSpec as P

HEADS = 24
KV_HEADS = 8
HEAD_DIM = 64
EXP_FF = 512
TOP = 8

epsilon = 1e-06
rope_base = 10000.0
masked = -1e30

GROUP = HEADS // KV_HEADS
HALF = HEAD_DIM // 2
LANES = 128
SLAB = 3 * LANES
META_ROWS = 16
BLOCK = 256
SWAP = [(0, 1), (1, 0)]
bf16 = jnp.bfloat16
f32 = jnp.float32


def dot(a, b, da, db):
    return lax.dot_general(a, b, (((da,), (db,)), ((), ())), preferred_element_type=f32)


def gather_bits(x, order, every, waits={}):
    have = []
    for i, axis in enumerate(order):
        if i in waits:
            x = after(x, waits[i])
        other = lax.ppermute(x, axis, SWAP)
        place = sum(every.index(h) < every.index(axis) for h in have)
        first = lax.axis_index(axis) == 0
        x = jnp.stack([jnp.where(first, x, other), jnp.where(first, other, x)], place)
        have.append(axis)
    return x


def after(x, *others):
    return lax.optimization_barrier((x, *others))[0]


def scatter_bits(x, order, every, sends=None):
    left = list(every)
    for axis in order:
        place = left.index(axis)
        mine = lax.axis_index(axis)
        keep = lax.dynamic_index_in_dim(x, mine, place, keepdims=False)
        send = lax.dynamic_index_in_dim(x, 1 - mine, place, keepdims=False)
        send = send.astype(bf16)
        if sends is not None:
            sends.append(send)
        other = lax.ppermute(send, axis, SWAP)
        left.pop(place)
        x = keep.astype(f32) + other.astype(f32)
        if left:
            x = x.astype(bf16)
    return x


def project_kernel(a_ref, b_ref, gain_ref, w_ref, cos_ref, sin_ref, low_ref, q_ref, k_ref, v_ref):
    step = pl.program_id(0)
    half = pl.num_programs(0) // 2

    def work(x_ref):
        x = x_ref[...].astype(f32)
        r = lax.rsqrt(jnp.mean(x * x, -1, keepdims=True) + epsilon)
        low = (x * r * gain_ref[...]).astype(bf16)
        low_ref[...] = low
        p = dot(low, w_ref[...], 1, 0)
        lane = lax.broadcasted_iota(jnp.int32, (x.shape[0], LANES), 1)
        u, w = p[:, :LANES], p[:, LANES : 2 * LANES]
        v = jnp.where(lane < HEAD_DIM, p[:, 2 * LANES :], 0.0)
        c, s = cos_ref[...], sin_ref[...]
        for at, turned in ((0, u * c - w * s), (LANES, w * c + u * s)):
            key = jnp.where(lane >= GROUP * HALF, turned, 0.0)
            key = pltpu.roll(key, HALF, 1) + pltpu.roll(key, 2 * HALF, 1) + pltpu.roll(key, 3 * HALF, 1)
            k_ref[:, at : at + LANES] = key.astype(bf16)
            for h in range(GROUP):
                q_ref[h, :, at : at + LANES] = jnp.where(lane // HALF == h, turned, 0.0).astype(bf16)
        zero = jnp.zeros(v.shape, bf16)
        first, second = v.astype(bf16), pltpu.roll(v, HEAD_DIM, 1).astype(bf16)
        for h in range(GROUP):
            for at in range(2):
                part = zero if h // 2 != at else (first if h % 2 == 0 else second)
                v_ref[h, :, at * LANES : (at + 1) * LANES] = part

    pl.when(step < half)(lambda: work(a_ref))
    pl.when(step >= half)(lambda: work(b_ref))


def project(part_a, part_b, gain, w_slab, cosine, sine):
    rows, width = part_a.shape
    length = 2 * rows
    steps = length // BLOCK
    half = steps // 2
    wide = 2 * LANES
    row = lambda cols: pl.BlockSpec((BLOCK, cols), lambda i: (i, 0))
    heads = pl.BlockSpec((GROUP, BLOCK, wide), lambda i: (0, i, 0))
    return pl.pallas_call(
        project_kernel,
        grid=(steps,),
        in_specs=[
            pl.BlockSpec((BLOCK, width), lambda i: (jnp.minimum(i, half - 1), 0)),
            pl.BlockSpec((BLOCK, width), lambda i: (jnp.maximum(i - half, 0), 0)),
            pl.BlockSpec((1, width), lambda i: (0, 0)),
            pl.BlockSpec((width, SLAB), lambda i: (0, 0)),
            row(LANES),
            row(LANES),
        ],
        out_specs=[row(width), heads, row(wide), heads],
        out_shape=[
            jax.ShapeDtypeStruct((length, width), bf16),
            jax.ShapeDtypeStruct((GROUP, length, wide), bf16),
            jax.ShapeDtypeStruct((length, wide), bf16),
            jax.ShapeDtypeStruct((GROUP, length, wide), bf16),
        ],
        compiler_params=pltpu.CompilerParams(vmem_limit_bytes=40 * 2**20),
        cost_estimate=pl.CostEstimate(
            flops=2 * length * width * SLAB, bytes_accessed=12 * 2**20, transcendentals=length
        ),
    )(part_a, part_b, gain, w_slab, cosine, sine)


def allowed_block(col_ref, row_ref, start, width):
    shape = (BLOCK, width)
    places = start + lax.broadcasted_iota(jnp.int32, shape, 0)
    keys = lax.broadcasted_iota(jnp.int32, shape, 1)
    same = col_ref[start : start + BLOCK, :] == row_ref[:, :width]
    return same & (keys <= places)


def attend_kernel(q_ref, k_ref, v_ref, col_ref, row_ref, o_ref, lse_ref):
    lane = lax.broadcasted_iota(jnp.int32, (BLOCK, LANES), 1)
    for start in range(0, k_ref.shape[0], BLOCK):
        width = start + BLOCK
        rows = slice(start, width)
        allowed = allowed_block(col_ref, row_ref, start, width)
        total = jnp.zeros((BLOCK, 2 * LANES), f32)
        logs = jnp.zeros((BLOCK, LANES), f32)
        for h in range(GROUP):
            s = dot(q_ref[h, rows, :], k_ref[:width, :], 1, 1) * 0.125
            s = jnp.where(allowed, s, masked)
            top = jnp.max(s, -1, keepdims=True)
            p = jnp.exp(s - top)
            below = jnp.sum(p, -1, keepdims=True)
            total = total + dot((p / below).astype(bf16), v_ref[h, :width, :], 1, 0)
            logs = jnp.where(lane == h, top + jnp.log(below), logs)
        o_ref[rows, :] = total.astype(bf16)
        lse_ref[rows, :] = logs


def attend(q, k, v, docs_col, docs_row):
    length, wide = k.shape
    return pl.pallas_call(
        attend_kernel,
        out_shape=[
            jax.ShapeDtypeStruct((length, wide), bf16),
            jax.ShapeDtypeStruct((length, LANES), f32),
        ],
        compiler_params=pltpu.CompilerParams(vmem_limit_bytes=48 * 2**20),
        cost_estimate=pl.CostEstimate(
            flops=2 * GROUP * length * length * wide,
            bytes_accessed=8 * 2**20,
            transcendentals=GROUP * length * length // 2,
        ),
    )(q, k, v, docs_col, docs_row)


def attend_back_kernel(
    q_ref, k_ref, v_ref, g_ref, lse_ref, col_ref, row_ref, cos_ref, sin_ref, out_ref, dk_ref, dv_ref
):
    length = k_ref.shape[0]
    wide = 2 * LANES
    dk_ref[...] = jnp.zeros_like(dk_ref)
    dv_ref[...] = jnp.zeros_like(dv_ref)
    lane = lax.broadcasted_iota(jnp.int32, (BLOCK, LANES), 1)
    wide_lane = lax.broadcasted_iota(jnp.int32, (BLOCK, wide), 1)
    for start in range(0, length, BLOCK):
        width = start + BLOCK
        rows = slice(start, width)
        allowed = allowed_block(col_ref, row_ref, start, width)
        dq = jnp.zeros((BLOCK, wide), f32)
        grads = g_ref[rows, :].astype(f32)
        for h in range(GROUP):
            q = q_ref[h, rows, :]
            lse = jnp.sum(jnp.where(lane == h, lse_ref[rows, :], 0.0), -1, keepdims=True)
            s = dot(q, k_ref[:width, :], 1, 1) * 0.125
            p = jnp.where(allowed, jnp.exp(jnp.where(allowed, s, masked) - lse), 0.0)
            g = jnp.where(wide_lane // HEAD_DIM == h, grads, 0.0).astype(bf16)
            dp = dot(g, v_ref[h, :width, :], 1, 1)
            delta = jnp.sum(p * dp, -1, keepdims=True)
            ds = (p * (dp - delta)).astype(bf16)
            part = dot(ds, k_ref[:width, :], 1, 0)
            dq = dq + jnp.where(wide_lane % LANES // HALF == h, part, 0.0)
            dk_ref[:width, :] += dot(ds, q, 0, 0)
            dv_ref[:width, :] += dot(p.astype(bf16), g, 0, 0)
        out_ref[rows, :LANES] = dq[:, :LANES].astype(out_ref.dtype)
        out_ref[rows, LANES:wide] = dq[:, LANES:].astype(out_ref.dtype)
    for start in range(0, length, BLOCK):
        rows = slice(start, start + BLOCK)
        halves = []
        for at in (0, LANES):
            key = dk_ref[rows, at : at + LANES]
            key = pltpu.roll(key, 3 * HALF, 1) + pltpu.roll(key, 2 * HALF, 1) + pltpu.roll(key, HALF, 1)
            both = jnp.where(lane >= GROUP * HALF, key, out_ref[rows, at : at + LANES])
            halves.append(both * 0.125)
        c, s = cos_ref[rows, :], sin_ref[rows, :]
        u, w = halves
        out_ref[rows, :LANES] = u * c + w * s
        out_ref[rows, LANES:wide] = w * c - u * s
        v = dv_ref[rows, :LANES] + dv_ref[rows, LANES:]
        v = v + pltpu.roll(v, HEAD_DIM, 1)
        out_ref[rows, wide:] = jnp.where(lane < HEAD_DIM, v, 0.0)


def attend_back_entry(*refs):
    *ins, out_ref, full_ref, dk_ref, dv_ref = refs
    attend_back_kernel(*ins, full_ref, dk_ref, dv_ref)
    out_ref[...] = full_ref[...].astype(bf16)


def attend_back(q, k, v, g, lse, docs_col, docs_row, cosine, sine):
    length, wide = k.shape
    return pl.pallas_call(
        attend_back_entry,
        out_shape=jax.ShapeDtypeStruct((length, SLAB), bf16),
        scratch_shapes=[
            pltpu.VMEM((length, SLAB), f32),
            pltpu.VMEM((length, wide), f32),
            pltpu.VMEM((length, wide), f32),
        ],
        compiler_params=pltpu.CompilerParams(vmem_limit_bytes=52 * 2**20),
        cost_estimate=pl.CostEstimate(
            flops=5 * GROUP * length * length * wide,
            bytes_accessed=8 * 2**20,
            transcendentals=GROUP * length * length // 2,
        ),
    )(q, k, v, g, lse, docs_col, docs_row, cosine, sine)


def pack(gate_up, down):
    blocks = [down[:, c : c + EXP_FF] for c in range(0, down.shape[1], EXP_FF)]
    return jnp.concatenate([gate_up, jnp.concatenate(blocks, 0)], 1)


def unpack_down(packed, high):
    rows = packed.shape[0] // high
    return jnp.concatenate([packed[c * rows : (c + 1) * rows, 2 * EXP_FF :] for c in range(high)], 1)


def half_places(at_ref, half, size):
    high = at_ref[2]
    place = high if half == 0 else 1 - high
    return pl.multiple_of(place * size, LANES)


def plain_kernel(at_ref, g_ref, pa, pb, pc, pd, out_ref):
    rows = g_ref.shape[0] * g_ref.shape[2]
    part = EXP_FF // 2
    width = g_ref.shape[3]
    g = g_ref[:, 0].reshape(rows, width)
    for j, packed in enumerate(((pa, pb), (pc, pd))):
        for half, p in enumerate(packed):
            plain = None
            for c in range(width // EXP_FF):
                cols = slice(c * EXP_FF, (c + 1) * EXP_FF)
                term = dot(g[:, cols], p[c * part : (c + 1) * part, :], 1, 1)
                plain = term if plain is None else plain + term
            at = pl.multiple_of(j * EXP_FF + half_places(at_ref, half, part), LANES)
            out_ref[:, 0, :, pl.ds(at, part)] = plain.reshape(g_ref.shape[0], g_ref.shape[2], part)


def plain_grads(places, grads, packed):
    holders, batches, local, width = grads.shape
    size = packed[0].shape[0]
    near = BLOCK // local
    block = lambda cols: pl.BlockSpec((near, 1, local, cols), lambda i, m, _: (i, m, 0, 0))
    return pl.pallas_call(
        plain_kernel,
        grid_spec=pltpu.PrefetchScalarGridSpec(
            num_scalar_prefetch=1,
            grid=(holders // near, batches),
            in_specs=[
                block(width),
                *[pl.BlockSpec((size, EXP_FF), lambda i, m, _: (0, 2))] * 4,
            ],
            out_specs=block(2 * EXP_FF),
        ),
        out_shape=jax.ShapeDtypeStruct((holders, batches, local, 2 * EXP_FF), f32),
        compiler_params=pltpu.CompilerParams(vmem_limit_bytes=40 * 2**20),
        cost_estimate=pl.CostEstimate(
            flops=4 * holders * batches * local * width * EXP_FF,
            bytes_accessed=14 * 2**20,
            transcendentals=0,
        ),
    )(places, grads, *packed)


def expert_kernel(at_ref, x_ref, g_ref, pa, pb, pc, pd, sum_ref, hid_ref, pair_ref):
    rows = x_ref.shape[0]
    size, width = pa.shape[0], 2 * pa.shape[0]
    double = 2 * EXP_FF
    me, experts = at_ref[0], at_ref[1]
    extra = x_ref[:, width:].astype(f32)
    both_plain = g_ref[:, 0].reshape(rows, double)
    lane = lax.broadcasted_iota(jnp.int32, extra.shape, 1)
    back = jnp.zeros(extra.shape, f32)
    totals = [None, None]
    for j, packed in enumerate(((pa, pb), (pc, pd))):
        expert = me if j == 0 else me ^ 4
        high = lane == expert
        low = lane == expert + experts
        share = jnp.sum(jnp.where(high | low, extra, 0.0), -1, keepdims=True)
        gate_up = None
        for half, p in enumerate(packed):
            term = dot(x_ref[:, pl.ds(half_places(at_ref, half, size), size)], p[...], 1, 0)
            gate_up = term if gate_up is None else gate_up + term
        gate, up = gate_up[:, :EXP_FF], gate_up[:, EXP_FF:]
        sg = 1.0 / (1.0 + jnp.exp(-gate))
        grown = gate * sg
        hidden = (grown * up).astype(bf16).astype(f32)
        grad_plain = both_plain[:, j * EXP_FF : (j + 1) * EXP_FF]
        gate_grad = jnp.sum(grad_plain * hidden, -1, keepdims=True)
        gate_high = gate_grad.astype(bf16).astype(f32)
        back = jnp.where(high, gate_high, jnp.where(low, gate_grad - gate_high, back))
        grad_hidden = share * grad_plain
        at = j * EXP_FF
        hid_ref[:, at : at + EXP_FF] = (share * hidden).astype(bf16)
        at = j * double
        first = (grad_hidden * up * sg * (1.0 + gate * (1.0 - sg))).astype(bf16)
        pair_ref[:, at : at + EXP_FF] = first
        pair_ref[:, at + EXP_FF : at + double] = (grad_hidden * grown).astype(bf16)
        for half, p in enumerate(packed):
            term = dot(pair_ref[:, at : at + double], p[...], 1, 1)
            totals[half] = term if totals[half] is None else totals[half] + term
    for half in range(2):
        sum_ref[:, pl.ds(half_places(at_ref, half, size), size)] = totals[half].astype(bf16)
    sum_ref[:, width:] = back.astype(bf16)


def run_experts(places, x, plain, m, packed):
    rows, wide = x.shape
    local = plain.shape[2]
    size, width = packed[0].shape
    block = lambda cols: pl.BlockSpec((BLOCK, cols), lambda i, _: (i, 0))
    whole = pl.BlockSpec((size, 2 * EXP_FF), lambda i, _: (0, 0))
    return pl.pallas_call(
        expert_kernel,
        grid_spec=pltpu.PrefetchScalarGridSpec(
            num_scalar_prefetch=1,
            grid=(rows // BLOCK,),
            in_specs=[
                block(wide),
                pl.BlockSpec((BLOCK // local, 1, local, 2 * EXP_FF), lambda i, _: (i, m, 0, 0)),
                *[whole] * 4,
            ],
            out_specs=[block(wide), block(2 * EXP_FF), block(4 * EXP_FF)],
        ),
        out_shape=[
            jax.ShapeDtypeStruct((rows, wide), bf16),
            jax.ShapeDtypeStruct((rows, 2 * EXP_FF), bf16),
            jax.ShapeDtypeStruct((rows, 4 * EXP_FF), bf16),
        ],
        compiler_params=pltpu.CompilerParams(vmem_limit_bytes=56 * 2**20),
        cost_estimate=pl.CostEstimate(
            flops=16 * rows * width * EXP_FF, bytes_accessed=16 * 2**20, transcendentals=rows * 2 * EXP_FF
        ),
    )(places, x, plain, *packed)


def mixture_kernel(at_ref, a_ref, b_ref, pa, pb, pc, pd, out_ref):
    size, width = pa.shape
    part = EXP_FF // 2

    def work(hid_ref):
        for c in range(width // EXP_FF):
            total = None
            for j, packed in enumerate(((pa, pb), (pc, pd))):
                for half, p in enumerate(packed):
                    at = pl.multiple_of(j * EXP_FF + half_places(at_ref, half, part), LANES)
                    term = dot(
                        hid_ref[:, pl.ds(at, part)],
                        p[c * part : (c + 1) * part, 2 * EXP_FF :],
                        1,
                        0,
                    )
                    total = term if total is None else total + term
            cols = slice(c * EXP_FF, (c + 1) * EXP_FF)
            shape = out_ref.shape[0], out_ref.shape[2], EXP_FF
            out_ref[:, 0, :, cols] = total.astype(bf16).reshape(shape)

    pl.when(pl.program_id(0) == 0)(lambda: work(a_ref))
    pl.when(pl.program_id(0) == 1)(lambda: work(b_ref))


def mix_experts(places, weighted, local, packed):
    rows = weighted[0].shape[0]
    size, width = packed[0].shape
    blocks = rows // BLOCK
    whole = pl.BlockSpec((size, width), lambda m, i, _: (0, 0))
    first = pl.BlockSpec((BLOCK, 2 * EXP_FF), lambda m, i, _: (jnp.where(m == 0, i, blocks - 1), 0))
    second = pl.BlockSpec((BLOCK, 2 * EXP_FF), lambda m, i, _: (jnp.where(m == 1, i, 0), 0))
    return pl.pallas_call(
        mixture_kernel,
        grid_spec=pltpu.PrefetchScalarGridSpec(
            num_scalar_prefetch=1,
            grid=(2, blocks),
            in_specs=[first, second, *[whole] * 4],
            out_specs=pl.BlockSpec(
                (BLOCK // local, 1, local, width), lambda m, i, _: (i, m, 0, 0)
            ),
        ),
        out_shape=jax.ShapeDtypeStruct((rows // local, 2, local, width), bf16),
        compiler_params=pltpu.CompilerParams(vmem_limit_bytes=48 * 2**20),
        cost_estimate=pl.CostEstimate(
            flops=8 * rows * width * EXP_FF, bytes_accessed=16 * 2**20, transcendentals=0
        ),
    )(places, *weighted, *packed)


def weights_kernel(
    at_ref, xa_ref, xb_ref, g_ref, ha_ref, hb_ref, pa_ref, pb_ref, send_ref, keep_ref
):
    size, width = keep_ref.shape
    rows = xa_ref.shape[0]
    part = EXP_FF // 2
    double = 2 * EXP_FF

    def work(half, out_ref):
        cols = pl.ds(half_places(at_ref, half, size), size)
        total = dot(xa_ref[:, cols], pa_ref[...], 0, 0) + dot(xb_ref[:, cols], pb_ref[...], 0, 0)
        out_ref[:, :double] = total.astype(out_ref.dtype)
        cols = pl.ds(half_places(at_ref, half, part), part)
        for c in range(width // EXP_FF):
            at = slice(c * EXP_FF, (c + 1) * EXP_FF)
            total = dot(ha_ref[:, cols], g_ref[:, 0, :, at].reshape(rows, EXP_FF), 0, 0)
            total = total + dot(hb_ref[:, cols], g_ref[:, 1, :, at].reshape(rows, EXP_FF), 0, 0)
            out_ref[c * part : (c + 1) * part, double:] = total.astype(out_ref.dtype)

    pl.when(pl.program_id(0) == 0)(lambda: work(1, send_ref))
    pl.when(pl.program_id(0) == 1)(lambda: work(0, keep_ref))


def expert_weights(j, places, xs, grads, weighted, pairs):
    rows, wide = xs[0].shape
    width = grads.shape[3]
    size = width // 2
    whole = pl.BlockSpec((rows, wide), lambda h, _: (0, 0))
    hidden = pl.BlockSpec((rows, EXP_FF), lambda h, _: (0, j))
    pair = pl.BlockSpec((rows, 2 * EXP_FF), lambda h, _: (0, j))
    half = pl.BlockSpec((size, width), lambda h, _: (0, 0))
    return pl.pallas_call(
        weights_kernel,
        grid_spec=pltpu.PrefetchScalarGridSpec(
            num_scalar_prefetch=1,
            grid=(2,),
            in_specs=[
                whole,
                whole,
                pl.BlockSpec(grads.shape, lambda h, _: (0, 0, 0, 0)),
                hidden,
                hidden,
                pair,
                pair,
            ],
            out_specs=[half, half],
        ),
        out_shape=[
            jax.ShapeDtypeStruct((size, width), bf16),
            jax.ShapeDtypeStruct((size, width), f32 if j == 0 else bf16),
        ],
        compiler_params=pltpu.CompilerParams(vmem_limit_bytes=60 * 2**20),
        cost_estimate=pl.CostEstimate(
            flops=12 * rows * width * EXP_FF, bytes_accessed=16 * 2**20, transcendentals=0
        ),
    )(places, *xs, grads, *weighted, *pairs)


def heads_to_rows(a, b):
    lane = lax.broadcasted_iota(jnp.int32, (a.shape[0], LANES), 1)
    low = lane < HEAD_DIM
    b_first, b_second = (pltpu.roll(t, HEAD_DIM, 1) for t in (b[:, :LANES], b[:, LANES:]))
    return (a[:, :LANES], jnp.where(low, a[:, LANES:], b_first), jnp.where(low, b_first, b_second))


def rows_to_heads(first, second, third):
    lane = lax.broadcasted_iota(jnp.int32, first.shape, 1)
    low = lane < HEAD_DIM
    second_turned, third_turned = (pltpu.roll(t, HEAD_DIM, 1) for t in (second, third))
    a = (first, jnp.where(low, second, 0.0))
    b = (jnp.where(low, second_turned, third_turned), jnp.where(low, third_turned, 0.0))
    return a, b


def middle_kernel(
    experts, heads_ref, x_ref, w_ref, gain_ref, router_ref, routes_ref,
    y_ref, sent_ref, low_ref, probs_ref, gates_ref, chosen_ref, pick_ref, scale_ref,
):
    batches, local, width = x_ref.shape
    for m in range(batches):
        for k in range(0, KV_HEADS, 2):
            a, b = (heads_ref[m * KV_HEADS + k + i].astype(f32) for i in range(2))
            at = k * GROUP * HEAD_DIM
            for i, part in enumerate(heads_to_rows(a, b)):
                cols = slice(at + i * LANES, at + (i + 1) * LANES)
                low_ref[m * local : (m + 1) * local, cols] = part.astype(bf16)
    rows = batches * local
    y = x_ref[...].reshape(rows, width).astype(f32) + dot(low_ref[...], w_ref[...], 1, 1)
    y_ref[...] = y
    r = lax.rsqrt(jnp.mean(y * y, -1, keepdims=True) + epsilon)
    second = (y * r * gain_ref[...]).astype(bf16)
    lane = lax.broadcasted_iota(jnp.int32, (rows, LANES), 1)
    logits = jnp.where(lane < experts, dot(second, router_ref[...], 1, 0), masked)
    raised = jnp.exp(logits - jnp.max(logits, -1, keepdims=True))
    probs = raised / jnp.sum(raised, -1, keepdims=True)
    chosen = jnp.zeros((rows, LANES), f32)
    for k in range(TOP):
        chosen = jnp.where(routes_ref[:, k : k + 1] == lane, 1.0, chosen)
    picked = jnp.sum(chosen * probs, -1, keepdims=True)
    gates = chosen * probs / picked
    high = gates.astype(bf16).astype(f32)
    extra = high + pltpu.roll(gates - high, experts, 1)
    sent_ref[:, :, :width] = second.reshape(batches, local, width)
    sent_ref[:, :, width:] = extra.astype(bf16).reshape(batches, local, LANES)
    probs_ref[...] = probs
    gates_ref[...] = gates
    chosen_ref[...] = chosen
    pick_ref[...] = picked
    scale_ref[...] = r


def middle_rows(experts, heads, tokens, out_full, gain, router, routes):
    batches, local, width = tokens.shape
    rows = batches * local
    small = jax.ShapeDtypeStruct((rows, LANES), f32)
    column = jax.ShapeDtypeStruct((rows, 1), f32)
    return pl.pallas_call(
        lambda *refs: middle_kernel(experts, *refs),
        out_shape=[
            jax.ShapeDtypeStruct((rows, width), f32),
            jax.ShapeDtypeStruct((batches, local, width + LANES), bf16),
            jax.ShapeDtypeStruct((rows, width), bf16),
            small,
            small,
            small,
            column,
            column,
        ],
        compiler_params=pltpu.CompilerParams(vmem_limit_bytes=40 * 2**20),
        cost_estimate=pl.CostEstimate(
            flops=2 * rows * width * width, bytes_accessed=8 * 2**20, transcendentals=rows * LANES
        ),
    )(heads, tokens, out_full, gain, router, routes)


def middle_back_kernel(
    experts, came_a_ref, came_b_ref, g_ref, y_ref, probs_ref, gates_ref, chosen_ref,
    pick_ref, scale_ref, gain_ref, router_ref, w_ref,
    heads_ref, grad_ref, branch_ref, logits_ref, gain_grad_ref,
):
    batches, local, width = g_ref.shape
    rows = batches * local
    came = jnp.concatenate([came_a_ref[...], came_b_ref[...]], 0)
    extra = came[:, width:]
    lane = lax.broadcasted_iota(jnp.int32, (rows, LANES), 1)
    chosen, probs, gates = chosen_ref[...], probs_ref[...], gates_ref[...]
    both = extra + pltpu.roll(extra, LANES - experts, 1)
    grad_gates = jnp.where(lane < experts, both, 0.0) * chosen
    mean = jnp.sum(grad_gates * gates, -1, keepdims=True)
    grad_picked = chosen * (grad_gates - mean) / pick_ref[...]
    grad_logits = probs * (grad_picked - jnp.sum(probs * grad_picked, -1, keepdims=True))
    grad_logits = grad_logits.astype(bf16)
    logits_ref[...] = grad_logits
    grad_second = came[:, :width] + dot(grad_logits, router_ref[...], 1, 1)
    r = scale_ref[...]
    n = y_ref[...] * r
    gain_grad_ref[...] = jnp.sum(grad_second * n, 0, keepdims=True)
    c = grad_second * gain_ref[...]
    grad_y = g_ref[...].reshape(rows, width).astype(f32)
    grad_y = grad_y + r * (c - n * jnp.mean(c * n, -1, keepdims=True))
    grad_ref[...] = grad_y
    branch = grad_y.astype(bf16)
    branch_ref[...] = branch
    grad = dot(branch, w_ref[...], 1, 0)
    for k in range(0, KV_HEADS, 2):
        at = k * GROUP * HEAD_DIM
        parts = (grad[:, at + i * LANES : at + (i + 1) * LANES] for i in range(3))
        for j, head in enumerate(rows_to_heads(*parts)):
            for i, part in enumerate(head):
                part = part.astype(bf16).reshape(batches, local, LANES)
                for m in range(batches):
                    cols = slice(i * LANES, (i + 1) * LANES)
                    heads_ref[m * KV_HEADS + k + j, :, cols] = part[m]


def middle_back(experts, came, cotangent, kept, gain, router, out_full):
    batches, local, width = cotangent.shape
    rows = batches * local
    return pl.pallas_call(
        lambda *refs: middle_back_kernel(experts, *refs),
        out_shape=[
            jax.ShapeDtypeStruct((batches * KV_HEADS, local, 2 * LANES), bf16),
            jax.ShapeDtypeStruct((rows, width), f32),
            jax.ShapeDtypeStruct((rows, width), bf16),
            jax.ShapeDtypeStruct((rows, LANES), bf16),
            jax.ShapeDtypeStruct((1, width), f32),
        ],
        compiler_params=pltpu.CompilerParams(vmem_limit_bytes=40 * 2**20),
        cost_estimate=pl.CostEstimate(
            flops=2 * rows * width * width, bytes_accessed=10 * 2**20, transcendentals=0
        ),
    )(*came, cotangent, *kept, gain, router, out_full)


def finish_kernel(slab_ref, w_ref, gain_ref, grad_ref, gain_grad_ref):
    rows = w_ref.shape[0]
    lane = lax.broadcasted_iota(jnp.int32, (rows, LANES), 1)
    per_tile = LANES // HALF

    def tile(pieces):
        out = None
        for i, (source, group) in enumerate(pieces):
            shift = (i - group) % per_tile * HALF
            moved = pltpu.roll(source, shift, 1) if shift else source
            out = moved if out is None else jnp.where(lane // HALF == i, moved, out)
        return out

    batches = slab_ref.shape[0] // KV_HEADS
    total = jnp.zeros((rows, 1), f32)

    def put(at, value):
        grad_ref[:, at : at + LANES] = value
        return jnp.sum(value * w_ref[:, at : at + LANES].astype(f32), -1, keepdims=True)

    for k in range(0, KV_HEADS, 2):
        sums = []
        for i in range(2):
            terms = [slab_ref[m * KV_HEADS + k + i].astype(f32) for m in range(batches)]
            sums.append(sum(terms[1:], terms[0]))
        u, w, v = zip(*((t[:, :LANES], t[:, LANES : 2 * LANES], t[:, 2 * LANES :]) for t in sums))
        halves_of = [(part, group) for i in range(2) for group in range(GROUP) for part in (u[i], w[i])]
        for i in range(0, len(halves_of), per_tile):
            at = k * GROUP * HEAD_DIM + i * HALF
            total = total + put(at, tile(halves_of[i : i + per_tile]))
        at = HEADS * HEAD_DIM + k * HEAD_DIM
        total = total + put(at, tile([(part, GROUP) for i in range(2) for part in (u[i], w[i])]))
        at = (HEADS + KV_HEADS) * HEAD_DIM + k * HEAD_DIM
        total = total + put(at, jnp.where(lane < HEAD_DIM, v[0], pltpu.roll(v[1], HEAD_DIM, 1)))
    gain_grad_ref[...] = total / gain_ref[...].astype(f32)


def finish(slab, w_qkv, gain):
    return pl.pallas_call(
        finish_kernel,
        out_shape=[
            jax.ShapeDtypeStruct(w_qkv.shape, f32),
            jax.ShapeDtypeStruct(gain.shape, f32),
        ],
        compiler_params=pltpu.CompilerParams(vmem_limit_bytes=32 * 2**20),
    )(slab, w_qkv, gain)


def split_columns(w_qkv):
    rows = w_qkv.shape[0]
    q_width, k_width = HEADS * HEAD_DIM, KV_HEADS * HEAD_DIM
    q = w_qkv[:, :q_width].reshape(rows, KV_HEADS, GROUP, 2, HALF)
    k = w_qkv[:, q_width : q_width + k_width].reshape(rows, KV_HEADS, 1, 2, HALF)
    both = jnp.concatenate([q, k], 2)
    return (
        both[:, :, :, 0].reshape(rows, KV_HEADS, LANES),
        both[:, :, :, 1].reshape(rows, KV_HEADS, LANES),
        w_qkv[:, q_width + k_width :].reshape(rows, KV_HEADS, HEAD_DIM),
    )


def halves(x):
    high = lax.reduce_precision(x, 8, 7)
    return high.astype(bf16), (x - high).astype(bf16)


def gather_sequence(tokens, ex_axes, mb_axis):
    mine = lax.axis_index(mb_axis)
    own = lax.dynamic_index_in_dim(tokens, mine, 0, keepdims=False)
    other = lax.ppermute(
        lax.dynamic_index_in_dim(tokens, 1 - mine, 0, keepdims=False), mb_axis, SWAP
    )
    first = mine == 0
    group = jnp.stack([jnp.where(first, own, other), jnp.where(first, other, own)], 0)
    middle = tuple(a for a in ex_axes[:-2] if a != mb_axis)
    return gather_bits(group, middle, middle), middle, other


def on_device(
    dp_axes,
    ex_axes,
    tokens,
    cotangent,
    segments,
    positions,
    routes,
    w_qkv,
    w_out,
    w_router,
    norm_attn,
    norm_ffn,
    w_gate_up,
    w_down,
):
    batches, local, width = tokens.shape
    experts = w_router.shape[1]
    count = 2 ** len(ex_axes)
    length = count * local
    units = batches * KV_HEADS
    parts = count // units
    shard = w_qkv.shape[0]
    rows = batches * local
    me = lax.axis_index(ex_axes)
    bit = lambda b: ex_axes[len(ex_axes) - 1 - b]
    pair_axis = bit(2)
    far = tuple(a for a in ex_axes[:-2] if a != pair_axis)
    token_axes = ex_axes[-2:] + far
    orders = (far + (bit(0), bit(1)), far + (bit(1), bit(0)))

    mb_axis = bit(3)

    u_cols, w_cols, v_cols = split_columns(w_qkv)
    small = jnp.concatenate([norm_attn[:, None], norm_ffn[:, None], w_router], 1)
    small = jnp.pad(small, ((0, 0), (0, SLAB - 2 * LANES - HEAD_DIM - small.shape[1])))
    small = jnp.broadcast_to(small[:, None, :], (shard, KV_HEADS, small.shape[1]))
    slab = jnp.transpose(jnp.concatenate([u_cols, w_cols, v_cols, small], -1), (1, 0, 2))
    meta = jnp.stack([segments, positions // 64, positions % 64], 1).astype(bf16)
    meta = jnp.pad(meta, ((0, 0), (0, META_ROWS - 3), (0, SLAB - local)))
    payload = jnp.concatenate(
        [
            jnp.broadcast_to(slab[None], (batches,) + slab.shape),
            jnp.broadcast_to(meta[:, None], (batches, KV_HEADS) + meta.shape[1:]),
        ],
        2,
    ).reshape(units, shard + META_ROWS, SLAB)
    payload = jnp.concatenate([payload] * parts, 0)
    group, middle, swapped = gather_sequence(tokens, ex_axes, mb_axis)
    arrived = lax.all_to_all(after(payload, swapped), ex_axes, 0, 0, tiled=True)
    w_slab = gather_bits(arrived[:, :shard].reshape(count * shard, SLAB), dp_axes, dp_axes)
    w_slab = w_slab.reshape(width, SLAB)
    extra_at = 2 * LANES + HEAD_DIM
    gain_attn = w_slab[:, extra_at].astype(f32)
    gain_ffn = w_slab[:, extra_at + 1].astype(f32)
    router_full = w_slab[:, extra_at + 2 : extra_at + 2 + experts]
    info = arrived[:, shard : shard + 3, :local].astype(jnp.int32)
    docs = info[:, 0].reshape(length)
    places = (info[:, 1] * 64 + info[:, 2]).reshape(length)
    frequency = rope_base ** (-jnp.arange(HALF, dtype=f32) / HALF)
    angles = places.astype(f32)[:, None] * jnp.tile(frequency, GROUP + 1)[None, :]
    cosine, sine = jnp.cos(angles), jnp.sin(angles)
    docs_col, docs_row = docs[:, None], docs[None, :]

    high_axis, low_axes = dp_axes[0], dp_axes[1:]
    blocks = width // EXP_FF
    expert_own = pack(w_gate_up[0], w_down[0])
    if low_axes:
        parted = gather_bits(expert_own, low_axes, low_axes)
        parted = parted.reshape((-1,) + expert_own.shape)
        lower = parted[..., 2 * EXP_FF :].reshape(parted.shape[0], blocks, -1, EXP_FF)
        expert_own = jnp.concatenate(
            [
                parted[..., : 2 * EXP_FF].reshape(-1, 2 * EXP_FF),
                lower.transpose(1, 0, 2, 3).reshape(-1, EXP_FF),
            ],
            1,
        )
    group, expert_own = lax.optimization_barrier((group, expert_own))
    group = jnp.moveaxis(group, len(middle), 0)
    sides = []
    for part, last in ((group[0], (bit(0), bit(1))), (group[1], (bit(1), bit(0)))):
        pair = gather_bits(part, last, (bit(1), bit(0)), {1: arrived})
        sides.append(jnp.moveaxis(pair, (0, 1), (len(middle), len(middle) + 1)))
    if len(middle) == 1:
        sides = [s.reshape(length // 2, width) for s in sides]
    else:
        at = ex_axes.index(mb_axis)
        whole = jnp.stack(sides, at).reshape(length, width)
        sides = [whole[: length // 2], whole[length // 2 :]]

    out_full = lax.all_gather(w_out, dp_axes + ex_axes, axis=0, tiled=True)
    grad_rows = gather_bits(after(cotangent, group), far, far)
    grad_rows = lax.all_gather(grad_rows, ex_axes[-2:], axis=0)
    grad_rows = grad_rows.reshape((-1,) + cotangent.shape)
    qkv_mixed = jnp.concatenate([p.reshape(shard, -1) for p in (u_cols, w_cols, v_cols)], 1)
    qkv_full = lax.all_gather(qkv_mixed, dp_axes + ex_axes, axis=0, tiled=True)

    cut = expert_own.shape[0] // 2
    other_parts = [lax.ppermute(t, pair_axis, SWAP) for t in (expert_own[:cut], expert_own[cut:])]

    first_low, q, k, v = project(*sides, gain_attn[None, :], w_slab, cosine, sine)
    q = after(q, other_parts[0])
    attended, lse = attend(q, k, v, docs_col, docs_row)
    back = lax.all_to_all(attended.reshape(count, local, 2 * LANES), ex_axes, 0, 0, tiled=True)
    expert_other = jnp.concatenate([after(t, attended) for t in other_parts], 0)
    packed = [
        expert_own,
        lax.ppermute(expert_own, high_axis, SWAP),
        expert_other,
        lax.ppermute(expert_other, high_axis, SWAP),
    ]
    x = tokens.reshape(rows, width).astype(f32)
    router_full = jnp.pad(router_full, ((0, 0), (0, LANES - experts)))
    y_one, sent, attended_low, *kept = middle_rows(
        experts, back[:units], tokens, out_full, gain_ffn[None, :], router_full, routes.reshape(rows, TOP)
    )
    second_low = sent[:, :, :width].reshape(rows, width)
    sent = after(sent, other_parts[1])

    places_at = jnp.stack([me, jnp.int32(experts), lax.axis_index(high_axis)]).astype(jnp.int32)
    weighted, pairs, stages = [], [], []
    gathered = []
    ahead = sent
    for m in range(batches):
        far_part = gather_bits(after(sent[m], ahead), far, far)
        ahead = far_part
        if m == 0:
            grads = after(grad_rows, far_part)
            plain = plain_grads(places_at, grads, packed)
        last = orders[m % 2][len(far) :]
        part = gather_bits(far_part, last, (bit(1), bit(0)), {1: plain} if m else {})
        gathered.append(part.reshape(-1, width + LANES))
    for m in range(batches):
        back_rows, hid, pair = run_experts(places_at, gathered[m], plain, m, packed)
        back_rows = back_rows.reshape((2,) * len(token_axes) + (local, width + LANES))
        stages.append(scatter_bits(back_rows, orders[m % 2][-1:], token_axes))
        weighted.append(hid)
        pairs.append(pair)
    grad_inputs = []
    for m in range(batches):
        order = orders[m % 2][::-1]
        left = tuple(a for a in token_axes if a != order[0])
        grad_inputs.append(scatter_bits(stages[m], order[1:], left))

    def expert_grads(j, *others):
        send, keep = expert_weights(
            j, places_at, gathered, grad_rows, [after(t, *others) for t in weighted], pairs
        )
        grad = keep.astype(f32) + lax.ppermute(send, high_axis, SWAP).astype(f32)
        if low_axes:
            count_low = 2 ** len(low_axes)
            parted = grad[:, : 2 * EXP_FF].reshape(count_low, -1, 2 * EXP_FF)
            lower = grad[:, 2 * EXP_FF :].reshape(blocks, count_low, -1, EXP_FF)
            lower = lower.transpose(1, 0, 2, 3).reshape(count_low, -1, EXP_FF)
            parted = jnp.concatenate([parted, lower], -1)
            parted = parted.reshape((2,) * len(low_axes) + parted.shape[1:])
            grad = scatter_bits(parted.astype(bf16), low_axes, low_axes)
        return grad

    grad_theirs = expert_grads(1, stages[0]).astype(bf16)
    cut = grad_theirs.shape[0] // 2
    grad_received = [
        lax.ppermute(t, pair_axis, SWAP) for t in (grad_theirs[:cut], grad_theirs[cut:])
    ]
    grad_inputs[-1] = after(grad_inputs[-1], grad_theirs)

    payload, grad_y, grad_branch, grad_logits, grad_gain_ffn = middle_back(
        experts, grad_inputs, cotangent, [y_one, *kept], gain_ffn[None, :], router_full, out_full
    )
    payload = jnp.concatenate([payload] * parts, 0)
    grad_heads = lax.all_to_all(payload, ex_axes, 0, 0, tiled=True).reshape(length, 2 * LANES)

    mixture = mix_experts(places_at, [after(t, payload) for t in weighted], local, packed)
    mixtures = lax.psum_scatter(
        after(mixture.reshape(-1, width), qkv_full), token_axes, scatter_dimension=0, tiled=True
    )
    grad_branch = after(grad_branch, payload)
    grad_out = dot(grad_branch, attended_low, 0, 0)
    extras = dot(after(second_low, payload), grad_logits, 0, 0)
    extras = jnp.where(jnp.arange(LANES) == experts, grad_gain_ffn.reshape(width, 1), extras)
    dense = jnp.concatenate([grad_out, extras], 1).astype(bf16)
    dense = scatter_bits(
        dense.reshape((2,) * len(dp_axes) + (-1, dense.shape[1])), dp_axes, dp_axes
    )
    dense = dense.astype(bf16).reshape((2,) * len(ex_axes) + (shard, -1))
    grad_heads = after(grad_heads, dense, mixture, grad_received[0])
    dense_one = scatter_bits(dense, ex_axes[-1:], ex_axes)
    dense_two = scatter_bits(dense_one, ex_axes[-2:-1], ex_axes[:-1])
    dense = scatter_bits(dense_two, ex_axes[:-2][::-1], ex_axes[:-2])

    grad_proj = attend_back(q, k, v, grad_heads, lse, docs_col, docs_row, cosine, sine)
    back = lax.all_to_all(grad_proj.reshape(count, local, SLAB), ex_axes, 0, 0, tiled=True)
    back = back[:units].reshape(batches, KV_HEADS, local, SLAB).transpose(0, 2, 1, 3)
    back = jnp.concatenate(
        [
            back[..., :LANES].reshape(rows, -1),
            back[..., LANES : 2 * LANES].reshape(rows, -1),
            back[..., 2 * LANES : 2 * LANES + HEAD_DIM].reshape(rows, -1),
        ],
        1,
    )
    grad_first = dot(after(back, dense_two), qkv_full, 1, 1)
    grad_slab = dot(first_low, grad_proj, 0, 0)
    grad_slab = scatter_bits(
        grad_slab.reshape((2,) * len(dp_axes) + (-1, SLAB)), dp_axes, dp_axes
    )
    grad_slab = lax.all_to_all(
        after(grad_slab.astype(bf16), dense_one, grad_received[1]).reshape(count, shard, SLAB), ex_axes, 0, 0, tiled=True
    )
    grad_qkv, grad_gain_attn = finish(grad_slab[:units], w_qkv, norm_attn[:, None])
    grad_gain_attn = grad_gain_attn[:, 0]
    grad_packed = expert_grads(0, grad_proj) + jnp.concatenate(grad_received, 0).astype(f32)
    grad_gate_up = grad_packed[:, : 2 * EXP_FF]
    grad_down = unpack_down(grad_packed, blocks)
    mixed = y_one + after(mixtures, grad_slab).astype(f32)
    r_one = lax.rsqrt(jnp.mean(x * x, -1, keepdims=True) + epsilon)
    n_one = x * r_one
    c_one = grad_first * gain_attn
    grad_tokens = grad_y + r_one * (c_one - n_one * jnp.mean(c_one * n_one, -1, keepdims=True))

    out_width = HEADS * HEAD_DIM
    return (
        mixed.astype(bf16).reshape(tokens.shape),
        grad_tokens.reshape(tokens.shape),
        grad_qkv,
        dense[:, :out_width],
        dense[:, out_width : out_width + experts],
        grad_gain_attn,
        dense[:, out_width + experts],
        grad_gate_up[None],
        grad_down[None],
    )


def solution(mesh):
    dp_bits = int(math.log2(mesh.shape["dp"]))
    ex_bits = int(math.log2(mesh.shape["expert"]))
    dp_axes = tuple(f"d{b}" for b in reversed(range(dp_bits)))
    ex_axes = tuple(f"e{b}" for b in reversed(range(ex_bits)))
    cube = Mesh(mesh.devices.reshape((2,) * (dp_bits + ex_bits)), dp_axes + ex_axes)
    every = dp_axes + ex_axes
    by_tokens = P(None, every, None)

    def run(*arrays):
        return on_device(dp_axes, ex_axes, *arrays)

    return jax.shard_map(
        run,
        mesh=cube,
        in_specs=(
            by_tokens,
            by_tokens,
            P(None, every),
            P(None, every),
            by_tokens,
            P(every, None),
            P(every, None),
            P(every, None),
            P(every),
            P(every),
            P(ex_axes, dp_axes, None),
            P(ex_axes, dp_axes, None),
        ),
        out_specs=(
            by_tokens,
            by_tokens,
            P(every, None),
            P(every, None),
            P(every, None),
            P(every),
            P(every),
            P(ex_axes, dp_axes, None),
            P(ex_axes, dp_axes, None),
        ),
        check_vma=False,
    )
```

```python
import math

import jax
import jax.numpy as jnp
from jax import lax
from jax.experimental import pallas as pl
from jax.experimental.pallas import tpu as pltpu
from jax.sharding import Mesh
from jax.sharding import PartitionSpec as P

HEADS = 24
KV_HEADS = 8
HEAD_DIM = 64
EXP_FF = 512
TOP = 8

epsilon = 1e-06
rope_base = 10000.0
masked = -1e30

GROUP = HEADS // KV_HEADS
HALF = HEAD_DIM // 2
LANES = 128
SLAB = 3 * LANES
META_ROWS = 16
BLOCK = 256
SWAP = [(0, 1), (1, 0)]
bf16 = jnp.bfloat16
f32 = jnp.float32


def dot(a, b, da, db):
    return lax.dot_general(a, b, (((da,), (db,)), ((), ())), preferred_element_type=f32)


def gather_bits(x, order, every, waits={}):
    have = []
    for i, axis in enumerate(order):
        if i in waits:
            x = after(x, waits[i])
        other = lax.ppermute(x, axis, SWAP)
        place = sum(every.index(h) < every.index(axis) for h in have)
        first = lax.axis_index(axis) == 0
        x = jnp.stack([jnp.where(first, x, other), jnp.where(first, other, x)], place)
        have.append(axis)
    return x


def after(x, *others):
    return lax.optimization_barrier((x, *others))[0]


def scatter_bits(x, order, every, sends=None):
    left = list(every)
    for axis in order:
        place = left.index(axis)
        mine = lax.axis_index(axis)
        keep = lax.dynamic_index_in_dim(x, mine, place, keepdims=False)
        send = lax.dynamic_index_in_dim(x, 1 - mine, place, keepdims=False)
        send = send.astype(bf16)
        if sends is not None:
            sends.append(send)
        other = lax.ppermute(send, axis, SWAP)
        left.pop(place)
        x = keep.astype(f32) + other.astype(f32)
        if left:
            x = x.astype(bf16)
    return x


def project_kernel(a_ref, b_ref, gain_ref, w_ref, cos_ref, sin_ref, low_ref, q_ref, k_ref, v_ref):
    step = pl.program_id(0)
    half = pl.num_programs(0) // 2

    def work(x_ref):
        x = x_ref[...].astype(f32)
        r = lax.rsqrt(jnp.mean(x * x, -1, keepdims=True) + epsilon)
        low = (x * r * gain_ref[...]).astype(bf16)
        low_ref[...] = low
        p = dot(low, w_ref[...], 1, 0)
        lane = lax.broadcasted_iota(jnp.int32, (x.shape[0], LANES), 1)
        u, w = p[:, :LANES], p[:, LANES : 2 * LANES]
        v = jnp.where(lane < HEAD_DIM, p[:, 2 * LANES :], 0.0)
        c, s = cos_ref[...], sin_ref[...]
        for at, turned in ((0, u * c - w * s), (LANES, w * c + u * s)):
            key = jnp.where(lane >= GROUP * HALF, turned, 0.0)
            key = pltpu.roll(key, HALF, 1) + pltpu.roll(key, 2 * HALF, 1) + pltpu.roll(key, 3 * HALF, 1)
            k_ref[:, at : at + LANES] = key.astype(bf16)
            for h in range(GROUP):
                q_ref[h, :, at : at + LANES] = jnp.where(lane // HALF == h, turned, 0.0).astype(bf16)
        zero = jnp.zeros(v.shape, bf16)
        first, second = v.astype(bf16), pltpu.roll(v, HEAD_DIM, 1).astype(bf16)
        for h in range(GROUP):
            for at in range(2):
                part = zero if h // 2 != at else (first if h % 2 == 0 else second)
                v_ref[h, :, at * LANES : (at + 1) * LANES] = part

    pl.when(step < half)(lambda: work(a_ref))
    pl.when(step >= half)(lambda: work(b_ref))


def project(part_a, part_b, gain, w_slab, cosine, sine):
    rows, width = part_a.shape
    length = 2 * rows
    steps = length // BLOCK
    half = steps // 2
    wide = 2 * LANES
    row = lambda cols: pl.BlockSpec((BLOCK, cols), lambda i: (i, 0))
    heads = pl.BlockSpec((GROUP, BLOCK, wide), lambda i: (0, i, 0))
    return pl.pallas_call(
        project_kernel,
        grid=(steps,),
        in_specs=[
            pl.BlockSpec((BLOCK, width), lambda i: (jnp.minimum(i, half - 1), 0)),
            pl.BlockSpec((BLOCK, width), lambda i: (jnp.maximum(i - half, 0), 0)),
            pl.BlockSpec((1, width), lambda i: (0, 0)),
            pl.BlockSpec((width, SLAB), lambda i: (0, 0)),
            row(LANES),
            row(LANES),
        ],
        out_specs=[row(width), heads, row(wide), heads],
        out_shape=[
            jax.ShapeDtypeStruct((length, width), bf16),
            jax.ShapeDtypeStruct((GROUP, length, wide), bf16),
            jax.ShapeDtypeStruct((length, wide), bf16),
            jax.ShapeDtypeStruct((GROUP, length, wide), bf16),
        ],
        compiler_params=pltpu.CompilerParams(vmem_limit_bytes=40 * 2**20),
        cost_estimate=pl.CostEstimate(
            flops=2 * length * width * SLAB, bytes_accessed=12 * 2**20, transcendentals=length
        ),
    )(part_a, part_b, gain, w_slab, cosine, sine)


def allowed_block(col_ref, row_ref, start, width):
    shape = (BLOCK, width)
    places = start + lax.broadcasted_iota(jnp.int32, shape, 0)
    keys = lax.broadcasted_iota(jnp.int32, shape, 1)
    same = col_ref[start : start + BLOCK, :] == row_ref[:, :width]
    return same & (keys <= places)


def attend_kernel(q_ref, k_ref, v_ref, col_ref, row_ref, o_ref, lse_ref):
    lane = lax.broadcasted_iota(jnp.int32, (BLOCK, LANES), 1)
    for start in range(0, k_ref.shape[0], BLOCK):
        width = start + BLOCK
        rows = slice(start, width)
        allowed = allowed_block(col_ref, row_ref, start, width)
        total = jnp.zeros((BLOCK, 2 * LANES), f32)
        logs = jnp.zeros((BLOCK, LANES), f32)
        for h in range(GROUP):
            s = dot(q_ref[h, rows, :], k_ref[:width, :], 1, 1) * 0.125
            s = jnp.where(allowed, s, masked)
            top = jnp.max(s, -1, keepdims=True)
            p = jnp.exp(s - top)
            below = jnp.sum(p, -1, keepdims=True)
            total = total + dot((p / below).astype(bf16), v_ref[h, :width, :], 1, 0)
            logs = jnp.where(lane == h, top + jnp.log(below), logs)
        o_ref[rows, :] = total.astype(bf16)
        lse_ref[rows, :] = logs


def attend(q, k, v, docs_col, docs_row):
    length, wide = k.shape
    return pl.pallas_call(
        attend_kernel,
        out_shape=[
            jax.ShapeDtypeStruct((length, wide), bf16),
            jax.ShapeDtypeStruct((length, LANES), f32),
        ],
        compiler_params=pltpu.CompilerParams(vmem_limit_bytes=48 * 2**20),
        cost_estimate=pl.CostEstimate(
            flops=2 * GROUP * length * length * wide,
            bytes_accessed=8 * 2**20,
            transcendentals=GROUP * length * length // 2,
        ),
    )(q, k, v, docs_col, docs_row)


def attend_back_kernel(
    q_ref, k_ref, v_ref, g_ref, lse_ref, col_ref, row_ref, cos_ref, sin_ref, out_ref, dk_ref, dv_ref
):
    length = k_ref.shape[0]
    wide = 2 * LANES
    dk_ref[...] = jnp.zeros_like(dk_ref)
    dv_ref[...] = jnp.zeros_like(dv_ref)
    lane = lax.broadcasted_iota(jnp.int32, (BLOCK, LANES), 1)
    wide_lane = lax.broadcasted_iota(jnp.int32, (BLOCK, wide), 1)
    for start in range(0, length, BLOCK):
        width = start + BLOCK
        rows = slice(start, width)
        allowed = allowed_block(col_ref, row_ref, start, width)
        dq = jnp.zeros((BLOCK, wide), f32)
        grads = g_ref[rows, :].astype(f32)
        for h in range(GROUP):
            q = q_ref[h, rows, :]
            lse = jnp.sum(jnp.where(lane == h, lse_ref[rows, :], 0.0), -1, keepdims=True)
            s = dot(q, k_ref[:width, :], 1, 1) * 0.125
            p = jnp.where(allowed, jnp.exp(jnp.where(allowed, s, masked) - lse), 0.0)
            g = jnp.where(wide_lane // HEAD_DIM == h, grads, 0.0).astype(bf16)
            dp = dot(g, v_ref[h, :width, :], 1, 1)
            delta = jnp.sum(p * dp, -1, keepdims=True)
            ds = (p * (dp - delta)).astype(bf16)
            part = dot(ds, k_ref[:width, :], 1, 0)
            dq = dq + jnp.where(wide_lane % LANES // HALF == h, part, 0.0)
            dk_ref[:width, :] += dot(ds, q, 0, 0)
            dv_ref[:width, :] += dot(p.astype(bf16), g, 0, 0)
        out_ref[rows, :LANES] = dq[:, :LANES].astype(out_ref.dtype)
        out_ref[rows, LANES:wide] = dq[:, LANES:].astype(out_ref.dtype)
    for start in range(0, length, BLOCK):
        rows = slice(start, start + BLOCK)
        halves = []
        for at in (0, LANES):
            key = dk_ref[rows, at : at + LANES]
            key = pltpu.roll(key, 3 * HALF, 1) + pltpu.roll(key, 2 * HALF, 1) + pltpu.roll(key, HALF, 1)
            both = jnp.where(lane >= GROUP * HALF, key, out_ref[rows, at : at + LANES])
            halves.append(both * 0.125)
        c, s = cos_ref[rows, :], sin_ref[rows, :]
        u, w = halves
        out_ref[rows, :LANES] = u * c + w * s
        out_ref[rows, LANES:wide] = w * c - u * s
        v = dv_ref[rows, :LANES] + dv_ref[rows, LANES:]
        v = v + pltpu.roll(v, HEAD_DIM, 1)
        out_ref[rows, wide:] = jnp.where(lane < HEAD_DIM, v, 0.0)


def attend_back_entry(*refs):
    *ins, out_ref, full_ref, dk_ref, dv_ref = refs
    attend_back_kernel(*ins, full_ref, dk_ref, dv_ref)
    out_ref[...] = full_ref[...].astype(bf16)


def attend_back(q, k, v, g, lse, docs_col, docs_row, cosine, sine):
    length, wide = k.shape
    return pl.pallas_call(
        attend_back_entry,
        out_shape=jax.ShapeDtypeStruct((length, SLAB), bf16),
        scratch_shapes=[
            pltpu.VMEM((length, SLAB), f32),
            pltpu.VMEM((length, wide), f32),
            pltpu.VMEM((length, wide), f32),
        ],
        compiler_params=pltpu.CompilerParams(vmem_limit_bytes=52 * 2**20),
        cost_estimate=pl.CostEstimate(
            flops=5 * GROUP * length * length * wide,
            bytes_accessed=8 * 2**20,
            transcendentals=GROUP * length * length // 2,
        ),
    )(q, k, v, g, lse, docs_col, docs_row, cosine, sine)


def pack(gate_up, down):
    blocks = [down[:, c : c + EXP_FF] for c in range(0, down.shape[1], EXP_FF)]
    return jnp.concatenate([gate_up, jnp.concatenate(blocks, 0)], 1)


def unpack_down(packed, high):
    rows = packed.shape[0] // high
    return jnp.concatenate([packed[c * rows : (c + 1) * rows, 2 * EXP_FF :] for c in range(high)], 1)


def half_places(at_ref, half, size):
    high = at_ref[2]
    place = high if half == 0 else 1 - high
    return pl.multiple_of(place * size, LANES)


def plain_kernel(at_ref, g_ref, pa, pb, pc, pd, out_ref):
    rows = g_ref.shape[0] * g_ref.shape[2]
    part = EXP_FF // 2
    width = g_ref.shape[3]
    g = g_ref[:, 0].reshape(rows, width)
    for j, packed in enumerate(((pa, pb), (pc, pd))):
        for half, p in enumerate(packed):
            plain = None
            for c in range(width // EXP_FF):
                cols = slice(c * EXP_FF, (c + 1) * EXP_FF)
                term = dot(g[:, cols], p[c * part : (c + 1) * part, :], 1, 1)
                plain = term if plain is None else plain + term
            at = pl.multiple_of(j * EXP_FF + half_places(at_ref, half, part), LANES)
            out_ref[:, 0, :, pl.ds(at, part)] = plain.reshape(g_ref.shape[0], g_ref.shape[2], part)


def plain_grads(places, grads, packed):
    holders, batches, local, width = grads.shape
    size = packed[0].shape[0]
    near = BLOCK // local
    block = lambda cols: pl.BlockSpec((near, 1, local, cols), lambda i, m, _: (i, m, 0, 0))
    return pl.pallas_call(
        plain_kernel,
        grid_spec=pltpu.PrefetchScalarGridSpec(
            num_scalar_prefetch=1,
            grid=(holders // near, batches),
            in_specs=[
                block(width),
                *[pl.BlockSpec((size, EXP_FF), lambda i, m, _: (0, 2))] * 4,
            ],
            out_specs=block(2 * EXP_FF),
        ),
        out_shape=jax.ShapeDtypeStruct((holders, batches, local, 2 * EXP_FF), f32),
        compiler_params=pltpu.CompilerParams(vmem_limit_bytes=40 * 2**20),
        cost_estimate=pl.CostEstimate(
            flops=4 * holders * batches * local * width * EXP_FF,
            bytes_accessed=14 * 2**20,
            transcendentals=0,
        ),
    )(places, grads, *packed)


def expert_kernel(at_ref, x_ref, g_ref, pa, pb, pc, pd, sum_ref, hid_ref, pair_ref):
    rows = x_ref.shape[0]
    size, width = pa.shape[0], 2 * pa.shape[0]
    double = 2 * EXP_FF
    me, experts = at_ref[0], at_ref[1]
    extra = x_ref[:, width:].astype(f32)
    both_plain = g_ref[:, 0].reshape(rows, double)
    lane = lax.broadcasted_iota(jnp.int32, extra.shape, 1)
    back = jnp.zeros(extra.shape, f32)
    totals = [None, None]
    for j, packed in enumerate(((pa, pb), (pc, pd))):
        expert = me if j == 0 else me ^ 4
        high = lane == expert
        low = lane == expert + experts
        share = jnp.sum(jnp.where(high | low, extra, 0.0), -1, keepdims=True)
        gate_up = None
        for half, p in enumerate(packed):
            term = dot(x_ref[:, pl.ds(half_places(at_ref, half, size), size)], p[...], 1, 0)
            gate_up = term if gate_up is None else gate_up + term
        gate, up = gate_up[:, :EXP_FF], gate_up[:, EXP_FF:]
        sg = 1.0 / (1.0 + jnp.exp(-gate))
        grown = gate * sg
        hidden = (grown * up).astype(bf16).astype(f32)
        grad_plain = both_plain[:, j * EXP_FF : (j + 1) * EXP_FF]
        gate_grad = jnp.sum(grad_plain * hidden, -1, keepdims=True)
        gate_high = gate_grad.astype(bf16).astype(f32)
        back = jnp.where(high, gate_high, jnp.where(low, gate_grad - gate_high, back))
        grad_hidden = share * grad_plain
        at = j * EXP_FF
        hid_ref[:, at : at + EXP_FF] = (share * hidden).astype(bf16)
        at = j * double
        first = (grad_hidden * up * sg * (1.0 + gate * (1.0 - sg))).astype(bf16)
        pair_ref[:, at : at + EXP_FF] = first
        pair_ref[:, at + EXP_FF : at + double] = (grad_hidden * grown).astype(bf16)
        for half, p in enumerate(packed):
            term = dot(pair_ref[:, at : at + double], p[...], 1, 1)
            totals[half] = term if totals[half] is None else totals[half] + term
    for half in range(2):
        sum_ref[:, pl.ds(half_places(at_ref, half, size), size)] = totals[half].astype(bf16)
    sum_ref[:, width:] = back.astype(bf16)


def run_experts(places, x, plain, m, packed):
    rows, wide = x.shape
    local = plain.shape[2]
    size, width = packed[0].shape
    block = lambda cols: pl.BlockSpec((BLOCK, cols), lambda i, _: (i, 0))
    whole = pl.BlockSpec((size, 2 * EXP_FF), lambda i, _: (0, 0))
    return pl.pallas_call(
        expert_kernel,
        grid_spec=pltpu.PrefetchScalarGridSpec(
            num_scalar_prefetch=1,
            grid=(rows // BLOCK,),
            in_specs=[
                block(wide),
                pl.BlockSpec((BLOCK // local, 1, local, 2 * EXP_FF), lambda i, _: (i, m, 0, 0)),
                *[whole] * 4,
            ],
            out_specs=[block(wide), block(2 * EXP_FF), block(4 * EXP_FF)],
        ),
        out_shape=[
            jax.ShapeDtypeStruct((rows, wide), bf16),
            jax.ShapeDtypeStruct((rows, 2 * EXP_FF), bf16),
            jax.ShapeDtypeStruct((rows, 4 * EXP_FF), bf16),
        ],
        compiler_params=pltpu.CompilerParams(vmem_limit_bytes=56 * 2**20),
        cost_estimate=pl.CostEstimate(
            flops=16 * rows * width * EXP_FF, bytes_accessed=16 * 2**20, transcendentals=rows * 2 * EXP_FF
        ),
    )(places, x, plain, *packed)


def mixture_kernel(at_ref, a_ref, b_ref, pa, pb, pc, pd, out_ref):
    size, width = pa.shape
    part = EXP_FF // 2

    def work(hid_ref):
        for c in range(width // EXP_FF):
            total = None
            for j, packed in enumerate(((pa, pb), (pc, pd))):
                for half, p in enumerate(packed):
                    at = pl.multiple_of(j * EXP_FF + half_places(at_ref, half, part), LANES)
                    term = dot(
                        hid_ref[:, pl.ds(at, part)],
                        p[c * part : (c + 1) * part, 2 * EXP_FF :],
                        1,
                        0,
                    )
                    total = term if total is None else total + term
            cols = slice(c * EXP_FF, (c + 1) * EXP_FF)
            shape = out_ref.shape[0], out_ref.shape[2], EXP_FF
            out_ref[:, 0, :, cols] = total.astype(bf16).reshape(shape)

    pl.when(pl.program_id(0) == 0)(lambda: work(a_ref))
    pl.when(pl.program_id(0) == 1)(lambda: work(b_ref))


def mix_experts(places, weighted, local, packed):
    rows = weighted[0].shape[0]
    size, width = packed[0].shape
    blocks = rows // BLOCK
    whole = pl.BlockSpec((size, width), lambda m, i, _: (0, 0))
    first = pl.BlockSpec((BLOCK, 2 * EXP_FF), lambda m, i, _: (jnp.where(m == 0, i, blocks - 1), 0))
    second = pl.BlockSpec((BLOCK, 2 * EXP_FF), lambda m, i, _: (jnp.where(m == 1, i, 0), 0))
    return pl.pallas_call(
        mixture_kernel,
        grid_spec=pltpu.PrefetchScalarGridSpec(
            num_scalar_prefetch=1,
            grid=(2, blocks),
            in_specs=[first, second, *[whole] * 4],
            out_specs=pl.BlockSpec(
                (BLOCK // local, 1, local, width), lambda m, i, _: (i, m, 0, 0)
            ),
        ),
        out_shape=jax.ShapeDtypeStruct((rows // local, 2, local, width), bf16),
        compiler_params=pltpu.CompilerParams(vmem_limit_bytes=48 * 2**20),
        cost_estimate=pl.CostEstimate(
            flops=8 * rows * width * EXP_FF, bytes_accessed=16 * 2**20, transcendentals=0
        ),
    )(places, *weighted, *packed)


def weights_kernel(
    at_ref, xa_ref, xb_ref, g_ref, ha_ref, hb_ref, pa_ref, pb_ref, send_ref, keep_ref
):
    size, width = keep_ref.shape
    rows = xa_ref.shape[0]
    part = EXP_FF // 2
    double = 2 * EXP_FF

    def work(half, out_ref):
        cols = pl.ds(half_places(at_ref, half, size), size)
        total = dot(xa_ref[:, cols], pa_ref[...], 0, 0) + dot(xb_ref[:, cols], pb_ref[...], 0, 0)
        out_ref[:, :double] = total.astype(out_ref.dtype)
        cols = pl.ds(half_places(at_ref, half, part), part)
        for c in range(width // EXP_FF):
            at = slice(c * EXP_FF, (c + 1) * EXP_FF)
            total = dot(ha_ref[:, cols], g_ref[:, 0, :, at].reshape(rows, EXP_FF), 0, 0)
            total = total + dot(hb_ref[:, cols], g_ref[:, 1, :, at].reshape(rows, EXP_FF), 0, 0)
            out_ref[c * part : (c + 1) * part, double:] = total.astype(out_ref.dtype)

    pl.when(pl.program_id(0) == 0)(lambda: work(1, send_ref))
    pl.when(pl.program_id(0) == 1)(lambda: work(0, keep_ref))


def expert_weights(j, places, xs, grads, weighted, pairs):
    rows, wide = xs[0].shape
    width = grads.shape[3]
    size = width // 2
    whole = pl.BlockSpec((rows, wide), lambda h, _: (0, 0))
    hidden = pl.BlockSpec((rows, EXP_FF), lambda h, _: (0, j))
    pair = pl.BlockSpec((rows, 2 * EXP_FF), lambda h, _: (0, j))
    half = pl.BlockSpec((size, width), lambda h, _: (0, 0))
    return pl.pallas_call(
        weights_kernel,
        grid_spec=pltpu.PrefetchScalarGridSpec(
            num_scalar_prefetch=1,
            grid=(2,),
            in_specs=[
                whole,
                whole,
                pl.BlockSpec(grads.shape, lambda h, _: (0, 0, 0, 0)),
                hidden,
                hidden,
                pair,
                pair,
            ],
            out_specs=[half, half],
        ),
        out_shape=[
            jax.ShapeDtypeStruct((size, width), bf16),
            jax.ShapeDtypeStruct((size, width), f32 if j == 0 else bf16),
        ],
        compiler_params=pltpu.CompilerParams(vmem_limit_bytes=60 * 2**20),
        cost_estimate=pl.CostEstimate(
            flops=12 * rows * width * EXP_FF, bytes_accessed=16 * 2**20, transcendentals=0
        ),
    )(places, *xs, grads, *weighted, *pairs)


def heads_to_rows(a, b):
    lane = lax.broadcasted_iota(jnp.int32, (a.shape[0], LANES), 1)
    low = lane < HEAD_DIM
    b_first, b_second = (pltpu.roll(t, HEAD_DIM, 1) for t in (b[:, :LANES], b[:, LANES:]))
    return (a[:, :LANES], jnp.where(low, a[:, LANES:], b_first), jnp.where(low, b_first, b_second))


def rows_to_heads(first, second, third):
    lane = lax.broadcasted_iota(jnp.int32, first.shape, 1)
    low = lane < HEAD_DIM
    second_turned, third_turned = (pltpu.roll(t, HEAD_DIM, 1) for t in (second, third))
    a = (first, jnp.where(low, second, 0.0))
    b = (jnp.where(low, second_turned, third_turned), jnp.where(low, third_turned, 0.0))
    return a, b


def middle_kernel(
    experts, heads_ref, x_ref, w_ref, gain_ref, router_ref, routes_ref,
    y_ref, sent_ref, low_ref, probs_ref, gates_ref, chosen_ref, pick_ref, scale_ref,
):
    batches, local, width = x_ref.shape
    for m in range(batches):
        for k in range(0, KV_HEADS, 2):
            a, b = (heads_ref[m * KV_HEADS + k + i].astype(f32) for i in range(2))
            at = k * GROUP * HEAD_DIM
            for i, part in enumerate(heads_to_rows(a, b)):
                cols = slice(at + i * LANES, at + (i + 1) * LANES)
                low_ref[m * local : (m + 1) * local, cols] = part.astype(bf16)
    rows = batches * local
    y = x_ref[...].reshape(rows, width).astype(f32) + dot(low_ref[...], w_ref[...], 1, 1)
    y_ref[...] = y
    r = lax.rsqrt(jnp.mean(y * y, -1, keepdims=True) + epsilon)
    second = (y * r * gain_ref[...]).astype(bf16)
    lane = lax.broadcasted_iota(jnp.int32, (rows, LANES), 1)
    logits = jnp.where(lane < experts, dot(second, router_ref[...], 1, 0), masked)
    raised = jnp.exp(logits - jnp.max(logits, -1, keepdims=True))
    probs = raised / jnp.sum(raised, -1, keepdims=True)
    chosen = jnp.zeros((rows, LANES), f32)
    for k in range(TOP):
        chosen = jnp.where(routes_ref[:, k : k + 1] == lane, 1.0, chosen)
    picked = jnp.sum(chosen * probs, -1, keepdims=True)
    gates = chosen * probs / picked
    high = gates.astype(bf16).astype(f32)
    extra = high + pltpu.roll(gates - high, experts, 1)
    sent_ref[:, :, :width] = second.reshape(batches, local, width)
    sent_ref[:, :, width:] = extra.astype(bf16).reshape(batches, local, LANES)
    probs_ref[...] = probs
    gates_ref[...] = gates
    chosen_ref[...] = chosen
    pick_ref[...] = picked
    scale_ref[...] = r


def middle_rows(experts, heads, tokens, out_full, gain, router, routes):
    batches, local, width = tokens.shape
    rows = batches * local
    small = jax.ShapeDtypeStruct((rows, LANES), f32)
    column = jax.ShapeDtypeStruct((rows, 1), f32)
    return pl.pallas_call(
        lambda *refs: middle_kernel(experts, *refs),
        out_shape=[
            jax.ShapeDtypeStruct((rows, width), f32),
            jax.ShapeDtypeStruct((batches, local, width + LANES), bf16),
            jax.ShapeDtypeStruct((rows, width), bf16),
            small,
            small,
            small,
            column,
            column,
        ],
        compiler_params=pltpu.CompilerParams(vmem_limit_bytes=40 * 2**20),
        cost_estimate=pl.CostEstimate(
            flops=2 * rows * width * width, bytes_accessed=8 * 2**20, transcendentals=rows * LANES
        ),
    )(heads, tokens, out_full, gain, router, routes)


def middle_back_kernel(
    experts, came_a_ref, came_b_ref, g_ref, y_ref, probs_ref, gates_ref, chosen_ref,
    pick_ref, scale_ref, gain_ref, router_ref, w_ref,
    heads_ref, grad_ref, branch_ref, logits_ref, gain_grad_ref,
):
    batches, local, width = g_ref.shape
    rows = batches * local
    came = jnp.concatenate([came_a_ref[...], came_b_ref[...]], 0)
    extra = came[:, width:]
    lane = lax.broadcasted_iota(jnp.int32, (rows, LANES), 1)
    chosen, probs, gates = chosen_ref[...], probs_ref[...], gates_ref[...]
    both = extra + pltpu.roll(extra, LANES - experts, 1)
    grad_gates = jnp.where(lane < experts, both, 0.0) * chosen
    mean = jnp.sum(grad_gates * gates, -1, keepdims=True)
    grad_picked = chosen * (grad_gates - mean) / pick_ref[...]
    grad_logits = probs * (grad_picked - jnp.sum(probs * grad_picked, -1, keepdims=True))
    grad_logits = grad_logits.astype(bf16)
    logits_ref[...] = grad_logits
    grad_second = came[:, :width] + dot(grad_logits, router_ref[...], 1, 1)
    r = scale_ref[...]
    n = y_ref[...] * r
    gain_grad_ref[...] = jnp.sum(grad_second * n, 0, keepdims=True)
    c = grad_second * gain_ref[...]
    grad_y = g_ref[...].reshape(rows, width).astype(f32)
    grad_y = grad_y + r * (c - n * jnp.mean(c * n, -1, keepdims=True))
    grad_ref[...] = grad_y
    branch = grad_y.astype(bf16)
    branch_ref[...] = branch
    grad = dot(branch, w_ref[...], 1, 0)
    for k in range(0, KV_HEADS, 2):
        at = k * GROUP * HEAD_DIM
        parts = (grad[:, at + i * LANES : at + (i + 1) * LANES] for i in range(3))
        for j, head in enumerate(rows_to_heads(*parts)):
            for i, part in enumerate(head):
                part = part.astype(bf16).reshape(batches, local, LANES)
                for m in range(batches):
                    cols = slice(i * LANES, (i + 1) * LANES)
                    heads_ref[m * KV_HEADS + k + j, :, cols] = part[m]


def middle_back(experts, came, cotangent, kept, gain, router, out_full):
    batches, local, width = cotangent.shape
    rows = batches * local
    return pl.pallas_call(
        lambda *refs: middle_back_kernel(experts, *refs),
        out_shape=[
            jax.ShapeDtypeStruct((batches * KV_HEADS, local, 2 * LANES), bf16),
            jax.ShapeDtypeStruct((rows, width), f32),
            jax.ShapeDtypeStruct((rows, width), bf16),
            jax.ShapeDtypeStruct((rows, LANES), bf16),
            jax.ShapeDtypeStruct((1, width), f32),
        ],
        compiler_params=pltpu.CompilerParams(vmem_limit_bytes=40 * 2**20),
        cost_estimate=pl.CostEstimate(
            flops=2 * rows * width * width, bytes_accessed=10 * 2**20, transcendentals=0
        ),
    )(*came, cotangent, *kept, gain, router, out_full)


def finish_kernel(slab_ref, w_ref, gain_ref, grad_ref, gain_grad_ref):
    rows = w_ref.shape[0]
    lane = lax.broadcasted_iota(jnp.int32, (rows, LANES), 1)
    per_tile = LANES // HALF

    def tile(pieces):
        out = None
        for i, (source, group) in enumerate(pieces):
            shift = (i - group) % per_tile * HALF
            moved = pltpu.roll(source, shift, 1) if shift else source
            out = moved if out is None else jnp.where(lane // HALF == i, moved, out)
        return out

    batches = slab_ref.shape[0] // KV_HEADS
    total = jnp.zeros((rows, 1), f32)

    def put(at, value):
        grad_ref[:, at : at + LANES] = value
        return jnp.sum(value * w_ref[:, at : at + LANES].astype(f32), -1, keepdims=True)

    for k in range(0, KV_HEADS, 2):
        sums = []
        for i in range(2):
            terms = [slab_ref[m * KV_HEADS + k + i].astype(f32) for m in range(batches)]
            sums.append(sum(terms[1:], terms[0]))
        u, w, v = zip(*((t[:, :LANES], t[:, LANES : 2 * LANES], t[:, 2 * LANES :]) for t in sums))
        halves_of = [(part, group) for i in range(2) for group in range(GROUP) for part in (u[i], w[i])]
        for i in range(0, len(halves_of), per_tile):
            at = k * GROUP * HEAD_DIM + i * HALF
            total = total + put(at, tile(halves_of[i : i + per_tile]))
        at = HEADS * HEAD_DIM + k * HEAD_DIM
        total = total + put(at, tile([(part, GROUP) for i in range(2) for part in (u[i], w[i])]))
        at = (HEADS + KV_HEADS) * HEAD_DIM + k * HEAD_DIM
        total = total + put(at, jnp.where(lane < HEAD_DIM, v[0], pltpu.roll(v[1], HEAD_DIM, 1)))
    gain_grad_ref[...] = total / gain_ref[...].astype(f32)


def finish(slab, w_qkv, gain):
    return pl.pallas_call(
        finish_kernel,
        out_shape=[
            jax.ShapeDtypeStruct(w_qkv.shape, f32),
            jax.ShapeDtypeStruct(gain.shape, f32),
        ],
        compiler_params=pltpu.CompilerParams(vmem_limit_bytes=32 * 2**20),
    )(slab, w_qkv, gain)


def split_columns(w_qkv):
    rows = w_qkv.shape[0]
    q_width, k_width = HEADS * HEAD_DIM, KV_HEADS * HEAD_DIM
    q = w_qkv[:, :q_width].reshape(rows, KV_HEADS, GROUP, 2, HALF)
    k = w_qkv[:, q_width : q_width + k_width].reshape(rows, KV_HEADS, 1, 2, HALF)
    both = jnp.concatenate([q, k], 2)
    return (
        both[:, :, :, 0].reshape(rows, KV_HEADS, LANES),
        both[:, :, :, 1].reshape(rows, KV_HEADS, LANES),
        w_qkv[:, q_width + k_width :].reshape(rows, KV_HEADS, HEAD_DIM),
    )


def halves(x):
    high = lax.reduce_precision(x, 8, 7)
    return high.astype(bf16), (x - high).astype(bf16)


def gather_sequence(tokens, ex_axes, mb_axis):
    mine = lax.axis_index(mb_axis)
    own = lax.dynamic_index_in_dim(tokens, mine, 0, keepdims=False)
    other = lax.ppermute(
        lax.dynamic_index_in_dim(tokens, 1 - mine, 0, keepdims=False), mb_axis, SWAP
    )
    first = mine == 0
    group = jnp.stack([jnp.where(first, own, other), jnp.where(first, other, own)], 0)
    middle = tuple(a for a in ex_axes[:-2] if a != mb_axis)
    return gather_bits(group, middle, middle), middle, other


def on_device(
    dp_axes,
    ex_axes,
    tokens,
    cotangent,
    segments,
    positions,
    routes,
    w_qkv,
    w_out,
    w_router,
    norm_attn,
    norm_ffn,
    w_gate_up,
    w_down,
):
    batches, local, width = tokens.shape
    experts = w_router.shape[1]
    count = 2 ** len(ex_axes)
    length = count * local
    units = batches * KV_HEADS
    parts = count // units
    shard = w_qkv.shape[0]
    rows = batches * local
    me = lax.axis_index(ex_axes)
    bit = lambda b: ex_axes[len(ex_axes) - 1 - b]
    pair_axis = bit(2)
    far = tuple(a for a in ex_axes[:-2] if a != pair_axis)
    token_axes = ex_axes[-2:] + far
    orders = (far + (bit(0), bit(1)), far + (bit(1), bit(0)))

    mb_axis = bit(3)

    u_cols, w_cols, v_cols = split_columns(w_qkv)
    small = jnp.concatenate([norm_attn[:, None], norm_ffn[:, None], w_router], 1)
    small = jnp.pad(small, ((0, 0), (0, SLAB - 2 * LANES - HEAD_DIM - small.shape[1])))
    small = jnp.broadcast_to(small[:, None, :], (shard, KV_HEADS, small.shape[1]))
    slab = jnp.transpose(jnp.concatenate([u_cols, w_cols, v_cols, small], -1), (1, 0, 2))
    meta = jnp.stack([segments, positions // 64, positions % 64], 1).astype(bf16)
    meta = jnp.pad(meta, ((0, 0), (0, META_ROWS - 3), (0, SLAB - local)))
    payload = jnp.concatenate(
        [
            jnp.broadcast_to(slab[None], (batches,) + slab.shape),
            jnp.broadcast_to(meta[:, None], (batches, KV_HEADS) + meta.shape[1:]),
        ],
        2,
    ).reshape(units, shard + META_ROWS, SLAB)
    payload = jnp.concatenate([payload] * parts, 0)
    group, middle, swapped = gather_sequence(tokens, ex_axes, mb_axis)
    arrived = lax.all_to_all(after(payload, swapped), ex_axes, 0, 0, tiled=True)
    w_slab = gather_bits(arrived[:, :shard].reshape(count * shard, SLAB), dp_axes, dp_axes)
    w_slab = w_slab.reshape(width, SLAB)
    extra_at = 2 * LANES + HEAD_DIM
    gain_attn = w_slab[:, extra_at].astype(f32)
    gain_ffn = w_slab[:, extra_at + 1].astype(f32)
    router_full = w_slab[:, extra_at + 2 : extra_at + 2 + experts]
    info = arrived[:, shard : shard + 3, :local].astype(jnp.int32)
    docs = info[:, 0].reshape(length)
    places = (info[:, 1] * 64 + info[:, 2]).reshape(length)
    frequency = rope_base ** (-jnp.arange(HALF, dtype=f32) / HALF)
    angles = places.astype(f32)[:, None] * jnp.tile(frequency, GROUP + 1)[None, :]
    cosine, sine = jnp.cos(angles), jnp.sin(angles)
    docs_col, docs_row = docs[:, None], docs[None, :]

    high_axis, low_axes = dp_axes[0], dp_axes[1:]
    blocks = width // EXP_FF
    expert_own = pack(w_gate_up[0], w_down[0])
    if low_axes:
        parted = gather_bits(expert_own, low_axes, low_axes)
        parted = parted.reshape((-1,) + expert_own.shape)
        lower = parted[..., 2 * EXP_FF :].reshape(parted.shape[0], blocks, -1, EXP_FF)
        expert_own = jnp.concatenate(
            [
                parted[..., : 2 * EXP_FF].reshape(-1, 2 * EXP_FF),
                lower.transpose(1, 0, 2, 3).reshape(-1, EXP_FF),
            ],
            1,
        )
    group, expert_own = lax.optimization_barrier((group, expert_own))
    group = jnp.moveaxis(group, len(middle), 0)
    sides = []
    for part, last in ((group[0], (bit(0), bit(1))), (group[1], (bit(1), bit(0)))):
        pair = gather_bits(part, last, (bit(1), bit(0)), {1: arrived})
        sides.append(jnp.moveaxis(pair, (0, 1), (len(middle), len(middle) + 1)))
    if len(middle) == 1:
        sides = [s.reshape(length // 2, width) for s in sides]
    else:
        at = ex_axes.index(mb_axis)
        whole = jnp.stack(sides, at).reshape(length, width)
        sides = [whole[: length // 2], whole[length // 2 :]]

    out_full = lax.all_gather(w_out, dp_axes + ex_axes, axis=0, tiled=True)
    grad_rows = gather_bits(after(cotangent, group), far, far)
    grad_rows = lax.all_gather(grad_rows, ex_axes[-2:], axis=0)
    grad_rows = grad_rows.reshape((-1,) + cotangent.shape)
    qkv_mixed = jnp.concatenate([p.reshape(shard, -1) for p in (u_cols, w_cols, v_cols)], 1)
    qkv_full = lax.all_gather(qkv_mixed, dp_axes + ex_axes, axis=0, tiled=True)

    cut = expert_own.shape[0] // 2
    other_parts = [lax.ppermute(t, pair_axis, SWAP) for t in (expert_own[:cut], expert_own[cut:])]

    first_low, q, k, v = project(*sides, gain_attn[None, :], w_slab, cosine, sine)
    q = after(q, other_parts[0])
    attended, lse = attend(q, k, v, docs_col, docs_row)
    back = lax.all_to_all(attended.reshape(count, local, 2 * LANES), ex_axes, 0, 0, tiled=True)
    expert_other = jnp.concatenate([after(t, attended) for t in other_parts], 0)
    packed = [
        expert_own,
        lax.ppermute(expert_own, high_axis, SWAP),
        expert_other,
        lax.ppermute(expert_other, high_axis, SWAP),
    ]
    x = tokens.reshape(rows, width).astype(f32)
    router_full = jnp.pad(router_full, ((0, 0), (0, LANES - experts)))
    y_one, sent, attended_low, *kept = middle_rows(
        experts, back[:units], tokens, out_full, gain_ffn[None, :], router_full, routes.reshape(rows, TOP)
    )
    second_low = sent[:, :, :width].reshape(rows, width)
    sent = after(sent, other_parts[1])

    places_at = jnp.stack([me, jnp.int32(experts), lax.axis_index(high_axis)]).astype(jnp.int32)
    weighted, pairs, stages = [], [], []
    gathered = []
    ahead = sent
    for m in range(batches):
        far_part = gather_bits(after(sent[m], ahead), far, far)
        ahead = far_part
        if m == 0:
            grads = after(grad_rows, far_part)
            plain = plain_grads(places_at, grads, packed)
        last = orders[m % 2][len(far) :]
        part = gather_bits(far_part, last, (bit(1), bit(0)), {1: plain} if m else {})
        gathered.append(part.reshape(-1, width + LANES))
    for m in range(batches):
        back_rows, hid, pair = run_experts(places_at, gathered[m], plain, m, packed)
        back_rows = back_rows.reshape((2,) * len(token_axes) + (local, width + LANES))
        stages.append(scatter_bits(back_rows, orders[m % 2][-1:], token_axes))
        weighted.append(hid)
        pairs.append(pair)
    grad_inputs = []
    for m in range(batches):
        order = orders[m % 2][::-1]
        left = tuple(a for a in token_axes if a != order[0])
        grad_inputs.append(scatter_bits(stages[m], order[1:], left))

    def expert_grads(j, *others):
        send, keep = expert_weights(
            j, places_at, gathered, grad_rows, [after(t, *others) for t in weighted], pairs
        )
        grad = keep.astype(f32) + lax.ppermute(send, high_axis, SWAP).astype(f32)
        if low_axes:
            count_low = 2 ** len(low_axes)
            parted = grad[:, : 2 * EXP_FF].reshape(count_low, -1, 2 * EXP_FF)
            lower = grad[:, 2 * EXP_FF :].reshape(blocks, count_low, -1, EXP_FF)
            lower = lower.transpose(1, 0, 2, 3).reshape(count_low, -1, EXP_FF)
            parted = jnp.concatenate([parted, lower], -1)
            parted = parted.reshape((2,) * len(low_axes) + parted.shape[1:])
            grad = scatter_bits(parted.astype(bf16), low_axes, low_axes)
        return grad

    grad_theirs = expert_grads(1, stages[0]).astype(bf16)
    cut = grad_theirs.shape[0] // 2
    grad_received = [
        lax.ppermute(t, pair_axis, SWAP) for t in (grad_theirs[:cut], grad_theirs[cut:])
    ]
    grad_inputs[-1] = after(grad_inputs[-1], grad_theirs)

    payload, grad_y, grad_branch, grad_logits, grad_gain_ffn = middle_back(
        experts, grad_inputs, cotangent, [y_one, *kept], gain_ffn[None, :], router_full, out_full
    )
    payload = jnp.concatenate([payload] * parts, 0)
    grad_heads = lax.all_to_all(payload, ex_axes, 0, 0, tiled=True).reshape(length, 2 * LANES)

    mixture = mix_experts(places_at, [after(t, stages[0]) for t in weighted], local, packed)
    mixtures = lax.psum_scatter(
        after(mixture.reshape(-1, width), qkv_full), token_axes, scatter_dimension=0, tiled=True
    )
    grad_branch = after(grad_branch, payload)
    grad_out = dot(grad_branch, attended_low, 0, 0)
    extras = dot(after(second_low, payload), grad_logits, 0, 0)
    extras = jnp.where(jnp.arange(LANES) == experts, grad_gain_ffn.reshape(width, 1), extras)
    dense = jnp.concatenate([grad_out, extras], 1).astype(bf16)
    dense = scatter_bits(
        dense.reshape((2,) * len(dp_axes) + (-1, dense.shape[1])), dp_axes, dp_axes
    )
    dense = dense.astype(bf16).reshape((2,) * len(ex_axes) + (shard, -1))
    grad_heads = after(grad_heads, dense, grad_received[0])
    dense_one = scatter_bits(dense, ex_axes[-1:], ex_axes)
    dense_two = scatter_bits(dense_one, ex_axes[-2:-1], ex_axes[:-1])
    dense = scatter_bits(dense_two, ex_axes[:-2][::-1], ex_axes[:-2])

    grad_proj = attend_back(q, k, v, grad_heads, lse, docs_col, docs_row, cosine, sine)
    back = lax.all_to_all(grad_proj.reshape(count, local, SLAB), ex_axes, 0, 0, tiled=True)
    back = back[:units].reshape(batches, KV_HEADS, local, SLAB).transpose(0, 2, 1, 3)
    back = jnp.concatenate(
        [
            back[..., :LANES].reshape(rows, -1),
            back[..., LANES : 2 * LANES].reshape(rows, -1),
            back[..., 2 * LANES : 2 * LANES + HEAD_DIM].reshape(rows, -1),
        ],
        1,
    )
    grad_first = dot(after(back, dense_two), qkv_full, 1, 1)
    grad_slab = dot(first_low, grad_proj, 0, 0)
    grad_slab = scatter_bits(
        grad_slab.reshape((2,) * len(dp_axes) + (-1, SLAB)), dp_axes, dp_axes
    )
    grad_slab = lax.all_to_all(
        after(grad_slab.astype(bf16), dense_one, grad_received[1]).reshape(count, shard, SLAB), ex_axes, 0, 0, tiled=True
    )
    grad_qkv, grad_gain_attn = finish(grad_slab[:units], w_qkv, norm_attn[:, None])
    grad_gain_attn = grad_gain_attn[:, 0]
    grad_packed = expert_grads(0, grad_proj) + jnp.concatenate(grad_received, 0).astype(f32)
    grad_gate_up = grad_packed[:, : 2 * EXP_FF]
    grad_down = unpack_down(grad_packed, blocks)
    mixed = y_one + after(mixtures, grad_slab).astype(f32)
    r_one = lax.rsqrt(jnp.mean(x * x, -1, keepdims=True) + epsilon)
    n_one = x * r_one
    c_one = grad_first * gain_attn
    grad_tokens = grad_y + r_one * (c_one - n_one * jnp.mean(c_one * n_one, -1, keepdims=True))

    out_width = HEADS * HEAD_DIM
    return (
        mixed.astype(bf16).reshape(tokens.shape),
        grad_tokens.reshape(tokens.shape),
        grad_qkv,
        dense[:, :out_width],
        dense[:, out_width : out_width + experts],
        grad_gain_attn,
        dense[:, out_width + experts],
        grad_gate_up[None],
        grad_down[None],
    )


def solution(mesh):
    dp_bits = int(math.log2(mesh.shape["dp"]))
    ex_bits = int(math.log2(mesh.shape["expert"]))
    dp_axes = tuple(f"d{b}" for b in reversed(range(dp_bits)))
    ex_axes = tuple(f"e{b}" for b in reversed(range(ex_bits)))
    cube = Mesh(mesh.devices.reshape((2,) * (dp_bits + ex_bits)), dp_axes + ex_axes)
    every = dp_axes + ex_axes
    by_tokens = P(None, every, None)

    def run(*arrays):
        return on_device(dp_axes, ex_axes, *arrays)

    return jax.shard_map(
        run,
        mesh=cube,
        in_specs=(
            by_tokens,
            by_tokens,
            P(None, every),
            P(None, every),
            by_tokens,
            P(every, None),
            P(every, None),
            P(every, None),
            P(every),
            P(every),
            P(ex_axes, dp_axes, None),
            P(ex_axes, dp_axes, None),
        ),
        out_specs=(
            by_tokens,
            by_tokens,
            P(every, None),
            P(every, None),
            P(every, None),
            P(every),
            P(every),
            P(ex_axes, dp_axes, None),
            P(ex_axes, dp_axes, None),
        ),
        check_vma=False,
    )
```
